32 devices in a mesh: rep: 2 (over x), grp: 2 (over core), tp: 8 (over z, y).
Axes of the slice: x: 2, y: 2, z: 4, core: 2. Of those that a mesh axis runs over, the one named last changes fastest.
Arguments:
- tokens: bfloat16 [4, 128, 8192], P(('rep', 'grp'), 'tp'), parts along dimension 0, may hold values from -6 to 6
- base_projection_weight: bfloat16 [8192, 10240], P(None, 'tp'), may hold values from -0.0625 to 0.0625
- adapter_down_panels: bfloat16 [16, 8192, 64], P(('grp', 'tp')), may hold values from -0.0625 to 0.0625
- adapter_up_panels: bfloat16 [16, 64, 10240], P(('grp', 'tp')), may hold values from -0.75 to 0.75
- request_adapter_ids: int32 [4, 12], P('rep'), parts along dimension 0, may hold values from 0 to 15, all different within a row
- request_token_lengths: int32 [4, 12], P(('rep', 'grp')), parts along dimension 0, may hold values from 1 to 16, 128 in all within a row
- adapter_store_slot: int32 [16], replicated, may hold values from 0 to 15, each once
Outputs:
- projected: bfloat16 [4, 128, 10240], P(('rep', 'grp'), None, 'tp'), parts along dimension 0
The draws below stay inside these ranges and needn't reach their ends.
There are 2 independent parts, one for each index of `rep`. The reference program is written for one: setup_inputs(seed, part) draws one part's arguments, and reference() takes and returns one part's arrays. A program takes and returns all parts, laid end to end along the dimension named above; an argument that names none is the same for every part. Nothing has to cross between parts.
Inputs may be any that keep to these rules, and one draw needn't show every extreme that they name: `request_adapter_ids`: each group names 12 different adapters, and every adapter is named by some group. `request_token_lengths`: each group's requests cover its 128 tokens, the longest exactly 16. `adapter_store_slot`: each slot holds one adapter.
All inputs are finite; a program needn't handle non-finite values.
Results may differ from the reference program's by a relative error of at most 0.0039.
Values may be sent and summed in bfloat16 or wider, within the bound.
No kernel may reach another device: no remote copies, remote signals or barrier semaphores. Data moves between devices by JAX's collectives and lax.ppermute only.
A program may use at most 64 MiB of HBM per device.

```python
import math
import jax
import jax.numpy as jnp
import numpy as np
from jax import lax

MODEL_WIDTH = 8192
QUERY_KEY_VALUE = 10240
ADAPTER_RANK = 64
TOKENS = 128
ADAPTER_COUNT = 16
SEGS = 12
N_GRP = 2


def steps_of(rng, dims, cuts, low, largest):
    factor_of, own = 1.0, jax.random.fold_in(rng, 6)
    for dim, blocks in cuts:
        draws = jnp.exp(jax.random.uniform(jax.random.fold_in(own, dim), (blocks,), jnp.float32, low / len(cuts), largest / len(cuts)))
        factor_of = factor_of * jnp.repeat(draws, dims[dim] // blocks).reshape([-1 if axis == dim else 1 for axis in range(len(dims))])
    return factor_of


def picks_of(key, rows, amount, top, lift):
    ranking = jax.random.permutation(jax.random.fold_in(key, 1), amount)
    boost = ranking
    for power in range(3):
        boost = boost * boost // amount
    boost = boost * lift // amount
    tickets = jax.random.randint(jax.random.fold_in(key, 2), (rows, amount), 0, 4096) + boost
    sure = jax.random.permutation(jax.random.fold_in(key, 3), rows)[jnp.arange(amount) % rows]
    tickets = jnp.where(jnp.arange(rows)[:, None] == sure[None, :], 1 << 14, tickets)
    merit = tickets * amount + jnp.arange(amount)
    return lax.top_k(merit.astype(jnp.int32), top)[1].astype(jnp.int32)


def profile(amount, total, bound, lean):
    portions = [(1 << 20) // math.isqrt(rank ** lean) + 1 for rank in range(2, amount + 1)]
    surplus, given = total - bound - (amount - 1), [1] * (amount - 1)
    while surplus > 0:
        movable = [i for i in range(amount - 1) if given[i] < bound]
        pool, left = sum([portions[i] for i in movable]), surplus
        for i in movable:
            addition = min(bound - given[i], max(1, left * portions[i] // pool), surplus)
            given[i] = given[i] + addition
            surplus = surplus - addition
    return np.array([bound] + given)


def ragged_sizes(rng, amount, total, bound, slope):
    if amount == 2:
        one = jax.random.randint(rng, (), max(1, total - bound), min(bound, total - 1) + 1)
        return jnp.stack([one, total - one])
    sizes = jnp.asarray(profile(amount, total, bound, slope), jnp.int32)
    twos = (amount - 1) // 2
    donor, sink = sizes[1:1 + 2 * twos:2], sizes[2:2 + 2 * twos:2]
    slack = jnp.minimum(donor - 1, bound - sink)
    moved = jax.random.randint(jax.random.fold_in(rng, 1), (twos,), 0, 1 << 20) % (slack + 1)
    sizes = sizes.at[1:1 + 2 * twos:2].set(donor - moved).at[2:2 + 2 * twos:2].set(sink + moved)
    return sizes[jax.random.permutation(jax.random.fold_in(rng, 2), amount)]


def scatter_about(own_key, shape, width, reach, shards=(), kind=jnp.bfloat16):
    result = width * jax.random.normal(own_key, shape, jnp.float32)
    if shards:
        result = result * steps_of(own_key, shape, shards, -0.22, 0.18)
    return jnp.clip(result, -reach, reach).astype(kind)


def setup_inputs(seed: int = 0, part: int = 0) -> dict:
    splits = jax.random.split(jax.random.key(seed), 8)
    part_splits = jax.random.split(jax.random.fold_in(splits[7], part), 8)
    return {
        "tokens": scatter_about(part_splits[0], (N_GRP, TOKENS, MODEL_WIDTH), 1.0, 6.0, ((0, 2), (1, 8))),
        "base_projection_weight": scatter_about(splits[1], (MODEL_WIDTH, QUERY_KEY_VALUE), MODEL_WIDTH ** -0.5, 0.0625, ((1, 8),)),
        "adapter_down_panels": scatter_about(splits[2], (ADAPTER_COUNT, MODEL_WIDTH, ADAPTER_RANK), MODEL_WIDTH ** -0.5, 0.0625, ((0, 16),)),
        "adapter_up_panels": scatter_about(splits[3], (ADAPTER_COUNT, ADAPTER_RANK, QUERY_KEY_VALUE), ADAPTER_RANK ** -0.5, 0.75, ((0, 16),)),
        "request_adapter_ids": picks_of(part_splits[4], N_GRP, ADAPTER_COUNT, SEGS, 12000),
        "request_token_lengths": jax.vmap(lambda own: ragged_sizes(own, SEGS, TOKENS, TOKENS // 8, 2))(jax.random.split(part_splits[5], N_GRP)).reshape((N_GRP, SEGS)).astype(jnp.int32),
        "adapter_store_slot": jax.random.permutation(splits[6], ADAPTER_COUNT).astype(jnp.int32),
    }


adapter_scale = 1.0


def single_group(token_row_block, base_projection_weight, adapter_down_panels, adapter_up_panels, request_list, request_lengths, adapter_store_slot):
    base_output = jnp.dot(token_row_block, base_projection_weight, preferred_element_type=jnp.float32)
    ends = jnp.cumsum(request_lengths)
    starts = ends - request_lengths
    position = jnp.arange(token_row_block.shape[0], dtype=jnp.int32)[:, None]
    member = ((position >= starts[None, :]) & (position < ends[None, :])).astype(jnp.float32)
    store_slot_list = adapter_store_slot[request_list]
    down_projected = adapter_down_panels[store_slot_list]
    up_projected = adapter_up_panels[store_slot_list]
    segs = down_projected.shape[0]
    rank_index = down_projected.shape[2]
    down_cat = jnp.transpose(down_projected, (1, 0, 2)).reshape(token_row_block.shape[1], segs * rank_index)
    xa = jnp.dot(token_row_block, down_cat, preferred_element_type=jnp.float32).reshape(token_row_block.shape[0], segs, rank_index)
    low = jnp.sum(member[:, :, None] * xa, axis=1).astype(jnp.bfloat16)
    expanded = (member[:, :, None] * low.astype(jnp.float32)[:, None, :]).astype(jnp.bfloat16)
    expanded = expanded.reshape(token_row_block.shape[0], segs * rank_index)
    lifted_output = jnp.dot(expanded, up_projected.reshape(segs * rank_index, up_projected.shape[2]), preferred_element_type=jnp.float32)
    return (base_output + adapter_scale * lifted_output).astype(jnp.bfloat16)


def reference(tokens, base_projection_weight, adapter_down_panels, adapter_up_panels, request_adapter_ids, request_token_lengths, adapter_store_slot):
    output_rows = []
    for request_group in range(tokens.shape[0]):
        output_rows.append(single_group(tokens[request_group], base_projection_weight, adapter_down_panels, adapter_up_panels, request_adapter_ids[request_group], request_token_lengths[request_group], adapter_store_slot))
    return jnp.stack(output_rows, axis=0)
```

```python
import jax
import jax.numpy as jnp
from jax import lax
from jax.sharding import PartitionSpec as P

adapter_scale = 1.0


def swapped(x, axis):
    n = lax.axis_size(axis)
    return [x] + [
        lax.ppermute(x, axis, [((i + s) % n, i) for i in range(n)]) for s in range(1, n)
    ]


def on_device(
    tokens,
    base_projection_weight,
    adapter_down_panels,
    adapter_up_panels,
    request_adapter_ids,
    request_token_lengths,
    adapter_store_slot,
):
    groups = lax.axis_size("grp")
    tp = lax.axis_size("tp")
    reps = lax.axis_size("rep")
    my_group = lax.axis_index("grp")
    my_tp = lax.axis_index("tp")
    my_rep = lax.axis_index("rep")
    rank = adapter_down_panels.shape[2]
    rank_portion = rank // reps
    columns = base_projection_weight.shape[1]
    store_size = adapter_store_slot.shape[0]
    tok_all = tokens.shape[1] * tp

    gathered = lax.all_gather(tokens[0], "tp", axis=0, tiled=True)

    downs = swapped(jnp.transpose(adapter_down_panels[0]), "grp")

    up_mine = lax.dynamic_slice_in_dim(
        adapter_up_panels[0], my_rep * rank_portion, rank_portion, axis=0
    )
    up_send = jnp.transpose(up_mine.reshape(rank_portion, tp, columns), (1, 0, 2))
    up_got = lax.all_to_all(up_send, "tp", split_axis=0, concat_axis=0, tiled=True)
    ups = [swapped(part, "grp") for part in swapped(up_got, "rep")]

    ids = jnp.arange(store_size, dtype=jnp.int32)
    my_ids = lax.dynamic_index_in_dim(request_adapter_ids, my_group, 0, keepdims=False)
    my_slots = jnp.sum(
        jnp.where(my_ids[:, None] == ids[None, :], adapter_store_slot[None, :], 0), axis=-1
    )
    lengths = request_token_lengths[0]
    ends = jnp.cumsum(lengths)
    starts = ends - lengths
    position = jnp.arange(tok_all, dtype=jnp.int32)[:, None]
    member = (position >= starts[None, :]) & (position < ends[None, :])
    token_slot = jnp.sum(jnp.where(member, my_slots[None, :], 0), axis=1)

    low = jnp.concatenate(
        [
            jnp.where(
                (token_slot == ((my_group + s) % groups) * tp + my_tp)[:, None],
                lax.dot_general(
                    gathered, down, (((1,), (1,)), ((), ())), preferred_element_type=jnp.float32
                ),
                0.0,
            )
            for s, down in enumerate(downs)
        ],
        axis=0,
    ).astype(jnp.bfloat16)
    low = lax.dynamic_slice_in_dim(
        jnp.concatenate([low, low], axis=1), my_rep * rank_portion, rank, axis=1
    )
    low_all = lax.all_gather(low, "tp", axis=0).reshape(tp, groups, tok_all, reps, rank_portion)

    total = jnp.dot(gathered, base_projection_weight, preferred_element_type=jnp.float32)
    for r in range(reps):
        for s in range(groups):
            total = total + adapter_scale * lax.dot_general(
                low_all[:, s, :, r, :],
                ups[r][s],
                (((0, 2), (0, 1)), ((), ())),
                preferred_element_type=jnp.float32,
            )
    return total.astype(jnp.bfloat16)[None]


def solution(mesh):
    return jax.shard_map(
        on_device,
        mesh=mesh,
        in_specs=(
            P(("rep", "grp"), "tp", None),
            P(None, "tp"),
            P(("grp", "tp"), None, None),
            P(("grp", "tp"), None, None),
            P("rep", None),
            P(("rep", "grp"), None),
            P(),
        ),
        out_specs=P(("rep", "grp"), None, "tp"),
        check_vma=False,
    )
```

```python
import jax
import jax.numpy as jnp
from jax import lax
from jax.sharding import PartitionSpec as P

adapter_scale = 1.0


def swapped(x, axis):
    n = lax.axis_size(axis)
    return [x] + [
        lax.ppermute(x, axis, [((i + s) % n, i) for i in range(n)]) for s in range(1, n)
    ]


def ring_of(n):
    return list(range(0, n, 2)) + list(range(1, n, 2))[::-1]


def ring_gather(block, axis):
    n = lax.axis_size(axis)
    ring = ring_of(n)
    rows, width = block.shape
    me = lax.axis_index(axis)
    place = jnp.where(me % 2 == 0, me // 2, n - 1 - me // 2)
    up = [(ring[i], ring[(i + 1) % n]) for i in range(n)]
    down = [(ring[(i + 1) % n], ring[i]) for i in range(n)]
    out = jnp.zeros((n * rows, width), block.dtype)

    def put(out, part, distance, column):
        at = lax.rem(place - distance + n, n)
        source = jnp.where(at < n // 2, 2 * at, 2 * (n - 1 - at) + 1)
        return lax.dynamic_update_slice(out, part, (source * rows, column))

    out = put(out, block, 0, 0)
    ahead = behind = block
    for step in range(1, n // 2):
        ahead = lax.ppermute(ahead, axis, up)
        behind = lax.ppermute(behind, axis, down)
        out = put(out, ahead, step, 0)
        out = put(out, behind, -step, 0)
    half = width // 2
    out = put(out, lax.ppermute(ahead[:, :half], axis, up), n // 2, 0)
    out = put(out, lax.ppermute(behind[:, half:], axis, down), n // 2, half)
    return out


def direct_gather(block, axis):
    n = lax.axis_size(axis)
    me = lax.axis_index(axis)
    out = jnp.zeros((n, *block.shape), block.dtype)
    for shift in range(n):
        part = block if shift == 0 else lax.ppermute(
            block, axis, [(i, (i + shift) % n) for i in range(n)]
        )
        out = lax.dynamic_update_index_in_dim(out, part, lax.rem(me - shift + n, n), 0)
    return out


def on_device(
    tokens,
    base_projection_weight,
    adapter_down_panels,
    adapter_up_panels,
    request_adapter_ids,
    request_token_lengths,
    adapter_store_slot,
):
    groups = lax.axis_size("grp")
    tp = lax.axis_size("tp")
    reps = lax.axis_size("rep")
    my_group = lax.axis_index("grp")
    my_tp = lax.axis_index("tp")
    my_rep = lax.axis_index("rep")
    rank = adapter_down_panels.shape[2]
    rank_portion = rank // reps
    columns = base_projection_weight.shape[1]
    store_size = adapter_store_slot.shape[0]
    tok_all = tokens.shape[1] * tp

    gathered = ring_gather(tokens[0], "tp")

    downs = swapped(jnp.transpose(adapter_down_panels[0]), "grp")

    up_mine = lax.dynamic_slice_in_dim(
        adapter_up_panels[0], my_rep * rank_portion, rank_portion, axis=0
    )
    up_send = jnp.transpose(up_mine.reshape(rank_portion, tp, columns), (1, 0, 2))
    up_got = lax.all_to_all(up_send, "tp", split_axis=0, concat_axis=0, tiled=True)
    ups = [swapped(part, "grp") for part in swapped(up_got, "rep")]

    ids = jnp.arange(store_size, dtype=jnp.int32)
    my_ids = lax.dynamic_index_in_dim(request_adapter_ids, my_group, 0, keepdims=False)
    my_slots = jnp.sum(
        jnp.where(my_ids[:, None] == ids[None, :], adapter_store_slot[None, :], 0), axis=-1
    )
    lengths = request_token_lengths[0]
    ends = jnp.cumsum(lengths)
    starts = ends - lengths
    position = jnp.arange(tok_all, dtype=jnp.int32)[:, None]
    member = (position >= starts[None, :]) & (position < ends[None, :])
    token_slot = jnp.sum(jnp.where(member, my_slots[None, :], 0), axis=1)

    low = sum(
        jnp.where(
            (token_slot == ((my_group + s) % groups) * tp + my_tp)[:, None],
            lax.dot_general(
                gathered, down, (((1,), (1,)), ((), ())), preferred_element_type=jnp.float32
            ),
            0.0,
        )
        for s, down in enumerate(downs)
    ).astype(jnp.bfloat16)
    low = lax.dynamic_slice_in_dim(
        jnp.concatenate([low, low], axis=1), my_rep * rank_portion, rank, axis=1
    )
    low_all = direct_gather(low, "tp")
    owners = jnp.arange(tp, dtype=jnp.int32)
    expanded = [
        jnp.where(
            (token_slot[None, :] == (((my_group + s) % groups) * tp + owners)[:, None])[:, :, None],
            low_all,
            jnp.zeros_like(low_all),
        )
        for s in range(groups)
    ]

    total = jnp.dot(gathered, base_projection_weight, preferred_element_type=jnp.float32)
    for r in range(reps):
        for s in range(groups):
            total = total + adapter_scale * lax.dot_general(
                expanded[s][:, :, r * rank_portion : (r + 1) * rank_portion],
                ups[r][s],
                (((0, 2), (0, 1)), ((), ())),
                preferred_element_type=jnp.float32,
            )
    return total.astype(jnp.bfloat16)[None]


def solution(mesh):
    return jax.shard_map(
        on_device,
        mesh=mesh,
        in_specs=(
            P(("rep", "grp"), "tp", None),
            P(None, "tp"),
            P(("grp", "tp"), None, None),
            P(("grp", "tp"), None, None),
            P("rep", None),
            P(("rep", "grp"), None),
            P(),
        ),
        out_specs=P(("rep", "grp"), None, "tp"),
        check_vma=False,
    )
```

```python
import functools

import jax
import jax.numpy as jnp
from jax import lax
from jax.experimental import pallas as pl
from jax.experimental.pallas import tpu as pltpu
from jax.sharding import PartitionSpec as P

adapter_scale = 1.0


def swapped(x, axis):
    n = lax.axis_size(axis)
    return [x] + [
        lax.ppermute(x, axis, [((i + s) % n, i) for i in range(n)]) for s in range(1, n)
    ]


def ring_of(n):
    return list(range(0, n, 2)) + list(range(1, n, 2))[::-1]


def ring_gather(block, axis):
    n = lax.axis_size(axis)
    ring = ring_of(n)
    rows, width = block.shape
    me = lax.axis_index(axis)
    place = jnp.where(me % 2 == 0, me // 2, n - 1 - me // 2)
    up = [(ring[i], ring[(i + 1) % n]) for i in range(n)]
    down = [(ring[(i + 1) % n], ring[i]) for i in range(n)]
    out = jnp.zeros((n * rows, width), block.dtype)

    def put(out, part, distance, column):
        at = lax.rem(place - distance + n, n)
        source = jnp.where(at < n // 2, 2 * at, 2 * (n - 1 - at) + 1)
        return lax.dynamic_update_slice(out, part, (source * rows, column))

    out = put(out, block, 0, 0)
    ahead = behind = block
    first = None
    for step in range(1, n // 2):
        ahead = lax.ppermute(ahead, axis, up)
        behind = lax.ppermute(behind, axis, down)
        if first is None:
            first = (ahead, behind)
        out = put(out, ahead, step, 0)
        out = put(out, behind, -step, 0)
    half = width // 2
    out = put(out, lax.ppermute(ahead[:, :half], axis, up), n // 2, 0)
    out = put(out, lax.ppermute(behind[:, half:], axis, down), n // 2, half)
    return out, first


def sum_over(x, axis):
    n = lax.axis_size(axis)
    if n & (n - 1):
        return lax.psum(x, axis)
    shift = 1
    while shift < n:
        x = x + lax.ppermute(x, axis, [(i, i ^ shift) for i in range(n)])
        shift *= 2
    return x


def lift_kernel(reps, groups, pieces, at_ref, slot_ref, low_ref, *refs):
    ups, bases, out_ref = refs[: reps * groups], refs[reps * groups : -1], refs[-1]
    depth = ups[0].shape[0]
    rank = low_ref.shape[1]
    rank_portion = rank // reps
    low = low_ref[...]
    token_slot = slot_ref[...]
    row = lax.broadcasted_iota(jnp.int32, (rank, depth), 0)
    column = lax.broadcasted_iota(jnp.int32, (rank, depth), 1)
    lane = lax.broadcasted_iota(jnp.int32, (low.shape[0], depth), 1)
    expanded = []
    for r in range(reps):
        spread = (row == at_ref[r] + lax.rem(column, rank_portion)).astype(jnp.bfloat16)
        wide = jnp.dot(low, spread, preferred_element_type=jnp.float32)
        for s in range(groups):
            chosen = token_slot == at_ref[reps + s] + lane // rank_portion
            expanded.append(jnp.where(chosen, wide, 0.0).astype(jnp.bfloat16))
    for (start, size), base in zip(pieces, bases):
        total = base[...]
        for part, panel in zip(expanded, ups):
            total = total + adapter_scale * jnp.dot(
                part, panel[:, start : start + size], preferred_element_type=jnp.float32
            )
        out_ref[:, start : start + size] = total.astype(out_ref.dtype)


def on_device(
    tokens,
    base_projection_weight,
    adapter_down_panels,
    adapter_up_panels,
    request_adapter_ids,
    request_token_lengths,
    adapter_store_slot,
):
    groups = lax.axis_size("grp")
    tp = lax.axis_size("tp")
    reps = lax.axis_size("rep")
    my_group = lax.axis_index("grp")
    my_tp = lax.axis_index("tp")
    my_rep = lax.axis_index("rep")
    rank = adapter_down_panels.shape[2]
    rank_portion = rank // reps
    columns = base_projection_weight.shape[1]
    store_size = adapter_store_slot.shape[0]
    tok_all = tokens.shape[1] * tp

    gathered, first = ring_gather(tokens[0], "tp")

    downs = swapped(jnp.transpose(adapter_down_panels[0]), "grp")

    up_mine = lax.dynamic_slice_in_dim(
        adapter_up_panels[0], my_rep * rank_portion, rank_portion, axis=0
    )
    up_send = jnp.transpose(up_mine.reshape(rank_portion, tp, columns), (1, 0, 2))
    up_send = lax.optimization_barrier((up_send, *first))[0]
    up_got = lax.all_to_all(up_send, "tp", split_axis=0, concat_axis=0, tiled=True)
    ups = [swapped(part, "grp") for part in swapped(up_got, "rep")]

    ids = jnp.arange(store_size, dtype=jnp.int32)
    my_ids = lax.dynamic_index_in_dim(request_adapter_ids, my_group, 0, keepdims=False)
    my_slots = jnp.sum(
        jnp.where(my_ids[:, None] == ids[None, :], adapter_store_slot[None, :], 0), axis=-1
    )
    lengths = request_token_lengths[0]
    ends = jnp.cumsum(lengths)
    starts = ends - lengths
    position = jnp.arange(tok_all, dtype=jnp.int32)[:, None]
    member = (position >= starts[None, :]) & (position < ends[None, :])
    token_slot = jnp.sum(jnp.where(member, my_slots[None, :], 0), axis=1)

    low = sum(
        jnp.where(
            (token_slot == ((my_group + s) % groups) * tp + my_tp)[:, None],
            lax.dot_general(
                gathered, down, (((1,), (1,)), ((), ())), preferred_element_type=jnp.float32
            ),
            0.0,
        )
        for s, down in enumerate(downs)
    ).astype(jnp.bfloat16)
    low = sum_over(low, "tp")

    pieces = [(a, min(512, columns - a)) for a in range(0, columns, 512)]
    bases = [
        jnp.dot(
            gathered, base_projection_weight[:, a : a + n], preferred_element_type=jnp.float32
        )
        for a, n in pieces
    ]
    at = jnp.stack(
        [lax.rem(my_rep + r, reps) * rank_portion for r in range(reps)]
        + [lax.rem(my_group + s, groups) * tp for s in range(groups)]
    ).astype(jnp.int32)
    panels = [part.reshape(tp * rank_portion, columns) for row in ups for part in row]
    in_vmem = pl.BlockSpec(memory_space=pltpu.VMEM)
    out = pl.pallas_call(
        functools.partial(lift_kernel, reps, groups, pieces),
        out_shape=jax.ShapeDtypeStruct((tok_all, columns), jnp.bfloat16),
        in_specs=[pl.BlockSpec(memory_space=pltpu.SMEM)]
        + [in_vmem] * (2 + len(panels) + len(bases)),
        out_specs=in_vmem,
        cost_estimate=pl.CostEstimate(
            flops=2 * tok_all * columns * rank * groups * tp,
            bytes_accessed=2 * rank * groups * tp * columns + 6 * tok_all * columns,
            transcendentals=0,
        ),
        name="lift",
    )(at, token_slot[:, None], low, *panels, *bases)
    return out[None]


def solution(mesh):
    return jax.shard_map(
        on_device,
        mesh=mesh,
        in_specs=(
            P(("rep", "grp"), "tp", None),
            P(None, "tp"),
            P(("grp", "tp"), None, None),
            P(("grp", "tp"), None, None),
            P("rep", None),
            P(("rep", "grp"), None),
            P(),
        ),
        out_specs=P(("rep", "grp"), None, "tp"),
        check_vma=False,
    )
```

```python
import functools

import jax
import jax.numpy as jnp
from jax import lax
from jax.experimental import pallas as pl
from jax.experimental.pallas import tpu as pltpu
from jax.sharding import PartitionSpec as P

adapter_scale = 1.0


def swapped(x, axis):
    n = lax.axis_size(axis)
    return [x] + [
        lax.ppermute(x, axis, [((i + s) % n, i) for i in range(n)]) for s in range(1, n)
    ]


def ring_of(n):
    return list(range(0, n, 2)) + list(range(1, n, 2))[::-1]


def ring_gather(block, axis, behind_which=None):
    n = lax.axis_size(axis)
    ring = ring_of(n)
    rows, width = block.shape
    me = lax.axis_index(axis)
    place = jnp.where(me % 2 == 0, me // 2, n - 1 - me // 2)
    up = [(ring[i], ring[(i + 1) % n]) for i in range(n)]
    down = [(ring[(i + 1) % n], ring[i]) for i in range(n)]
    out = jnp.zeros((n * rows, width), block.dtype)

    def put(out, part, distance, column):
        at = lax.rem(place - distance + n, n)
        source = jnp.where(at < n // 2, 2 * at, 2 * (n - 1 - at) + 1)
        return lax.dynamic_update_slice(out, part, (source * rows, column))

    out = put(out, block, 0, 0)
    ahead = behind = block
    for step in range(1, n // 2):
        ahead = lax.ppermute(ahead, axis, up)
        behind = lax.ppermute(behind, axis, down)
        out = put(out, ahead, step, 0)
        out = put(out, behind, -step, 0)
    half = width // 2
    if behind_which is not None:
        ahead, behind, behind_which = lax.optimization_barrier((ahead, behind, behind_which))
    out = put(out, lax.ppermute(ahead[:, :half], axis, up), n // 2, 0)
    out = put(out, lax.ppermute(behind[:, half:], axis, down), n // 2, half)
    return out, behind_which


def sum_over(x, axis):
    n = lax.axis_size(axis)
    if n & (n - 1):
        return lax.psum(x, axis)
    shift = 1
    while shift < n:
        x = x + lax.ppermute(x, axis, [(i, i ^ shift) for i in range(n)])
        shift *= 2
    return x


def cut_kernel(parts, columns, at_ref, panel_ref, out_ref):
    rows = pl.ds(pl.multiple_of(at_ref[0], out_ref.shape[1]), out_ref.shape[1])
    for part in range(parts):
        out_ref[part] = panel_ref[rows, part * columns : (part + 1) * columns]


def low_kernel(reps, groups, at_ref, slot_ref, tokens_ref, *refs):
    downs, out_ref = refs[:-1], refs[-1]
    total = jnp.zeros(out_ref.shape, jnp.float32)
    for s, down in enumerate(downs):
        mine = slot_ref[...] == at_ref[reps + s] + at_ref[reps + groups]
        product = lax.dot_general(
            tokens_ref[...], down[...], (((1,), (1,)), ((), ())),
            preferred_element_type=jnp.float32,
        )
        total = jnp.where(mine, product, total)
    out_ref[...] = total.astype(out_ref.dtype)


def base_kernel(tokens_ref, weight_ref, *refs):
    before, out_ref = refs[:-1], refs[-1]
    product = jnp.dot(tokens_ref[...], weight_ref[...], preferred_element_type=jnp.float32)
    first = pl.program_id(0) == 0

    @pl.when(first)
    def _():
        out_ref[...] = product + before[0][...] if before else product

    @pl.when(jnp.logical_not(first))
    def _():
        out_ref[...] += product


def lift_kernel(reps, groups, at_ref, slot_ref, low_ref, base_ref, *refs):
    ups, out_ref = refs[:-1], refs[-1]
    depth = ups[0].shape[0]
    rank = low_ref.shape[1]
    rank_portion = rank // reps
    low = low_ref[...]
    token_slot = slot_ref[...]
    row = lax.broadcasted_iota(jnp.int32, (rank, depth), 0)
    column = lax.broadcasted_iota(jnp.int32, (rank, depth), 1)
    lane = lax.broadcasted_iota(jnp.int32, (low.shape[0], depth), 1)
    total = base_ref[...]
    for r in range(reps):
        spread = (row == at_ref[r] + lax.rem(column, rank_portion)).astype(jnp.bfloat16)
        wide = jnp.dot(low, spread, preferred_element_type=jnp.float32)
        for s in range(groups):
            chosen = token_slot == at_ref[reps + s] + lane // rank_portion
            expanded = jnp.where(chosen, wide, 0.0).astype(jnp.bfloat16)
            total = total + adapter_scale * jnp.dot(
                expanded, ups[r * groups + s][...], preferred_element_type=jnp.float32
            )
    out_ref[...] = total.astype(out_ref.dtype)


def on_device(
    tokens,
    base_projection_weight,
    adapter_down_panels,
    adapter_up_panels,
    request_adapter_ids,
    request_token_lengths,
    adapter_store_slot,
):
    groups = lax.axis_size("grp")
    tp = lax.axis_size("tp")
    reps = lax.axis_size("rep")
    my_group = lax.axis_index("grp")
    my_tp = lax.axis_index("tp")
    my_rep = lax.axis_index("rep")
    rank = adapter_down_panels.shape[2]
    rank_portion = rank // reps
    columns = base_projection_weight.shape[1]
    store_size = adapter_store_slot.shape[0]
    tok_all = tokens.shape[1] * tp
    width = tokens.shape[2]
    in_vmem = pl.BlockSpec(memory_space=pltpu.VMEM)

    downs = swapped(jnp.transpose(adapter_down_panels[0]), "grp")

    up_send = pl.pallas_call(
        functools.partial(cut_kernel, tp, columns),
        out_shape=jax.ShapeDtypeStruct((tp, rank_portion, columns), jnp.bfloat16),
        in_specs=[pl.BlockSpec(memory_space=pltpu.SMEM), in_vmem],
        out_specs=in_vmem,
        name="cut",
    )((my_rep * rank_portion).astype(jnp.int32).reshape(1), adapter_up_panels[0])
    up_got = lax.all_to_all(up_send, "tp", split_axis=0, concat_axis=0, tiled=True)

    gathered, up_got = ring_gather(tokens[0], "tp", up_got)
    ups = [swapped(part, "grp") for part in swapped(up_got, "rep")]

    ids = jnp.arange(store_size, dtype=jnp.int32)
    my_ids = lax.dynamic_index_in_dim(request_adapter_ids, my_group, 0, keepdims=False)
    my_slots = jnp.sum(
        jnp.where(my_ids[:, None] == ids[None, :], adapter_store_slot[None, :], 0), axis=-1
    )
    lengths = request_token_lengths[0]
    ends = jnp.cumsum(lengths)
    starts = ends - lengths
    position = jnp.arange(tok_all, dtype=jnp.int32)[:, None]
    member = (position >= starts[None, :]) & (position < ends[None, :])
    token_slot = jnp.sum(jnp.where(member, my_slots[None, :], 0), axis=1)

    at = jnp.stack(
        [lax.rem(my_rep + r, reps) * rank_portion for r in range(reps)]
        + [lax.rem(my_group + s, groups) * tp for s in range(groups)]
        + [my_tp]
    ).astype(jnp.int32)
    token_slot = token_slot[:, None]
    low = pl.pallas_call(
        functools.partial(low_kernel, reps, groups),
        out_shape=jax.ShapeDtypeStruct((tok_all, rank), jnp.bfloat16),
        in_specs=[pl.BlockSpec(memory_space=pltpu.SMEM)] + [in_vmem] * (2 + groups),
        out_specs=in_vmem,
        compiler_params=pltpu.CompilerParams(vmem_limit_bytes=24 * 2**20),
        cost_estimate=pl.CostEstimate(
            flops=2 * tok_all * width * rank * groups,
            bytes_accessed=2 * width * (tok_all + rank * groups),
            transcendentals=0,
        ),
        name="low",
    )(at, token_slot, gathered, *downs)
    low, gathered = lax.optimization_barrier((low, gathered))
    low = sum_over(low, "tp")

    base = None
    parts, block = 4, 512
    steps = width // parts // block
    whole = pl.BlockSpec((tok_all, columns), lambda i: (0, 0))
    for part in range(parts):
        base = pl.pallas_call(
            base_kernel,
            grid=(steps,),
            out_shape=jax.ShapeDtypeStruct((tok_all, columns), jnp.float32),
            in_specs=[
                pl.BlockSpec((tok_all, block), lambda i, part=part: (0, part * steps + i)),
                pl.BlockSpec((block, columns), lambda i, part=part: (part * steps + i, 0)),
            ]
            + ([] if base is None else [whole]),
            out_specs=whole,
            compiler_params=pltpu.CompilerParams(vmem_limit_bytes=48 * 2**20),
            cost_estimate=pl.CostEstimate(
                flops=2 * tok_all * columns * width // parts,
                bytes_accessed=2 * columns * width // parts,
                transcendentals=0,
            ),
            name="base",
        )(gathered, base_projection_weight, *([] if base is None else [base]))
    panels = [part.reshape(tp * rank_portion, columns) for row in ups for part in row]
    out = pl.pallas_call(
        functools.partial(lift_kernel, reps, groups),
        out_shape=jax.ShapeDtypeStruct((tok_all, columns), jnp.bfloat16),
        in_specs=[pl.BlockSpec(memory_space=pltpu.SMEM)]
        + [in_vmem] * (3 + len(panels)),
        out_specs=in_vmem,
        cost_estimate=pl.CostEstimate(
            flops=2 * tok_all * columns * rank * groups * tp,
            bytes_accessed=2 * rank * groups * tp * columns + 6 * tok_all * columns,
            transcendentals=0,
        ),
        name="lift",
    )(at, token_slot, low, base, *panels)
    return out[None]


def solution(mesh):
    return jax.shard_map(
        on_device,
        mesh=mesh,
        in_specs=(
            P(("rep", "grp"), "tp", None),
            P(None, "tp"),
            P(("grp", "tp"), None, None),
            P(("grp", "tp"), None, None),
            P("rep", None),
            P(("rep", "grp"), None),
            P(),
        ),
        out_specs=P(("rep", "grp"), None, "tp"),
        check_vma=False,
    )
```

```python
import functools

import jax
import jax.numpy as jnp
from jax import lax
from jax.experimental import pallas as pl
from jax.experimental.pallas import tpu as pltpu
from jax.sharding import PartitionSpec as P

adapter_scale = 1.0


def swapped(x, axis):
    n = lax.axis_size(axis)
    return [x] + [
        lax.ppermute(x, axis, [((i + s) % n, i) for i in range(n)]) for s in range(1, n)
    ]


def ring_of(n):
    return list(range(0, n, 2)) + list(range(1, n, 2))[::-1]


class Ring:
    def __init__(self, block, axis, last_from_behind):
        n = lax.axis_size(axis)
        ring = ring_of(n)
        self.n, self.axis, self.last_from_behind = n, axis, last_from_behind
        self.up = [(ring[i], ring[(i + 1) % n]) for i in range(n)]
        self.down = [(ring[(i + 1) % n], ring[i]) for i in range(n)]
        self.ahead = self.behind = block
        self.pieces = [block]

    def step(self, i):
        last = i == self.n // 2
        if not last or self.last_from_behind:
            self.ahead = lax.ppermute(self.ahead, self.axis, self.up)
            self.pieces.append(self.ahead)
        if not last or not self.last_from_behind:
            self.behind = lax.ppermute(self.behind, self.axis, self.down)
            self.pieces.append(self.behind)

    def wait_for(self, value):
        self.ahead, self.behind, value = lax.optimization_barrier(
            (self.ahead, self.behind, value)
        )
        return value


def ring_sources(axis):
    n = lax.axis_size(axis)
    me = lax.axis_index(axis)
    place = jnp.where(me % 2 == 0, me // 2, n - 1 - me // 2)
    distances = [0] + [d for i in range(1, n // 2) for d in (i, -i)] + [n // 2]
    sources = []
    for distance in distances:
        at = lax.rem(place - distance + n, n)
        sources.append(jnp.where(at < n // 2, 2 * at, 2 * (n - 1 - at) + 1))
    return sources


def sum_over(x, axis):
    n = lax.axis_size(axis)
    if n & (n - 1):
        return lax.psum(x, axis)
    shift = 1
    while shift < n:
        x = x + lax.ppermute(x, axis, [(i, i ^ shift) for i in range(n)])
        shift *= 2
    return x


def cut_kernel(parts, columns, at_ref, panel_ref, out_ref):
    rows = pl.ds(pl.multiple_of(at_ref[0], out_ref.shape[1]), out_ref.shape[1])
    for part in range(parts):
        out_ref[part] = panel_ref[rows, part * columns : (part + 1) * columns]


def halve_kernel(block_ref, *out_refs):
    width = out_refs[0].shape[1]
    for i, out_ref in enumerate(out_refs):
        out_ref[...] = block_ref[:, i * width : (i + 1) * width]


def low_kernel(reps, groups, tp, at_ref, slot_ref, *refs):
    pieces, refs = refs[:tp], refs[tp:]
    before, downs = refs[: -groups - 2], refs[-groups - 2 : -2]
    tokens_ref, out_ref = refs[-2:]
    rows = pieces[0].shape[0]
    for i, piece in enumerate(pieces):
        start = pl.multiple_of(at_ref[reps + groups + 1 + i] * rows, rows)
        tokens_ref[pl.ds(start, rows), :] = piece[...]
    last = bool(before)
    total = None
    for s, down in enumerate(downs):
        product = lax.dot_general(
            tokens_ref[...], down[...], (((1,), (1,)), ((), ())),
            preferred_element_type=jnp.float32,
        )
        if last:
            product = product + before[0][s]
            mine = slot_ref[...] == at_ref[reps + s] + at_ref[reps + groups]
            total = jnp.where(mine, product, 0.0 if total is None else total)
        else:
            out_ref[s] = product
    if last:
        out_ref[...] = total.astype(out_ref.dtype)


def lift_kernel(reps, groups, at_ref, slot_ref, low_ref, base_ref, *refs):
    ups, out_ref = refs[:-1], refs[-1]
    depth = ups[0].shape[0]
    rank = low_ref.shape[1]
    rank_portion = rank // reps
    low = low_ref[...]
    token_slot = slot_ref[...]
    row = lax.broadcasted_iota(jnp.int32, (rank, depth), 0)
    column = lax.broadcasted_iota(jnp.int32, (rank, depth), 1)
    lane = lax.broadcasted_iota(jnp.int32, (low.shape[0], depth), 1)
    total = base_ref[...]
    for r in range(reps):
        spread = (row == at_ref[r] + lax.rem(column, rank_portion)).astype(jnp.bfloat16)
        wide = jnp.dot(low, spread, preferred_element_type=jnp.float32)
        for s in range(groups):
            chosen = token_slot == at_ref[reps + s] + lane // rank_portion
            expanded = jnp.where(chosen, wide, 0.0).astype(jnp.bfloat16)
            total = total + adapter_scale * jnp.dot(
                expanded, ups[r * groups + s][...], preferred_element_type=jnp.float32
            )
    out_ref[...] = total.astype(out_ref.dtype)


def on_device(
    tokens,
    base_projection_weight,
    adapter_down_panels,
    adapter_up_panels,
    request_adapter_ids,
    request_token_lengths,
    adapter_store_slot,
):
    groups = lax.axis_size("grp")
    tp = lax.axis_size("tp")
    reps = lax.axis_size("rep")
    my_group = lax.axis_index("grp")
    my_tp = lax.axis_index("tp")
    my_rep = lax.axis_index("rep")
    rank = adapter_down_panels.shape[2]
    rank_portion = rank // reps
    columns = base_projection_weight.shape[1]
    store_size = adapter_store_slot.shape[0]
    tok_all = tokens.shape[1] * tp
    width = tokens.shape[2]
    in_vmem = pl.BlockSpec(memory_space=pltpu.VMEM)

    downs = swapped(jnp.transpose(adapter_down_panels[0]), "grp")

    up_send = pl.pallas_call(
        functools.partial(cut_kernel, tp, columns),
        out_shape=jax.ShapeDtypeStruct((tp, rank_portion, columns), jnp.bfloat16),
        in_specs=[pl.BlockSpec(memory_space=pltpu.SMEM), in_vmem],
        out_specs=in_vmem,
        compiler_params=pltpu.CompilerParams(vmem_limit_bytes=16 * 2**20),
        name="cut",
    )((my_rep * rank_portion).astype(jnp.int32).reshape(1), adapter_up_panels[0])
    up_got = lax.all_to_all(up_send, "tp", split_axis=0, concat_axis=0, tiled=True)

    half = width // 2
    steps = tp // 2
    halves = pl.pallas_call(
        halve_kernel,
        out_shape=[jax.ShapeDtypeStruct((tokens.shape[1], half), jnp.bfloat16)] * 2,
        in_specs=[in_vmem],
        out_specs=[in_vmem] * 2,
        compiler_params=pltpu.CompilerParams(vmem_limit_bytes=16 * 2**20),
        name="halve",
    )(tokens[0])
    rings = [Ring(part, "tp", k == 0) for k, part in enumerate(halves)]
    rings[0].step(1)
    rings[1].wait_for(rings[0].ahead)
    for i in range(2, steps + 1):
        rings[0].step(i)
        rings[1].step(i - 1)
    up_got = rings[1].wait_for(up_got)
    rings[1].step(steps)

    ids = jnp.arange(store_size, dtype=jnp.int32)
    my_ids = lax.dynamic_index_in_dim(request_adapter_ids, my_group, 0, keepdims=False)
    my_slots = jnp.sum(
        jnp.where(my_ids[:, None] == ids[None, :], adapter_store_slot[None, :], 0), axis=-1
    )
    lengths = request_token_lengths[0]
    ends = jnp.cumsum(lengths)
    starts = ends - lengths
    position = jnp.arange(tok_all, dtype=jnp.int32)[:, None]
    member = (position >= starts[None, :]) & (position < ends[None, :])
    token_slot = jnp.sum(jnp.where(member, my_slots[None, :], 0), axis=1)

    at = jnp.stack(
        [lax.rem(my_rep + r, reps) * rank_portion for r in range(reps)]
        + [lax.rem(my_group + s, groups) * tp for s in range(groups)]
        + [my_tp]
        + ring_sources("tp")
    ).astype(jnp.int32)
    token_slot = token_slot[:, None]
    low = base = None
    for k, ring in enumerate(rings):
        last = k == len(rings) - 1
        gathered, low = pl.pallas_call(
            functools.partial(low_kernel, reps, groups, tp),
            out_shape=[
                jax.ShapeDtypeStruct((tok_all, half), jnp.bfloat16),
                jax.ShapeDtypeStruct((tok_all, rank), jnp.bfloat16)
                if last
                else jax.ShapeDtypeStruct((groups, tok_all, rank), jnp.float32),
            ],
            in_specs=[pl.BlockSpec(memory_space=pltpu.SMEM)]
            + [in_vmem] * (1 + tp + k + groups),
            out_specs=[in_vmem] * 2,
            compiler_params=pltpu.CompilerParams(vmem_limit_bytes=16 * 2**20),
            cost_estimate=pl.CostEstimate(
                flops=2 * tok_all * half * rank * groups,
                bytes_accessed=2 * half * (tok_all + rank * groups),
                transcendentals=0,
            ),
            name="low",
        )(
            at,
            token_slot,
            *ring.pieces,
            *([low] if last else []),
            *[down[:, k * half : (k + 1) * half] for down in downs],
        )
        if last:
            across = swapped(up_got, "rep")
            own = swapped(up_got, "grp")
            low, gathered, *across = lax.optimization_barrier((low, gathered, *across))
            ups = [own] + [swapped(part, "grp") for part in across[1:]]
            low = sum_over(low, "tp")
        product = jnp.dot(
            gathered,
            base_projection_weight[k * half : (k + 1) * half],
            preferred_element_type=jnp.float32,
        )
        base = product if base is None else base + product
        if not last:
            low, base = lax.optimization_barrier((low, base))

    panels = [part.reshape(tp * rank_portion, columns) for row in ups for part in row]
    out = pl.pallas_call(
        functools.partial(lift_kernel, reps, groups),
        out_shape=jax.ShapeDtypeStruct((tok_all, columns), jnp.bfloat16),
        in_specs=[pl.BlockSpec(memory_space=pltpu.SMEM)]
        + [in_vmem] * (3 + len(panels)),
        out_specs=in_vmem,
        cost_estimate=pl.CostEstimate(
            flops=2 * tok_all * columns * rank * groups * tp,
            bytes_accessed=2 * rank * groups * tp * columns + 6 * tok_all * columns,
            transcendentals=0,
        ),
        compiler_params=pltpu.CompilerParams(vmem_limit_bytes=16 * 2**20),
        name="lift",
    )(at, token_slot, low, base, *panels)
    return out[None]


def solution(mesh):
    return jax.shard_map(
        on_device,
        mesh=mesh,
        in_specs=(
            P(("rep", "grp"), "tp", None),
            P(None, "tp"),
            P(("grp", "tp"), None, None),
            P(("grp", "tp"), None, None),
            P("rep", None),
            P(("rep", "grp"), None),
            P(),
        ),
        out_specs=P(("rep", "grp"), None, "tp"),
        check_vma=False,
    )
```

```python
import functools

import jax
import jax.numpy as jnp
from jax import lax
from jax.experimental import pallas as pl
from jax.experimental.pallas import tpu as pltpu
from jax.sharding import PartitionSpec as P

adapter_scale = 1.0


def swapped(x, axis):
    n = lax.axis_size(axis)
    return [x] + [
        lax.ppermute(x, axis, [((i + s) % n, i) for i in range(n)]) for s in range(1, n)
    ]


def ring_of(n):
    return list(range(0, n, 2)) + list(range(1, n, 2))[::-1]


class Ring:
    def __init__(self, block, axis, last_from_behind):
        n = lax.axis_size(axis)
        ring = ring_of(n)
        self.n, self.axis, self.last_from_behind = n, axis, last_from_behind
        self.up = [(ring[i], ring[(i + 1) % n]) for i in range(n)]
        self.down = [(ring[(i + 1) % n], ring[i]) for i in range(n)]
        self.ahead = self.behind = block
        self.pieces = [block]

    def step(self, i):
        last = i == self.n // 2
        if not last or self.last_from_behind:
            self.ahead = lax.ppermute(self.ahead, self.axis, self.up)
            self.pieces.append(self.ahead)
        if not last or not self.last_from_behind:
            self.behind = lax.ppermute(self.behind, self.axis, self.down)
            self.pieces.append(self.behind)

    def wait_for(self, value):
        self.ahead, self.behind, value = lax.optimization_barrier(
            (self.ahead, self.behind, value)
        )
        return value


def ring_sources(axis):
    n = lax.axis_size(axis)
    me = lax.axis_index(axis)
    place = jnp.where(me % 2 == 0, me // 2, n - 1 - me // 2)
    distances = [0] + [d for i in range(1, n // 2) for d in (i, -i)] + [n // 2]
    sources = []
    for distance in distances:
        at = lax.rem(place - distance + n, n)
        sources.append(jnp.where(at < n // 2, 2 * at, 2 * (n - 1 - at) + 1))
    return sources


def halve_kernel(block_ref, *out_refs):
    width = out_refs[0].shape[1]
    for i, out_ref in enumerate(out_refs):
        out_ref[...] = block_ref[:, i * width : (i + 1) * width]


def stack_kernel(groups, *refs):
    downs, ups, (down_ref, up_ref) = refs[:groups], refs[groups:-2], refs[-2:]
    rank = ups[0].shape[0]
    down_ref[...] = jnp.concatenate([down[...] for down in downs], axis=0).T
    for s, up in enumerate(ups):
        up_ref[s * rank : (s + 1) * rank, :] = up[...]


def lift_kernel(tp, at_ref, place_ref, down_ref, up_ref, *refs):
    pieces, (tokens_ref, out_ref) = refs[:-2], refs[-2:]
    rows, width = pieces[0].shape
    per_half = len(pieces) // 2
    for i, piece in enumerate(pieces):
        start = pl.multiple_of(at_ref[1 + i % per_half] * rows, rows)
        column = i // per_half * width
        tokens_ref[pl.ds(start, rows), column : column + width] = piece[...]
    low = jnp.dot(tokens_ref[...], down_ref[...], preferred_element_type=jnp.float32)
    low = low.astype(jnp.bfloat16)
    slots, columns = out_ref.shape[1], out_ref.shape[2]
    all_ranks = up_ref.shape[0]
    here = lax.broadcasted_iota(jnp.int32, (slots, low.shape[0]), 0) + at_ref[0]
    chosen = (here == place_ref[...]).astype(jnp.bfloat16)
    picked = jnp.dot(chosen, low, preferred_element_type=jnp.float32)
    panels = slots // (tokens_ref.shape[0] // 8)
    row_panel = lax.broadcasted_iota(jnp.int32, picked.shape, 0) // (slots // panels)
    rank_panel = lax.broadcasted_iota(jnp.int32, picked.shape, 1) // (all_ranks // panels)
    picked = jnp.where(row_panel == rank_panel, picked, 0.0).astype(jnp.bfloat16)
    for part in range(tp):
        out_ref[part] = jnp.dot(
            picked,
            up_ref[:, part * columns : (part + 1) * columns],
            preferred_element_type=jnp.float32,
        ).astype(out_ref.dtype)


def add_kernel(place_ref, base_ref, lifts_ref, out_ref):
    place = lax.broadcasted_iota(jnp.int32, (base_ref.shape[0], lifts_ref.shape[0]), 1)
    chosen = (place == place_ref[...]).astype(jnp.bfloat16)
    lift = jnp.dot(chosen, lifts_ref[...], preferred_element_type=jnp.float32)
    out_ref[...] = (base_ref[...] + adapter_scale * lift).astype(out_ref.dtype)


def on_device(
    tokens,
    base_projection_weight,
    adapter_down_panels,
    adapter_up_panels,
    request_adapter_ids,
    request_token_lengths,
    adapter_store_slot,
):
    groups = lax.axis_size("grp")
    tp = lax.axis_size("tp")
    my_group = lax.axis_index("grp")
    my_tp = lax.axis_index("tp")
    width, rank = adapter_down_panels.shape[1:]
    columns = base_projection_weight.shape[1]
    store_size = adapter_store_slot.shape[0]
    tok_all = tokens.shape[1] * tp
    longest = tok_all // 8
    here = groups * longest
    half = width // 2
    in_vmem = pl.BlockSpec(memory_space=pltpu.VMEM)
    in_smem = pl.BlockSpec(memory_space=pltpu.SMEM)
    small = pltpu.CompilerParams(vmem_limit_bytes=16 * 2**20)

    halves = pl.pallas_call(
        halve_kernel,
        out_shape=[jax.ShapeDtypeStruct((tokens.shape[1], half), jnp.bfloat16)] * 2,
        in_specs=[in_vmem],
        out_specs=[in_vmem] * 2,
        compiler_params=small,
        name="halve",
    )(tokens[0])
    rings = [Ring(part, "tp", k == 0) for k, part in enumerate(halves)]
    for i in range(1, tp // 2 + 1):
        for ring in rings:
            ring.step(i)

    down_stack, up_stack = pl.pallas_call(
        functools.partial(stack_kernel, groups),
        out_shape=[
            jax.ShapeDtypeStruct((width, groups * rank), jnp.bfloat16),
            jax.ShapeDtypeStruct((groups * rank, tp * columns), jnp.bfloat16),
        ],
        in_specs=[in_vmem] * (2 * groups),
        out_specs=[in_vmem] * 2,
        compiler_params=pltpu.CompilerParams(vmem_limit_bytes=24 * 2**20),
        name="stack",
    )(
        *swapped(jnp.transpose(adapter_down_panels[0]), "grp"),
        *swapped(adapter_up_panels[0], "grp"),
    )

    ids = jnp.arange(store_size, dtype=jnp.int32)
    my_ids = lax.dynamic_index_in_dim(request_adapter_ids, my_group, 0, keepdims=False)
    my_slots = jnp.sum(
        jnp.where(my_ids[:, None] == ids[None, :], adapter_store_slot[None, :], 0), axis=-1
    )
    lengths = request_token_lengths[0]
    ends = jnp.cumsum(lengths)
    starts = ends - lengths
    panel = lax.rem(my_slots // tp - my_group + groups, groups)
    first = lax.rem(my_slots, tp) * here + panel * longest - starts
    position = jnp.arange(tok_all, dtype=jnp.int32)[:, None]
    member = (position >= starts[None, :]) & (position < ends[None, :])
    place = jnp.sum(jnp.where(member, first[None, :] + position, 0), axis=1)

    at = jnp.stack([my_tp * here] + ring_sources("tp")).astype(jnp.int32)
    gathered, lifts = pl.pallas_call(
        functools.partial(lift_kernel, tp),
        out_shape=[
            jax.ShapeDtypeStruct((tok_all, width), jnp.bfloat16),
            jax.ShapeDtypeStruct((tp, here, columns), jnp.bfloat16),
        ],
        in_specs=[in_smem] + [in_vmem] * (3 + 2 * tp),
        out_specs=[in_vmem] * 2,
        compiler_params=pltpu.CompilerParams(vmem_limit_bytes=24 * 2**20),
        cost_estimate=pl.CostEstimate(
            flops=2 * groups * rank * (tok_all * width + here * tp * columns),
            bytes_accessed=2 * groups * rank * (width + tp * columns),
            transcendentals=0,
        ),
        name="lift",
    )(at, place[None, :], down_stack, up_stack, *rings[0].pieces, *rings[1].pieces)
    lifts = lax.all_to_all(lifts, "tp", split_axis=0, concat_axis=0, tiled=True)

    base = jnp.dot(gathered, base_projection_weight, preferred_element_type=jnp.float32)
    out = pl.pallas_call(
        add_kernel,
        out_shape=jax.ShapeDtypeStruct((tok_all, columns), jnp.bfloat16),
        in_specs=[in_vmem] * 3,
        out_specs=in_vmem,
        compiler_params=small,
        name="add",
    )(place[:, None], base, lifts.reshape(tp * here, columns))
    return out[None]


def solution(mesh):
    return jax.shard_map(
        on_device,
        mesh=mesh,
        in_specs=(
            P(("rep", "grp"), "tp", None),
            P(None, "tp"),
            P(("grp", "tp"), None, None),
            P(("grp", "tp"), None, None),
            P("rep", None),
            P(("rep", "grp"), None),
            P(),
        ),
        out_specs=P(("rep", "grp"), None, "tp"),
        check_vma=False,
    )
```

```python
import functools

import jax
import jax.numpy as jnp
from jax import lax
from jax.experimental import pallas as pl
from jax.experimental.pallas import tpu as pltpu
from jax.sharding import PartitionSpec as P

adapter_scale = 1.0


def swapped(x, axis):
    n = lax.axis_size(axis)
    return [x] + [
        lax.ppermute(x, axis, [((i + s) % n, i) for i in range(n)]) for s in range(1, n)
    ]


def ring_of(n):
    return list(range(0, n, 2)) + list(range(1, n, 2))[::-1]


class Ring:
    def __init__(self, block, axis):
        n = lax.axis_size(axis)
        ring = ring_of(n)
        self.n, self.axis = n, axis
        self.up = [(ring[i], ring[(i + 1) % n]) for i in range(n)]
        self.down = [(ring[(i + 1) % n], ring[i]) for i in range(n)]
        self.ahead = self.behind = block
        self.pieces = [block]

    def step(self, i):
        if i == self.n // 2:
            half = self.ahead.shape[1] // 2
            self.ahead, self.behind = self.ahead[:, :half], self.behind[:, half:]
        self.ahead = lax.ppermute(self.ahead, self.axis, self.up)
        self.behind = lax.ppermute(self.behind, self.axis, self.down)
        self.pieces += [self.ahead, self.behind]

    def wait_for(self, *values):
        self.ahead, self.behind, *values = lax.optimization_barrier(
            (self.ahead, self.behind, *values)
        )
        return values


def ring_sources(axis):
    n = lax.axis_size(axis)
    me = lax.axis_index(axis)
    place = jnp.where(me % 2 == 0, me // 2, n - 1 - me // 2)
    distances = [0] + [d for i in range(1, n // 2) for d in (i, -i)] + [n // 2]
    sources = []
    for distance in distances:
        at = lax.rem(place - distance + n, n)
        sources.append(jnp.where(at < n // 2, 2 * at, 2 * (n - 1 - at) + 1))
    return sources


def stack_kernel(groups, *refs):
    downs, ups, (down_ref, up_ref) = refs[:groups], refs[groups:-2], refs[-2:]
    rank = ups[0].shape[0]
    down_ref[...] = jnp.concatenate([down[...] for down in downs], axis=0).T
    for s, up in enumerate(ups):
        up_ref[s * rank : (s + 1) * rank, :] = up[...]


def lift_kernel(tp, at_ref, place_ref, down_ref, up_ref, *refs):
    pieces, (tokens_ref, out_ref) = refs[:-2], refs[-2:]
    rows, half = pieces[-1].shape
    for i, piece in enumerate(pieces):
        opposite = i >= len(pieces) - 2
        start = pl.multiple_of(at_ref[1 + min(i, len(pieces) - 2)] * rows, rows)
        column = half if i == len(pieces) - 1 else 0
        size = half if opposite else 2 * half
        tokens_ref[pl.ds(start, rows), column : column + size] = piece[...]
    low = jnp.dot(tokens_ref[...], down_ref[...], preferred_element_type=jnp.float32)
    low = low.astype(jnp.bfloat16)
    slots, columns = out_ref.shape[1], out_ref.shape[2]
    all_ranks = up_ref.shape[0]
    here = lax.broadcasted_iota(jnp.int32, (slots, low.shape[0]), 0) + at_ref[0]
    chosen = (here == place_ref[...]).astype(jnp.bfloat16)
    picked = jnp.dot(chosen, low, preferred_element_type=jnp.float32)
    panels = slots // (tokens_ref.shape[0] // 8)
    row_panel = lax.broadcasted_iota(jnp.int32, picked.shape, 0) // (slots // panels)
    rank_panel = lax.broadcasted_iota(jnp.int32, picked.shape, 1) // (all_ranks // panels)
    picked = jnp.where(row_panel == rank_panel, picked, 0.0).astype(jnp.bfloat16)
    for part in range(tp):
        out_ref[part] = jnp.dot(
            picked,
            up_ref[:, part * columns : (part + 1) * columns],
            preferred_element_type=jnp.float32,
        ).astype(out_ref.dtype)


def add_kernel(place_ref, base_ref, lifts_ref, out_ref):
    place = lax.broadcasted_iota(jnp.int32, (base_ref.shape[0], lifts_ref.shape[0]), 1)
    chosen = (place == place_ref[...]).astype(jnp.bfloat16)
    lift = jnp.dot(chosen, lifts_ref[...], preferred_element_type=jnp.float32)
    out_ref[...] = (base_ref[...] + adapter_scale * lift).astype(out_ref.dtype)


def on_device(
    tokens,
    base_projection_weight,
    adapter_down_panels,
    adapter_up_panels,
    request_adapter_ids,
    request_token_lengths,
    adapter_store_slot,
):
    groups = lax.axis_size("grp")
    tp = lax.axis_size("tp")
    my_group = lax.axis_index("grp")
    my_tp = lax.axis_index("tp")
    width, rank = adapter_down_panels.shape[1:]
    columns = base_projection_weight.shape[1]
    store_size = adapter_store_slot.shape[0]
    tok_all = tokens.shape[1] * tp
    longest = tok_all // 8
    here = groups * longest
    in_vmem = pl.BlockSpec(memory_space=pltpu.VMEM)
    in_smem = pl.BlockSpec(memory_space=pltpu.SMEM)
    small = pltpu.CompilerParams(vmem_limit_bytes=16 * 2**20)

    ring = Ring(tokens[0], "tp")
    ring.step(1)
    ring.step(2)

    down_stack, up_stack = pl.pallas_call(
        functools.partial(stack_kernel, groups),
        out_shape=[
            jax.ShapeDtypeStruct((width, groups * rank), jnp.bfloat16),
            jax.ShapeDtypeStruct((groups * rank, tp * columns), jnp.bfloat16),
        ],
        in_specs=[in_vmem] * (2 * groups),
        out_specs=[in_vmem] * 2,
        compiler_params=pltpu.CompilerParams(vmem_limit_bytes=24 * 2**20),
        name="stack",
    )(
        *swapped(jnp.transpose(adapter_down_panels[0]), "grp"),
        *swapped(adapter_up_panels[0], "grp"),
    )

    ids = jnp.arange(store_size, dtype=jnp.int32)
    my_ids = lax.dynamic_index_in_dim(request_adapter_ids, my_group, 0, keepdims=False)
    my_slots = jnp.sum(
        jnp.where(my_ids[:, None] == ids[None, :], adapter_store_slot[None, :], 0), axis=-1
    )
    lengths = request_token_lengths[0]
    ends = jnp.cumsum(lengths)
    starts = ends - lengths
    panel = lax.rem(my_slots // tp - my_group + groups, groups)
    first = lax.rem(my_slots, tp) * here + panel * longest - starts
    position = jnp.arange(tok_all, dtype=jnp.int32)[:, None]
    member = (position >= starts[None, :]) & (position < ends[None, :])
    place = jnp.sum(jnp.where(member, first[None, :] + position, 0), axis=1)

    at = jnp.stack([my_tp * here] + ring_sources("tp")).astype(jnp.int32)
    down_stack, up_stack, place, at = ring.wait_for(down_stack, up_stack, place, at)
    for i in range(3, tp // 2 + 1):
        ring.step(i)
    gathered, lifts = pl.pallas_call(
        functools.partial(lift_kernel, tp),
        out_shape=[
            jax.ShapeDtypeStruct((tok_all, width), jnp.bfloat16),
            jax.ShapeDtypeStruct((tp, here, columns), jnp.bfloat16),
        ],
        in_specs=[in_smem] + [in_vmem] * (3 + len(ring.pieces)),
        out_specs=[in_vmem] * 2,
        compiler_params=pltpu.CompilerParams(vmem_limit_bytes=24 * 2**20),
        cost_estimate=pl.CostEstimate(
            flops=2 * groups * rank * (tok_all * width + here * tp * columns),
            bytes_accessed=2 * groups * rank * (width + tp * columns),
            transcendentals=0,
        ),
        name="lift",
    )(at, place[None, :], down_stack, up_stack, *ring.pieces)
    lifts = lax.all_to_all(lifts, "tp", split_axis=0, concat_axis=0, tiled=True)

    base = jnp.dot(gathered, base_projection_weight, preferred_element_type=jnp.float32)
    out = pl.pallas_call(
        add_kernel,
        out_shape=jax.ShapeDtypeStruct((tok_all, columns), jnp.bfloat16),
        in_specs=[in_vmem] * 3,
        out_specs=in_vmem,
        compiler_params=small,
        name="add",
    )(place[:, None], base, lifts.reshape(tp * here, columns))
    return out[None]


def solution(mesh):
    return jax.shard_map(
        on_device,
        mesh=mesh,
        in_specs=(
            P(("rep", "grp"), "tp", None),
            P(None, "tp"),
            P(("grp", "tp"), None, None),
            P(("grp", "tp"), None, None),
            P("rep", None),
            P(("rep", "grp"), None),
            P(),
        ),
        out_specs=P(("rep", "grp"), None, "tp"),
        check_vma=False,
    )
```

```python
import functools

import jax
import jax.numpy as jnp
from jax import lax
from jax.experimental import pallas as pl
from jax.experimental.pallas import tpu as pltpu
from jax.sharding import PartitionSpec as P

adapter_scale = 1.0


def swapped(x, axis):
    n = lax.axis_size(axis)
    return [x] + [
        lax.ppermute(x, axis, [((i + s) % n, i) for i in range(n)]) for s in range(1, n)
    ]


def ring_of(n):
    return list(range(0, n, 2)) + list(range(1, n, 2))[::-1]


def ring_gather(block, rows_axis, pair_axis):
    n = lax.axis_size(rows_axis)
    ring = ring_of(n)
    pair = lax.axis_index(pair_axis)
    me = lax.axis_index(rows_axis)
    place = jnp.where(me % 2 == 0, me // 2, n - 1 - me // 2)
    half = block.shape[1] // 2
    onward = []
    for i in range(n):
        onward.append((ring[i], ring[(i + 1) % n]))
        onward.append((n + ring[(i + 1) % n], n + ring[i]))

    def sent(x):
        return lax.ppermute(x, (pair_axis, rows_axis), onward)

    def handed(x):
        return lax.ppermute(x, pair_axis, [(0, 1), (1, 0)])

    def cut(x):
        return jnp.where(pair == 0, x[:, :half], x[:, half:])

    def source(distance):
        at = lax.rem(place - distance + 2 * n, n)
        return jnp.where(at < n // 2, 2 * at, 2 * (n - 1 - at) + 1)

    way = 1 - 2 * pair
    mine = block
    other = first = handed(block)
    pieces, sources = [block], [source(0)]
    for step in range(1, n // 2 + 1):
        if step == n // 2:
            mine, other = cut(mine), cut(other)
        mine, other = sent(mine), sent(other)
        pieces += [mine, handed(other)]
        sources += [source(way * step), source(-way * step)]
    return pieces, sources, [pair * half, (1 - pair) * half], first


def fetch_kernel(after_ref, *refs):
    n = len(refs) // 2
    copies = [
        pltpu.make_async_copy(refs[i], refs[n + i], refs[2 * n].at[i]) for i in range(n)
    ]
    for copy in copies:
        copy.start()
    for copy in copies:
        copy.wait()


def lift_kernel(groups, at_ref, place_ref, *refs):
    downs, ups, pieces = refs[:groups], refs[groups : 2 * groups], refs[2 * groups : -3]
    tokens_ref, out_ref, up_ref = refs[-3:]
    rows, half = pieces[-1].shape
    for i, piece in enumerate(pieces):
        start = pl.multiple_of(at_ref[1 + i] * rows, rows)
        last = len(pieces) - 1 - i
        if last > 1:
            tokens_ref[pl.ds(start, rows), :] = piece[...]
        else:
            column = pl.multiple_of(at_ref[2 + len(pieces) - last], half)
            tokens_ref[pl.ds(start, rows), pl.ds(column, half)] = piece[...]
    rank = ups[0].shape[0]
    for s, up in enumerate(ups):
        up_ref[s * rank : (s + 1) * rank, :] = up[...]
    down = jnp.concatenate([down[...] for down in downs], axis=0).T
    low = jnp.dot(tokens_ref[...], down, preferred_element_type=jnp.float32)
    low = low.astype(jnp.bfloat16)
    parts, slots, columns = out_ref.shape
    here = lax.broadcasted_iota(jnp.int32, (slots, low.shape[0]), 0) + at_ref[0]
    chosen = (here == place_ref[...]).astype(jnp.bfloat16)
    picked = jnp.dot(chosen, low, preferred_element_type=jnp.float32)
    row_panel = lax.broadcasted_iota(jnp.int32, picked.shape, 0) // (slots // groups)
    rank_panel = lax.broadcasted_iota(jnp.int32, picked.shape, 1) // rank
    picked = jnp.where(row_panel == rank_panel, picked, 0.0).astype(jnp.bfloat16)
    for part in range(parts):
        out_ref[part] = jnp.dot(
            picked,
            up_ref[:, part * columns : (part + 1) * columns],
            preferred_element_type=jnp.float32,
        ).astype(out_ref.dtype)


def add_kernel(place_ref, base_ref, lifts_ref, out_ref):
    place = lax.broadcasted_iota(jnp.int32, (base_ref.shape[0], lifts_ref.shape[0]), 1)
    chosen = (place == place_ref[...]).astype(jnp.bfloat16)
    lift = jnp.dot(chosen, lifts_ref[...], preferred_element_type=jnp.float32)
    out_ref[...] = (base_ref[...] + adapter_scale * lift).astype(out_ref.dtype)


def on_device(
    tokens,
    base_projection_weight,
    adapter_down_panels,
    adapter_up_panels,
    request_adapter_ids,
    request_token_lengths,
    adapter_store_slot,
):
    groups = lax.axis_size("grp")
    tp = lax.axis_size("tp")
    my_group = lax.axis_index("grp")
    my_tp = lax.axis_index("tp")
    width, rank = adapter_down_panels.shape[1:]
    columns = base_projection_weight.shape[1]
    store_size = adapter_store_slot.shape[0]
    tok_all = tokens.shape[1] * tp
    longest = tok_all // 8
    here = groups * longest
    in_vmem = pl.BlockSpec(memory_space=pltpu.VMEM)
    in_smem = pl.BlockSpec(memory_space=pltpu.SMEM)
    small = pltpu.CompilerParams(vmem_limit_bytes=16 * 2**20)

    pieces, sources, cuts, first_handed = ring_gather(tokens[0], "tp", "grp")

    down, up = adapter_down_panels[0].T, adapter_up_panels[0]
    down, up = pl.pallas_call(
        fetch_kernel,
        out_shape=[jax.ShapeDtypeStruct(x.shape, x.dtype) for x in (down, up)],
        in_specs=[pl.BlockSpec(memory_space=pl.ANY)] * 3,
        out_specs=[in_vmem] * 2,
        scratch_shapes=[pltpu.SemaphoreType.DMA((2,))],
        compiler_params=small,
        name="fetch",
    )(first_handed, down, up)
    panels = swapped(down, "grp") + swapped(up, "grp")

    ids = jnp.arange(store_size, dtype=jnp.int32)
    my_ids = lax.dynamic_index_in_dim(request_adapter_ids, my_group, 0, keepdims=False)
    my_slots = jnp.sum(
        jnp.where(my_ids[:, None] == ids[None, :], adapter_store_slot[None, :], 0), axis=-1
    )
    lengths = request_token_lengths[0]
    ends = jnp.cumsum(lengths)
    starts = ends - lengths
    panel = lax.rem(my_slots // tp - my_group + groups, groups)
    first = lax.rem(my_slots, tp) * here + panel * longest - starts
    position = jnp.arange(tok_all, dtype=jnp.int32)[:, None]
    member = (position >= starts[None, :]) & (position < ends[None, :])
    place = jnp.sum(jnp.where(member, first[None, :] + position, 0), axis=1)

    at = jnp.stack([my_tp * here] + sources + cuts).astype(jnp.int32)
    gathered, lifts = pl.pallas_call(
        functools.partial(lift_kernel, groups),
        out_shape=[
            jax.ShapeDtypeStruct((tok_all, width), jnp.bfloat16),
            jax.ShapeDtypeStruct((tp, here, columns), jnp.bfloat16),
        ],
        in_specs=[in_smem] + [in_vmem] * (1 + len(panels) + len(pieces)),
        out_specs=[in_vmem] * 2,
        scratch_shapes=[pltpu.VMEM((groups * rank, tp * columns), jnp.bfloat16)],
        compiler_params=pltpu.CompilerParams(vmem_limit_bytes=24 * 2**20),
        cost_estimate=pl.CostEstimate(
            flops=2 * groups * rank * (tok_all * width + here * tp * columns),
            bytes_accessed=2 * groups * rank * (width + tp * columns),
            transcendentals=0,
        ),
        name="lift",
    )(at, place[None, :], *panels, *pieces)
    lifts = lax.all_to_all(lifts, "tp", split_axis=0, concat_axis=0, tiled=True)

    base = jnp.dot(gathered, base_projection_weight, preferred_element_type=jnp.float32)
    out = pl.pallas_call(
        add_kernel,
        out_shape=jax.ShapeDtypeStruct((tok_all, columns), jnp.bfloat16),
        in_specs=[in_vmem] * 3,
        out_specs=in_vmem,
        compiler_params=small,
        name="add",
    )(place[:, None], base, lifts.reshape(tp * here, columns))
    return out[None]


def solution(mesh):
    return jax.shard_map(
        on_device,
        mesh=mesh,
        in_specs=(
            P(("rep", "grp"), "tp", None),
            P(None, "tp"),
            P(("grp", "tp"), None, None),
            P(("grp", "tp"), None, None),
            P("rep", None),
            P(("rep", "grp"), None),
            P(),
        ),
        out_specs=P(("rep", "grp"), None, "tp"),
        check_vma=False,
    )
```

```python
import functools

import jax
import jax.numpy as jnp
from jax import lax
from jax.experimental import pallas as pl
from jax.experimental.pallas import tpu as pltpu
from jax.sharding import PartitionSpec as P

adapter_scale = 1.0


def swapped(x, axis):
    n = lax.axis_size(axis)
    return [x] + [
        lax.ppermute(x, axis, [((i + s) % n, i) for i in range(n)]) for s in range(1, n)
    ]


def ring_of(n):
    return list(range(0, n, 2)) + list(range(1, n, 2))[::-1]


def ring_gather(block):
    n = lax.axis_size("tp")
    ring = ring_of(n)
    onward = []
    for i in range(n):
        onward.append((ring[i], ring[(i + 1) % n]))
        onward.append((n + ring[(i + 1) % n], n + ring[i]))

    def sent(x):
        return lax.ppermute(x, ("grp", "tp"), onward)

    def handed(x):
        return lax.ppermute(x, "grp", [(0, 1), (1, 0)])

    mine, other = block, handed(block)
    pieces = [block]
    for step in range(1, n // 2):
        mine, other = sent(mine), sent(other)
        pieces += [mine, handed(other)]
    return pieces + [sent(mine)]


def ring_sources(n):
    me = lax.axis_index("tp")
    way = 1 - 2 * lax.axis_index("grp")
    place = jnp.where(lax.rem(me, 2) == 0, me // 2, n - 1 - me // 2)
    distances = [0] + [d for i in range(1, n // 2) for d in (way * i, -way * i)] + [n // 2]
    sources = []
    for distance in distances:
        at = lax.rem(place - distance + 2 * n, n)
        sources.append(jnp.where(at < n // 2, 2 * at, 2 * (n - 1 - at) + 1))
    return sources


def places_of(position, tp, groups, longest, ids_ref, lengths_ref, slots_ref):
    group = lax.axis_index("grp")

    def add(request, carry):
        start, place = carry
        slot = slots_ref[ids_ref[group, request]]
        end = start + lengths_ref[0, request]
        panel = lax.rem(slot // tp - group + groups, groups)
        first = (lax.rem(slot, tp) * groups + panel) * longest - start
        here = (position >= start) & (position < end)
        return end, jnp.where(here, first + position, place)

    carry = (jnp.int32(0), jnp.zeros_like(position))
    return lax.fori_loop(0, ids_ref.shape[1], add, carry)[1]


def lift_kernel(groups, tp, ids_ref, lengths_ref, slots_ref, *refs):
    downs, ups, pieces = refs[:groups], refs[groups : 2 * groups], refs[2 * groups : -5]
    tokens_ref, out_ref, down_ref, up_ref, sems = refs[-5:]
    rank = ups[0].shape[0]
    rows = pieces[0].shape[0]
    parts, slots, columns = out_ref.shape
    copies = [
        pltpu.make_async_copy(down, down_ref.at[pl.ds(s * rank, rank)], sems.at[s])
        for s, down in enumerate(downs)
    ]
    for i, (piece, source) in enumerate(zip(pieces, ring_sources(tp))):
        at = pl.ds(pl.multiple_of(source * rows, rows), rows)
        copies.append(
            pltpu.make_async_copy(piece, tokens_ref.at[at], sems.at[groups + i])
        )
    up_copies = [
        pltpu.make_async_copy(
            up, up_ref.at[pl.ds(s * rank, rank)], sems.at[groups + len(pieces) + s]
        )
        for s, up in enumerate(ups)
    ]
    for copy in copies + up_copies:
        copy.start()
    tok_all = tokens_ref.shape[0]
    position = lax.broadcasted_iota(jnp.int32, (1, tok_all), 1)
    place = places_of(position, tp, groups, slots // groups, ids_ref, lengths_ref, slots_ref)
    here = lax.broadcasted_iota(jnp.int32, (slots, tok_all), 0) + lax.axis_index("tp") * slots
    chosen = (here == place).astype(jnp.bfloat16)
    for copy in copies:
        copy.wait()
    low = jnp.dot(tokens_ref[...], down_ref[...].T, preferred_element_type=jnp.float32)
    picked = jnp.dot(chosen, low.astype(jnp.bfloat16), preferred_element_type=jnp.float32)
    row_panel = lax.broadcasted_iota(jnp.int32, picked.shape, 0) // (slots // groups)
    rank_panel = lax.broadcasted_iota(jnp.int32, picked.shape, 1) // rank
    picked = jnp.where(row_panel == rank_panel, picked, 0.0).astype(jnp.bfloat16)
    for copy in up_copies:
        copy.wait()
    for part in range(parts):
        out_ref[part] = jnp.dot(
            picked,
            up_ref[:, part * columns : (part + 1) * columns],
            preferred_element_type=jnp.float32,
        ).astype(out_ref.dtype)


def add_kernel(groups, tp, ids_ref, lengths_ref, slots_ref, base_ref, lifts_ref, out_ref):
    tok_all, rows = base_ref.shape[0], lifts_ref.shape[0]
    position = lax.broadcasted_iota(jnp.int32, (tok_all, 1), 0)
    place = places_of(
        position, tp, groups, rows // tp // groups, ids_ref, lengths_ref, slots_ref
    )
    chosen = lax.broadcasted_iota(jnp.int32, (tok_all, rows), 1) == place
    lift = jnp.dot(
        chosen.astype(jnp.bfloat16), lifts_ref[...], preferred_element_type=jnp.float32
    )
    out_ref[...] = (base_ref[...] + adapter_scale * lift).astype(out_ref.dtype)


def on_device(
    tokens,
    base_projection_weight,
    adapter_down_panels,
    adapter_up_panels,
    request_adapter_ids,
    request_token_lengths,
    adapter_store_slot,
):
    groups = lax.axis_size("grp")
    tp = lax.axis_size("tp")
    width, rank = adapter_down_panels.shape[1:]
    columns = base_projection_weight.shape[1]
    tok_all = tokens.shape[1] * tp
    longest = tok_all // 8
    here = groups * longest
    in_hbm = pl.BlockSpec(memory_space=pltpu.HBM)
    in_vmem = pl.BlockSpec(memory_space=pltpu.VMEM)
    in_smem = pl.BlockSpec(memory_space=pltpu.SMEM)
    requests = (request_adapter_ids, request_token_lengths, adapter_store_slot)

    pieces = ring_gather(tokens[0])
    panels = swapped(adapter_down_panels[0].T, "grp") + swapped(adapter_up_panels[0], "grp")

    gathered, lifts = pl.pallas_call(
        functools.partial(lift_kernel, groups, tp),
        out_shape=[
            jax.ShapeDtypeStruct((tok_all, width), jnp.bfloat16),
            jax.ShapeDtypeStruct((tp, here, columns), jnp.bfloat16),
        ],
        in_specs=[in_smem] * 3 + [in_hbm] * (len(panels) + len(pieces)),
        out_specs=[in_vmem] * 2,
        scratch_shapes=[
            pltpu.VMEM((groups * rank, width), jnp.bfloat16),
            pltpu.VMEM((groups * rank, tp * columns), jnp.bfloat16),
            pltpu.SemaphoreType.DMA((len(panels) + len(pieces),)),
        ],
        compiler_params=pltpu.CompilerParams(vmem_limit_bytes=28 * 2**20),
        cost_estimate=pl.CostEstimate(
            flops=2 * groups * rank * (tok_all * width + here * tp * columns),
            bytes_accessed=2 * groups * rank * (width + tp * columns),
            transcendentals=0,
        ),
        name="lift",
    )(*requests, *panels, *pieces)
    lifts = lax.all_to_all(lifts, "tp", split_axis=0, concat_axis=0, tiled=True)

    base = jnp.dot(gathered, base_projection_weight, preferred_element_type=jnp.float32)
    out = pl.pallas_call(
        functools.partial(add_kernel, groups, tp),
        out_shape=jax.ShapeDtypeStruct((tok_all, columns), jnp.bfloat16),
        in_specs=[in_smem] * 3 + [in_vmem] * 2,
        out_specs=in_vmem,
        compiler_params=pltpu.CompilerParams(vmem_limit_bytes=16 * 2**20),
        name="add",
    )(*requests, base, lifts.reshape(tp * here, columns))
    return out[None]


def solution(mesh):
    return jax.shard_map(
        on_device,
        mesh=mesh,
        in_specs=(
            P(("rep", "grp"), "tp", None),
            P(None, "tp"),
            P(("grp", "tp"), None, None),
            P(("grp", "tp"), None, None),
            P("rep", None),
            P(("rep", "grp"), None),
            P(),
        ),
        out_specs=P(("rep", "grp"), None, "tp"),
        check_vma=False,
    )
```

```python
import functools

import jax
import jax.numpy as jnp
from jax import lax
from jax.experimental import pallas as pl
from jax.experimental.pallas import tpu as pltpu
from jax.sharding import PartitionSpec as P

adapter_scale = 1.0


def swapped(x, axis):
    n = lax.axis_size(axis)
    return [x] + [
        lax.ppermute(x, axis, [((i + s) % n, i) for i in range(n)]) for s in range(1, n)
    ]


def ring_of(n):
    return list(range(0, n, 2)) + list(range(1, n, 2))[::-1]


def ring_gather(block):
    n = lax.axis_size("tp")
    ring = ring_of(n)
    onward = []
    for i in range(n):
        onward.append((ring[i], ring[(i + 1) % n]))
        onward.append((n + ring[(i + 1) % n], n + ring[i]))

    def sent(x):
        return lax.ppermute(x, ("grp", "tp"), onward)

    def handed(x):
        return lax.ppermute(x, "grp", [(0, 1), (1, 0)])

    mine, other = block, handed(block)
    pieces = [block]
    for step in range(1, n // 2):
        mine, other = sent(mine), sent(other)
        pieces += [mine, handed(other)]
    return pieces + [sent(mine)]


def ring_sources(n):
    me = lax.axis_index("tp")
    way = 1 - 2 * lax.axis_index("grp")
    place = jnp.where(lax.rem(me, 2) == 0, me // 2, n - 1 - me // 2)
    distances = [0] + [d for i in range(1, n // 2) for d in (way * i, -way * i)] + [n // 2]
    sources = []
    for distance in distances:
        at = lax.rem(place - distance + 2 * n, n)
        sources.append(jnp.where(at < n // 2, 2 * at, 2 * (n - 1 - at) + 1))
    return sources


def prepare_kernel(groups, tp, ids_ref, lengths_ref, slots_ref, *refs):
    n = (len(refs) - 2) // 2
    row_ref, column_ref = refs[n : n + 2]
    for source, target in zip(refs[:n], refs[n + 2 :]):
        target[...] = source[...]
    group = lax.axis_index("grp")
    tok_all = row_ref.shape[1]
    longest = tok_all // 8
    along = lax.broadcasted_iota(jnp.int32, row_ref.shape, 1)
    down = lax.broadcasted_iota(jnp.int32, column_ref.shape, 0)

    def add(request, carry):
        start, row, column = carry
        slot = slots_ref[ids_ref[group, request]]
        end = start + lengths_ref[0, request]
        panel = lax.rem(slot // tp - group + groups, groups)
        first = (lax.rem(slot, tp) * groups + panel) * longest - start
        row = jnp.where((along >= start) & (along < end), first + along, row)
        column = jnp.where((down >= start) & (down < end), first + down, column)
        return end, row, column

    carry = (jnp.int32(0), jnp.zeros_like(along), jnp.zeros_like(down))
    _, row_ref[...], column_ref[...] = lax.fori_loop(0, ids_ref.shape[1], add, carry)


def lift_kernel(groups, tp, place_ref, *refs):
    downs, ups, pieces = refs[:groups], refs[groups : 2 * groups], refs[2 * groups : -3]
    tokens_ref, out_ref, up_ref = refs[-3:]
    rank = ups[0].shape[0]
    rows = pieces[0].shape[0]
    tok_all = tokens_ref.shape[0]
    parts, slots, columns = out_ref.shape
    for piece, source in zip(pieces, ring_sources(tp)):
        tokens_ref[pl.ds(pl.multiple_of(source * rows, rows), rows), :] = piece[...]
    for s, up in enumerate(ups):
        up_ref[s * rank : (s + 1) * rank, :] = up[...]
    down = jnp.concatenate([down[...] for down in downs], axis=0).T
    low = jnp.dot(tokens_ref[...], down, preferred_element_type=jnp.float32)
    here = lax.broadcasted_iota(jnp.int32, (slots, tok_all), 0) + lax.axis_index("tp") * slots
    chosen = (here == place_ref[...]).astype(jnp.bfloat16)
    picked = jnp.dot(chosen, low.astype(jnp.bfloat16), preferred_element_type=jnp.float32)
    row_panel = lax.broadcasted_iota(jnp.int32, picked.shape, 0) // (slots // groups)
    rank_panel = lax.broadcasted_iota(jnp.int32, picked.shape, 1) // rank
    picked = jnp.where(row_panel == rank_panel, picked, 0.0).astype(jnp.bfloat16)
    for part in range(parts):
        out_ref[part] = jnp.dot(
            picked,
            up_ref[:, part * columns : (part + 1) * columns],
            preferred_element_type=jnp.float32,
        ).astype(out_ref.dtype)


def add_kernel(place_ref, base_ref, lifts_ref, out_ref):
    place = lax.broadcasted_iota(jnp.int32, (base_ref.shape[0], lifts_ref.shape[0]), 1)
    chosen = (place == place_ref[...]).astype(jnp.bfloat16)
    lift = jnp.dot(chosen, lifts_ref[...], preferred_element_type=jnp.float32)
    out_ref[...] = (base_ref[...] + adapter_scale * lift).astype(out_ref.dtype)


def on_device(
    tokens,
    base_projection_weight,
    adapter_down_panels,
    adapter_up_panels,
    request_adapter_ids,
    request_token_lengths,
    adapter_store_slot,
):
    groups = lax.axis_size("grp")
    tp = lax.axis_size("tp")
    width, rank = adapter_down_panels.shape[1:]
    columns = base_projection_weight.shape[1]
    tok_all = tokens.shape[1] * tp
    longest = tok_all // 8
    here = groups * longest
    in_vmem = pl.BlockSpec(memory_space=pltpu.VMEM)
    in_smem = pl.BlockSpec(memory_space=pltpu.SMEM)
    small = pltpu.CompilerParams(vmem_limit_bytes=16 * 2**20)

    arrays = (tokens[0], adapter_down_panels[0].T, adapter_up_panels[0])
    pieces = ring_gather(arrays[0])
    others = [swapped(x, "grp")[1:] for x in arrays[1:]]
    row, column, own, down, up = pl.pallas_call(
        functools.partial(prepare_kernel, groups, tp),
        out_shape=[
            jax.ShapeDtypeStruct((1, tok_all), jnp.int32),
            jax.ShapeDtypeStruct((tok_all, 1), jnp.int32),
        ]
        + [jax.ShapeDtypeStruct(x.shape, x.dtype) for x in arrays],
        in_specs=[in_smem] * 3 + [in_vmem] * 3,
        out_specs=[in_vmem] * 5,
        compiler_params=small,
        name="prepare",
    )(request_adapter_ids, request_token_lengths, adapter_store_slot, *arrays)
    panels = [down, *others[0], up, *others[1]]
    pieces[0] = own

    gathered, lifts = pl.pallas_call(
        functools.partial(lift_kernel, groups, tp),
        out_shape=[
            jax.ShapeDtypeStruct((tok_all, width), jnp.bfloat16),
            jax.ShapeDtypeStruct((tp, here, columns), jnp.bfloat16),
        ],
        in_specs=[in_vmem] * (1 + len(panels) + len(pieces)),
        out_specs=[in_vmem] * 2,
        scratch_shapes=[pltpu.VMEM((groups * rank, tp * columns), jnp.bfloat16)],
        compiler_params=pltpu.CompilerParams(vmem_limit_bytes=24 * 2**20),
        cost_estimate=pl.CostEstimate(
            flops=2 * groups * rank * (tok_all * width + here * tp * columns),
            bytes_accessed=2 * groups * rank * (width + tp * columns),
            transcendentals=0,
        ),
        name="lift",
    )(row, *panels, *pieces)
    lifts = lax.all_to_all(lifts, "tp", split_axis=0, concat_axis=0, tiled=True)

    base = jnp.dot(gathered, base_projection_weight, preferred_element_type=jnp.float32)
    out = pl.pallas_call(
        add_kernel,
        out_shape=jax.ShapeDtypeStruct((tok_all, columns), jnp.bfloat16),
        in_specs=[in_vmem] * 3,
        out_specs=in_vmem,
        compiler_params=small,
        name="add",
    )(column, base, lifts.reshape(tp * here, columns))
    return out[None]


def solution(mesh):
    return jax.shard_map(
        on_device,
        mesh=mesh,
        in_specs=(
            P(("rep", "grp"), "tp", None),
            P(None, "tp"),
            P(("grp", "tp"), None, None),
            P(("grp", "tp"), None, None),
            P("rep", None),
            P(("rep", "grp"), None),
            P(),
        ),
        out_specs=P(("rep", "grp"), None, "tp"),
        check_vma=False,
    )
```

```python
import functools

import jax
import jax.numpy as jnp
from jax import lax
from jax.experimental import pallas as pl
from jax.experimental.pallas import tpu as pltpu
from jax.sharding import PartitionSpec as P

adapter_scale = 1.0


def ring_of(n):
    return list(range(0, n, 2)) + list(range(1, n, 2))[::-1]


def handed(x):
    return lax.ppermute(x, "grp", [(0, 1), (1, 0)])


def ring_gather(block):
    n = lax.axis_size("tp")
    ring = ring_of(n)
    onward = []
    for i in range(n):
        onward.append((ring[i], ring[(i + 1) % n]))
        onward.append((n + ring[(i + 1) % n], n + ring[i]))

    def sent(x):
        return lax.ppermute(x, ("grp", "tp"), onward)

    mine, other = block, handed(block)
    pieces = [handed(other)]
    for step in range(1, n // 2):
        mine, other = sent(mine), sent(other)
        pieces += [mine, handed(other)]
    return pieces + [sent(mine)]


def ring_sources(n):
    me = lax.axis_index("tp")
    way = 1 - 2 * lax.axis_index("grp")
    place = jnp.where(lax.rem(me, 2) == 0, me // 2, n - 1 - me // 2)
    distances = [0] + [d for i in range(1, n // 2) for d in (way * i, -way * i)] + [n // 2]
    sources = []
    for distance in distances:
        at = lax.rem(place - distance + 2 * n, n)
        sources.append(jnp.where(at < n // 2, 2 * at, 2 * (n - 1 - at) + 1))
    return sources


def prepare_kernel(groups, tp, ids_ref, lengths_ref, slots_ref, row_ref, column_ref):
    group = lax.axis_index("grp")
    tok_all = row_ref.shape[1]
    longest = tok_all // 8
    along = lax.broadcasted_iota(jnp.int32, row_ref.shape, 1)
    down = lax.broadcasted_iota(jnp.int32, column_ref.shape, 0)

    def add(request, carry):
        start, row, column = carry
        slot = slots_ref[ids_ref[group, request]]
        end = start + lengths_ref[0, request]
        panel = lax.rem(slot // tp - group + groups, groups)
        first = (lax.rem(slot, tp) * groups + panel) * longest - start
        row = jnp.where((along >= start) & (along < end), first + along, row)
        column = jnp.where((down >= start) & (down < end), first + down, column)
        return end, row, column

    carry = (jnp.int32(0), jnp.zeros_like(along), jnp.zeros_like(down))
    _, row_ref[...], column_ref[...] = lax.fori_loop(0, ids_ref.shape[1], add, carry)


def lift_kernel(groups, tp, order, place_ref, *refs):
    downs, ups, refs = refs[:groups], refs[groups : 2 * groups], refs[2 * groups :]
    pieces, tokens_ref, outs, up_ref = refs[:tp], refs[tp], refs[tp + 1 : -1], refs[-1]
    rank = ups[0].shape[0]
    rows = pieces[0].shape[0]
    tok_all = tokens_ref.shape[0]
    slots, columns = outs[0].shape[-2:]
    for piece, source in zip(pieces, ring_sources(tp)):
        tokens_ref[pl.ds(pl.multiple_of(source * rows, rows), rows), :] = piece[...]
    for s, up in enumerate(ups):
        up_ref[s * rank : (s + 1) * rank, :] = up[...]
    down = jnp.concatenate([down[...] for down in downs], axis=0).T
    low = jnp.dot(tokens_ref[...], down, preferred_element_type=jnp.float32)
    me = lax.axis_index("tp")
    here = lax.broadcasted_iota(jnp.int32, (slots, tok_all), 0) + me * slots
    chosen = (here == place_ref[...]).astype(jnp.bfloat16)
    picked = jnp.dot(chosen, low.astype(jnp.bfloat16), preferred_element_type=jnp.float32)
    row_panel = lax.broadcasted_iota(jnp.int32, picked.shape, 0) // (slots // groups)
    rank_panel = lax.broadcasted_iota(jnp.int32, picked.shape, 1) // rank
    picked = jnp.where(row_panel == rank_panel, picked, 0.0).astype(jnp.bfloat16)

    def lifts(panel):
        return jnp.dot(picked, panel, preferred_element_type=jnp.float32).astype(jnp.bfloat16)

    if order is None:
        for part in range(tp):
            outs[0][part] = lifts(up_ref[:, part * columns : (part + 1) * columns])
    else:
        for out_ref, k in zip(outs, order):
            start = pl.multiple_of(jnp.bitwise_xor(me, k) * columns, columns)
            out_ref[...] = lifts(up_ref[:, pl.ds(start, columns)])


def add_kernel(order, place_ref, base_ref, *refs):
    parts, out_ref, lifts_ref = refs[:-2], refs[-2], refs[-1]
    slots = parts[0].shape[0]
    shape = (base_ref.shape[0], lifts_ref.shape[0])
    place = lax.broadcasted_iota(jnp.int32, shape, 1)
    if order is not None:
        chip = jnp.zeros(shape, jnp.int32)
        for i, k in enumerate(order):
            from_chip = jnp.bitwise_xor(lax.axis_index("tp"), k)
            chip = jnp.where(place // slots == i, from_chip, chip)
        place = chip * slots + lax.rem(place, slots)
    for i, part in enumerate(parts):
        lifts_ref[i * slots : (i + 1) * slots, :] = part[...]
    chosen = (place == place_ref[...]).astype(jnp.bfloat16)
    lift = jnp.dot(chosen, lifts_ref[...], preferred_element_type=jnp.float32)
    out_ref[...] = (base_ref[...] + adapter_scale * lift).astype(out_ref.dtype)


def on_device(
    tokens,
    base_projection_weight,
    adapter_down_panels,
    adapter_up_panels,
    request_adapter_ids,
    request_token_lengths,
    adapter_store_slot,
):
    groups = lax.axis_size("grp")
    tp = lax.axis_size("tp")
    width, rank = adapter_down_panels.shape[1:]
    columns = base_projection_weight.shape[1]
    tok_all = tokens.shape[1] * tp
    longest = tok_all // 8
    here = groups * longest
    in_vmem = pl.BlockSpec(memory_space=pltpu.VMEM)
    in_smem = pl.BlockSpec(memory_space=pltpu.SMEM)
    small = pltpu.CompilerParams(vmem_limit_bytes=16 * 2**20)

    pieces = ring_gather(tokens[0])
    panels = []
    for panel in (adapter_down_panels[0].T, adapter_up_panels[0]):
        other = handed(panel)
        panels += [handed(other), other]
    row, column = pl.pallas_call(
        functools.partial(prepare_kernel, groups, tp),
        out_shape=[
            jax.ShapeDtypeStruct((1, tok_all), jnp.int32),
            jax.ShapeDtypeStruct((tok_all, 1), jnp.int32),
        ],
        in_specs=[in_smem] * 3,
        out_specs=[in_vmem] * 2,
        compiler_params=small,
        name="prepare",
    )(request_adapter_ids, request_token_lengths, adapter_store_slot)

    pairwise = columns % 128 == 0 and tp & (tp - 1) == 0
    order = list(range(tp))[::-1] if pairwise else None
    part = jax.ShapeDtypeStruct((here, columns), jnp.bfloat16)
    gathered, *lifts = pl.pallas_call(
        functools.partial(lift_kernel, groups, tp, order),
        out_shape=[jax.ShapeDtypeStruct((tok_all, width), jnp.bfloat16)]
        + ([part] * tp if pairwise else [jax.ShapeDtypeStruct((tp, *part.shape), part.dtype)]),
        in_specs=[in_vmem] * (1 + len(panels) + len(pieces)),
        out_specs=[in_vmem] * (1 + (tp if pairwise else 1)),
        scratch_shapes=[pltpu.VMEM((groups * rank, tp * columns), jnp.bfloat16)],
        compiler_params=pltpu.CompilerParams(vmem_limit_bytes=24 * 2**20),
        cost_estimate=pl.CostEstimate(
            flops=2 * groups * rank * (tok_all * width + here * tp * columns),
            bytes_accessed=2 * groups * rank * (width + tp * columns),
            transcendentals=0,
        ),
        name="lift",
    )(row, *panels, *pieces)
    if pairwise:
        lifts = [
            lax.ppermute(x, "tp", [(i, i ^ k) for i in range(tp)]) if k else x
            for x, k in zip(lifts, order)
        ]
    else:
        lifts = lax.all_to_all(lifts[0], "tp", split_axis=0, concat_axis=0, tiled=True)
        lifts = [lifts.reshape(tp * here, columns)]

    base = jnp.dot(gathered, base_projection_weight, preferred_element_type=jnp.float32)
    out = pl.pallas_call(
        functools.partial(add_kernel, order),
        out_shape=jax.ShapeDtypeStruct((tok_all, columns), jnp.bfloat16),
        in_specs=[in_vmem] * (2 + len(lifts)),
        out_specs=in_vmem,
        scratch_shapes=[pltpu.VMEM((tp * here, columns), jnp.bfloat16)],
        compiler_params=small,
        name="add",
    )(column, base, *lifts)
    return out[None]


def solution(mesh):
    return jax.shard_map(
        on_device,
        mesh=mesh,
        in_specs=(
            P(("rep", "grp"), "tp", None),
            P(None, "tp"),
            P(("grp", "tp"), None, None),
            P(("grp", "tp"), None, None),
            P("rep", None),
            P(("rep", "grp"), None),
            P(),
        ),
        out_specs=P(("rep", "grp"), None, "tp"),
        check_vma=False,
    )
```

```python
import functools

import jax
import jax.numpy as jnp
from jax import lax
from jax.experimental import pallas as pl
from jax.experimental.pallas import tpu as pltpu
from jax.sharding import PartitionSpec as P

adapter_scale = 1.0


def ring_of(n):
    return list(range(0, n, 2)) + list(range(1, n, 2))[::-1]


def handed(x):
    return lax.ppermute(x, "grp", [(0, 1), (1, 0)])


def ring_gather(block, copied):
    n = lax.axis_size("tp")
    ring = ring_of(n)
    onward = []
    for i in range(n):
        onward.append((ring[i], ring[(i + 1) % n]))
        onward.append((n + ring[(i + 1) % n], n + ring[i]))

    def sent(x):
        return lax.ppermute(x, ("grp", "tp"), onward)

    mine, other = sent(block), handed(copied)
    pieces = [copied, mine]
    for step in range(2, n // 2 + 1):
        mine, other = sent(mine), sent(other)
        pieces += [handed(other), mine]
    return pieces


def ring_sources(n):
    me = lax.axis_index("tp")
    way = 1 - 2 * lax.axis_index("grp")
    place = jnp.where(lax.rem(me, 2) == 0, me // 2, n - 1 - me // 2)
    distances = [0, way]
    for i in range(2, n // 2 + 1):
        distances += [-way * (i - 1), way * i]
    sources = []
    for distance in distances:
        at = lax.rem(place - distance + 2 * n, n)
        sources.append(jnp.where(at < n // 2, 2 * at, 2 * (n - 1 - at) + 1))
    return sources


def prepare_kernel(groups, tp, ids_ref, lengths_ref, slots_ref, *refs):
    n = (len(refs) - 2) // 2
    row_ref, column_ref = refs[n : n + 2]
    for source, target in zip(refs[:n], refs[n + 2 :]):
        target[...] = source[...]
    group = lax.axis_index("grp")
    tok_all = row_ref.shape[1]
    longest = tok_all // 8
    along = lax.broadcasted_iota(jnp.int32, row_ref.shape, 1)
    down = lax.broadcasted_iota(jnp.int32, column_ref.shape, 0)

    def add(request, carry):
        start, row, column = carry
        slot = slots_ref[ids_ref[group, request]]
        end = start + lengths_ref[0, request]
        panel = lax.rem(slot // tp - group + groups, groups)
        first = (lax.rem(slot, tp) * groups + panel) * longest - start
        row = jnp.where((along >= start) & (along < end), first + along, row)
        column = jnp.where((down >= start) & (down < end), first + down, column)
        return end, row, column

    carry = (jnp.int32(0), jnp.zeros_like(along), jnp.zeros_like(down))
    _, row_ref[...], column_ref[...] = lax.fori_loop(0, ids_ref.shape[1], add, carry)


def lift_kernel(groups, tp, order, place_ref, *refs):
    downs, ups, refs = refs[:groups], refs[groups : 2 * groups], refs[2 * groups :]
    pieces, tokens_ref, outs, up_ref = refs[:tp], refs[tp], refs[tp + 1 : -1], refs[-1]
    rank = ups[0].shape[0]
    rows = pieces[0].shape[0]
    tok_all = tokens_ref.shape[0]
    slots, columns = outs[0].shape[-2:]
    for piece, source in zip(pieces, ring_sources(tp)):
        tokens_ref[pl.ds(pl.multiple_of(source * rows, rows), rows), :] = piece[...]
    for s, up in enumerate(ups):
        up_ref[s * rank : (s + 1) * rank, :] = up[...]
    down = jnp.concatenate([down[...] for down in downs], axis=0).T
    low = jnp.dot(tokens_ref[...], down, preferred_element_type=jnp.float32)
    me = lax.axis_index("tp")
    here = lax.broadcasted_iota(jnp.int32, (slots, tok_all), 0) + me * slots
    chosen = (here == place_ref[...]).astype(jnp.bfloat16)
    picked = jnp.dot(chosen, low.astype(jnp.bfloat16), preferred_element_type=jnp.float32)
    row_panel = lax.broadcasted_iota(jnp.int32, picked.shape, 0) // (slots // groups)
    rank_panel = lax.broadcasted_iota(jnp.int32, picked.shape, 1) // rank
    picked = jnp.where(row_panel == rank_panel, picked, 0.0).astype(jnp.bfloat16)

    def lifts(panel):
        return jnp.dot(picked, panel, preferred_element_type=jnp.float32).astype(jnp.bfloat16)

    if order is None:
        for part in range(tp):
            outs[0][part] = lifts(up_ref[:, part * columns : (part + 1) * columns])
    else:
        for out_ref, k in zip(outs, order):
            start = pl.multiple_of(jnp.bitwise_xor(me, k) * columns, columns)
            out_ref[...] = lifts(up_ref[:, pl.ds(start, columns)])


def pass_kernel(after_ref, *refs):
    n = len(refs) // 2
    for source, target in zip(refs[:n], refs[n:]):
        target[...] = source[...]


def add_kernel(order, place_ref, base_ref, *refs):
    parts, out_ref, lifts_ref = refs[:-2], refs[-2], refs[-1]
    slots = parts[0].shape[0]
    shape = (base_ref.shape[0], lifts_ref.shape[0])
    place = lax.broadcasted_iota(jnp.int32, shape, 1)
    if order is not None:
        chip = jnp.zeros(shape, jnp.int32)
        for i, k in enumerate(order):
            from_chip = jnp.bitwise_xor(lax.axis_index("tp"), k)
            chip = jnp.where(place // slots == i, from_chip, chip)
        place = chip * slots + lax.rem(place, slots)
    for i, part in enumerate(parts):
        lifts_ref[i * slots : (i + 1) * slots, :] = part[...]
    chosen = (place == place_ref[...]).astype(jnp.bfloat16)
    lift = jnp.dot(chosen, lifts_ref[...], preferred_element_type=jnp.float32)
    out_ref[...] = (base_ref[...] + adapter_scale * lift).astype(out_ref.dtype)


def on_device(
    tokens,
    base_projection_weight,
    adapter_down_panels,
    adapter_up_panels,
    request_adapter_ids,
    request_token_lengths,
    adapter_store_slot,
):
    groups = lax.axis_size("grp")
    tp = lax.axis_size("tp")
    width, rank = adapter_down_panels.shape[1:]
    columns = base_projection_weight.shape[1]
    tok_all = tokens.shape[1] * tp
    longest = tok_all // 8
    here = groups * longest
    in_vmem = pl.BlockSpec(memory_space=pltpu.VMEM)
    in_smem = pl.BlockSpec(memory_space=pltpu.SMEM)
    small = pltpu.CompilerParams(vmem_limit_bytes=16 * 2**20)

    arrays = (tokens[0], adapter_down_panels[0].T, adapter_up_panels[0])
    row, column, copied, down, up = pl.pallas_call(
        functools.partial(prepare_kernel, groups, tp),
        out_shape=[
            jax.ShapeDtypeStruct((1, tok_all), jnp.int32),
            jax.ShapeDtypeStruct((tok_all, 1), jnp.int32),
        ]
        + [jax.ShapeDtypeStruct(x.shape, x.dtype) for x in arrays],
        in_specs=[in_smem] * 3 + [in_vmem] * 3,
        out_specs=[in_vmem] * 5,
        compiler_params=small,
        name="prepare",
    )(request_adapter_ids, request_token_lengths, adapter_store_slot, *arrays)
    pieces = ring_gather(arrays[0], copied)
    panels = [down, handed(down), up, handed(up)]

    pairwise = columns % 128 == 0 and tp & (tp - 1) == 0
    order = list(range(tp))[::-1] if pairwise else None
    part = jax.ShapeDtypeStruct((here, columns), jnp.bfloat16)
    gathered, *lifts = pl.pallas_call(
        functools.partial(lift_kernel, groups, tp, order),
        out_shape=[jax.ShapeDtypeStruct((tok_all, width), jnp.bfloat16)]
        + ([part] * tp if pairwise else [jax.ShapeDtypeStruct((tp, *part.shape), part.dtype)]),
        in_specs=[in_vmem] * (1 + len(panels) + len(pieces)),
        out_specs=[in_vmem] * (1 + (tp if pairwise else 1)),
        scratch_shapes=[pltpu.VMEM((groups * rank, tp * columns), jnp.bfloat16)],
        compiler_params=pltpu.CompilerParams(vmem_limit_bytes=24 * 2**20),
        cost_estimate=pl.CostEstimate(
            flops=2 * groups * rank * (tok_all * width + here * tp * columns),
            bytes_accessed=2 * groups * rank * (width + tp * columns),
            transcendentals=0,
        ),
        name="lift",
    )(row, *panels, *pieces)
    base = jnp.dot(gathered, base_projection_weight, preferred_element_type=jnp.float32)
    if pairwise:
        far = tp // 2
        near = pl.pallas_call(
            pass_kernel,
            out_shape=[part] * (tp - far - 1),
            in_specs=[pl.BlockSpec(memory_space=pl.ANY)] + [in_vmem] * (tp - far - 1),
            out_specs=[in_vmem] * (tp - far - 1),
            compiler_params=small,
            name="near",
        )(base, *lifts[far:-1])
        lifts = [
            lax.ppermute(x, "tp", [(i, i ^ k) for i in range(tp)]) if k else x
            for x, k in zip([*lifts[:far], *near, lifts[-1]], order)
        ]
    else:
        lifts = lax.all_to_all(lifts[0], "tp", split_axis=0, concat_axis=0, tiled=True)
        lifts = [lifts.reshape(tp * here, columns)]

    out = pl.pallas_call(
        functools.partial(add_kernel, order),
        out_shape=jax.ShapeDtypeStruct((tok_all, columns), jnp.bfloat16),
        in_specs=[in_vmem] * (2 + len(lifts)),
        out_specs=in_vmem,
        scratch_shapes=[pltpu.VMEM((tp * here, columns), jnp.bfloat16)],
        compiler_params=small,
        name="add",
    )(column, base, *lifts)
    return out[None]


def solution(mesh):
    return jax.shard_map(
        on_device,
        mesh=mesh,
        in_specs=(
            P(("rep", "grp"), "tp", None),
            P(None, "tp"),
            P(("grp", "tp"), None, None),
            P(("grp", "tp"), None, None),
            P("rep", None),
            P(("rep", "grp"), None),
            P(),
        ),
        out_specs=P(("rep", "grp"), None, "tp"),
        check_vma=False,
    )
```

```python
import functools

import jax
import jax.numpy as jnp
from jax import lax
from jax.experimental import pallas as pl
from jax.experimental.pallas import tpu as pltpu
from jax.sharding import PartitionSpec as P

adapter_scale = 1.0


def fetched(x, axis="grp", shift=0):
    n = lax.axis_size(axis)
    return lax.ppermute(x, axis, [((i + shift) % n, i) for i in range(n)])


def ring_of(n):
    return list(range(0, n, 2)) + list(range(1, n, 2))[::-1]


class Ring:
    def __init__(self, block, axis, last_from_behind):
        n = lax.axis_size(axis)
        ring = ring_of(n)
        self.n, self.axis, self.last_from_behind = n, axis, last_from_behind
        self.up = [(ring[i], ring[(i + 1) % n]) for i in range(n)]
        self.down = [(ring[(i + 1) % n], ring[i]) for i in range(n)]
        self.ahead = self.behind = block
        self.pieces = [block]

    def step(self, i):
        last = i == self.n // 2
        if not last or self.last_from_behind:
            self.ahead = lax.ppermute(self.ahead, self.axis, self.up)
            self.pieces.append(self.ahead)
        if not last or not self.last_from_behind:
            self.behind = lax.ppermute(self.behind, self.axis, self.down)
            self.pieces.append(self.behind)


def ring_sources(axis):
    n = lax.axis_size(axis)
    me = lax.axis_index(axis)
    place = jnp.where(lax.rem(me, 2) == 0, me // 2, n - 1 - me // 2)
    distances = [0] + [d for i in range(1, n // 2) for d in (i, -i)] + [n // 2]
    sources = []
    for distance in distances:
        at = lax.rem(place - distance + n, n)
        sources.append(jnp.where(at < n // 2, 2 * at, 2 * (n - 1 - at) + 1))
    return sources


def halve_kernel(block_ref, *out_refs):
    width = out_refs[0].shape[1]
    for i, out_ref in enumerate(out_refs):
        out_ref[...] = block_ref[:, i * width : (i + 1) * width]


def place_kernel(groups, tp, ids_ref, lengths_ref, slots_ref, row_ref, column_ref):
    group = lax.axis_index("grp")
    longest = row_ref.shape[1] // 8
    along = lax.broadcasted_iota(jnp.int32, row_ref.shape, 1)
    down = lax.broadcasted_iota(jnp.int32, column_ref.shape, 0)

    def add(request, carry):
        start, row, column = carry
        slot = slots_ref[ids_ref[group, request]]
        end = start + lengths_ref[0, request]
        panel = lax.rem(slot // tp - group + groups, groups)
        first = (lax.rem(slot, tp) * groups + panel) * longest - start
        row = jnp.where((along >= start) & (along < end), first + along, row)
        column = jnp.where((down >= start) & (down < end), first + down, column)
        return end, row, column

    carry = (jnp.int32(0), jnp.zeros_like(along), jnp.zeros_like(down))
    _, row_ref[...], column_ref[...] = lax.fori_loop(0, ids_ref.shape[1], add, carry)


def lift_kernel(groups, place_ref, *refs):
    downs, ups, pieces = refs[:groups], refs[groups : 2 * groups], refs[2 * groups : -3]
    tokens_ref, out_ref, up_ref = refs[-3:]
    rank = ups[0].shape[0]
    rows, width = pieces[0].shape
    tok_all = tokens_ref.shape[0]
    parts, slots, columns = out_ref.shape
    sources = ring_sources("tp")
    for i, piece in enumerate(pieces):
        start = pl.multiple_of(sources[i % len(sources)] * rows, rows)
        column = i // len(sources) * width
        tokens_ref[pl.ds(start, rows), column : column + width] = piece[...]
    for s, up in enumerate(ups):
        up_ref[s * rank : (s + 1) * rank, :] = up[...]
    down = jnp.concatenate([down[...] for down in downs], axis=0).T
    low = jnp.dot(tokens_ref[...], down, preferred_element_type=jnp.float32)
    here = lax.broadcasted_iota(jnp.int32, (slots, tok_all), 0) + lax.axis_index("tp") * slots
    chosen = (here == place_ref[...]).astype(jnp.bfloat16)
    picked = jnp.dot(chosen, low.astype(jnp.bfloat16), preferred_element_type=jnp.float32)
    row_panel = lax.broadcasted_iota(jnp.int32, picked.shape, 0) // (slots // groups)
    rank_panel = lax.broadcasted_iota(jnp.int32, picked.shape, 1) // rank
    picked = jnp.where(row_panel == rank_panel, picked, 0.0).astype(jnp.bfloat16)
    for part in range(parts):
        out_ref[part] = jnp.dot(
            picked,
            up_ref[:, part * columns : (part + 1) * columns],
            preferred_element_type=jnp.float32,
        ).astype(out_ref.dtype)


def add_kernel(place_ref, base_ref, lifts_ref, out_ref):
    place = lax.broadcasted_iota(jnp.int32, (base_ref.shape[0], lifts_ref.shape[0]), 1)
    chosen = (place == place_ref[...]).astype(jnp.bfloat16)
    lift = jnp.dot(chosen, lifts_ref[...], preferred_element_type=jnp.float32)
    out_ref[...] = (base_ref[...] + adapter_scale * lift).astype(out_ref.dtype)


def on_device(
    tokens,
    base_projection_weight,
    adapter_down_panels,
    adapter_up_panels,
    request_adapter_ids,
    request_token_lengths,
    adapter_store_slot,
):
    groups = lax.axis_size("grp")
    tp = lax.axis_size("tp")
    width, rank = adapter_down_panels.shape[1:]
    columns = base_projection_weight.shape[1]
    tok_all = tokens.shape[1] * tp
    longest = tok_all // 8
    here = groups * longest
    half = width // 2
    in_vmem = pl.BlockSpec(memory_space=pltpu.VMEM)
    in_smem = pl.BlockSpec(memory_space=pltpu.SMEM)
    small = pltpu.CompilerParams(vmem_limit_bytes=16 * 2**20)

    halves = pl.pallas_call(
        halve_kernel,
        out_shape=[jax.ShapeDtypeStruct((tokens.shape[1], half), jnp.bfloat16)] * 2,
        in_specs=[in_vmem],
        out_specs=[in_vmem] * 2,
        compiler_params=small,
        name="halve",
    )(tokens[0])
    rings = [Ring(part, "tp", k == 0) for k, part in enumerate(halves)]
    for i in range(1, tp // 2 + 1):
        for ring in rings:
            ring.step(i)

    pieces = rings[0].pieces + rings[1].pieces

    panels = [
        fetched(panel, shift=s)
        for panel in (adapter_down_panels[0].T, adapter_up_panels[0])
        for s in range(groups)
    ]
    requests = [
        fetched(x) for x in (request_adapter_ids, request_token_lengths, adapter_store_slot)
    ]
    row, column = pl.pallas_call(
        functools.partial(place_kernel, groups, tp),
        out_shape=[
            jax.ShapeDtypeStruct((1, tok_all), jnp.int32),
            jax.ShapeDtypeStruct((tok_all, 1), jnp.int32),
        ],
        in_specs=[in_smem] * 3,
        out_specs=[in_vmem] * 2,
        compiler_params=small,
        name="place",
    )(*requests)

    gathered, lifts = pl.pallas_call(
        functools.partial(lift_kernel, groups),
        out_shape=[
            jax.ShapeDtypeStruct((tok_all, width), jnp.bfloat16),
            jax.ShapeDtypeStruct((tp, here, columns), jnp.bfloat16),
        ],
        in_specs=[in_vmem] * (1 + len(panels) + len(pieces)),
        out_specs=[in_vmem] * 2,
        scratch_shapes=[pltpu.VMEM((groups * rank, tp * columns), jnp.bfloat16)],
        compiler_params=pltpu.CompilerParams(vmem_limit_bytes=24 * 2**20),
        cost_estimate=pl.CostEstimate(
            flops=2 * groups * rank * (tok_all * width + here * tp * columns),
            bytes_accessed=2 * groups * rank * (width + tp * columns),
            transcendentals=0,
        ),
        name="lift",
    )(row, *panels, *pieces)
    lifts = lax.all_to_all(lifts, "tp", split_axis=0, concat_axis=0, tiled=True)

    base = jnp.dot(gathered, base_projection_weight, preferred_element_type=jnp.float32)
    out = pl.pallas_call(
        add_kernel,
        out_shape=jax.ShapeDtypeStruct((tok_all, columns), jnp.bfloat16),
        in_specs=[in_vmem] * 3,
        out_specs=in_vmem,
        compiler_params=small,
        name="add",
    )(column, base, lifts.reshape(tp * here, columns))
    return out[None]


def solution(mesh):
    return jax.shard_map(
        on_device,
        mesh=mesh,
        in_specs=(
            P(("rep", "grp"), "tp", None),
            P(None, "tp"),
            P(("grp", "tp"), None, None),
            P(("grp", "tp"), None, None),
            P("rep", None),
            P(("rep", "grp"), None),
            P(),
        ),
        out_specs=P(("rep", "grp"), None, "tp"),
        check_vma=False,
    )
```

```python
import functools

import jax
import jax.numpy as jnp
from jax import lax
from jax.experimental import pallas as pl
from jax.experimental.pallas import tpu as pltpu
from jax.sharding import PartitionSpec as P

adapter_scale = 1.0


def swapped(x, axis):
    n = lax.axis_size(axis)
    return [x] + [
        lax.ppermute(x, axis, [((i + s) % n, i) for i in range(n)]) for s in range(1, n)
    ]


def ring_of(n):
    return list(range(0, n, 2)) + list(range(1, n, 2))[::-1]


class Ring:
    def __init__(self, block, axis, last_from_behind):
        n = lax.axis_size(axis)
        ring = ring_of(n)
        self.n, self.axis, self.last_from_behind = n, axis, last_from_behind
        self.up = [(ring[i], ring[(i + 1) % n]) for i in range(n)]
        self.down = [(ring[(i + 1) % n], ring[i]) for i in range(n)]
        self.ahead = self.behind = block
        self.pieces = [block]

    def step(self, i):
        last = i == self.n // 2
        if not last or self.last_from_behind:
            self.ahead = lax.ppermute(self.ahead, self.axis, self.up)
            self.pieces.append(self.ahead)
        if not last or not self.last_from_behind:
            self.behind = lax.ppermute(self.behind, self.axis, self.down)
            self.pieces.append(self.behind)


def ring_sources(axis):
    n = lax.axis_size(axis)
    me = lax.axis_index(axis)
    place = jnp.where(lax.rem(me, 2) == 0, me // 2, n - 1 - me // 2)
    distances = [0] + [d for i in range(1, n // 2) for d in (i, -i)] + [n // 2]
    sources = []
    for distance in distances:
        at = lax.rem(place - distance + n, n)
        sources.append(jnp.where(at < n // 2, 2 * at, 2 * (n - 1 - at) + 1))
    return sources


def halve_kernel(block_ref, *out_refs):
    width = out_refs[0].shape[1]
    for i, out_ref in enumerate(out_refs):
        out_ref[...] = block_ref[:, i * width : (i + 1) * width]


def stack_kernel(groups, passed_ref, *refs):
    downs, ups, (pass_ref, down_ref, up_ref) = refs[:groups], refs[groups:-3], refs[-3:]
    pass_ref[...] = passed_ref[...]
    rank = ups[0].shape[0]
    down_ref[...] = jnp.concatenate([down[...] for down in downs], axis=0).T
    for s, up in enumerate(ups):
        up_ref[s * rank : (s + 1) * rank, :] = up[...]


def place_kernel(groups, tp, ids_ref, lengths_ref, slots_ref, passed_ref, pass_ref, row_ref, column_ref):
    pass_ref[...] = passed_ref[...]
    group = lax.axis_index("grp")
    longest = row_ref.shape[1] // 8
    along = lax.broadcasted_iota(jnp.int32, row_ref.shape, 1)
    down = lax.broadcasted_iota(jnp.int32, column_ref.shape, 0)

    def add(request, carry):
        start, row, column = carry
        slot = slots_ref[ids_ref[group, request]]
        end = start + lengths_ref[0, request]
        panel = lax.rem(slot // tp - group + groups, groups)
        first = (lax.rem(slot, tp) * groups + panel) * longest - start
        row = jnp.where((along >= start) & (along < end), first + along, row)
        column = jnp.where((down >= start) & (down < end), first + down, column)
        return end, row, column

    carry = (jnp.int32(0), jnp.zeros_like(along), jnp.zeros_like(down))
    _, row_ref[...], column_ref[...] = lax.fori_loop(0, ids_ref.shape[1], add, carry)


def lift_kernel(groups, place_ref, down_ref, up_ref, *refs):
    pieces, (tokens_ref, out_ref) = refs[:-2], refs[-2:]
    rank = up_ref.shape[0] // groups
    rows, width = pieces[0].shape
    tok_all = tokens_ref.shape[0]
    parts, slots, columns = out_ref.shape
    sources = ring_sources("tp")
    for i, piece in enumerate(pieces):
        start = pl.multiple_of(sources[i % len(sources)] * rows, rows)
        column = i // len(sources) * width
        tokens_ref[pl.ds(start, rows), column : column + width] = piece[...]
    low = jnp.dot(tokens_ref[...], down_ref[...], preferred_element_type=jnp.float32)
    here = lax.broadcasted_iota(jnp.int32, (slots, tok_all), 0) + lax.axis_index("tp") * slots
    chosen = (here == place_ref[...]).astype(jnp.bfloat16)
    picked = jnp.dot(chosen, low.astype(jnp.bfloat16), preferred_element_type=jnp.float32)
    row_panel = lax.broadcasted_iota(jnp.int32, picked.shape, 0) // (slots // groups)
    rank_panel = lax.broadcasted_iota(jnp.int32, picked.shape, 1) // rank
    picked = jnp.where(row_panel == rank_panel, picked, 0.0).astype(jnp.bfloat16)
    for part in range(parts):
        out_ref[part] = jnp.dot(
            picked,
            up_ref[:, part * columns : (part + 1) * columns],
            preferred_element_type=jnp.float32,
        ).astype(out_ref.dtype)


def add_kernel(place_ref, base_ref, lifts_ref, out_ref):
    place = lax.broadcasted_iota(jnp.int32, (base_ref.shape[0], lifts_ref.shape[0]), 1)
    chosen = (place == place_ref[...]).astype(jnp.bfloat16)
    lift = jnp.dot(chosen, lifts_ref[...], preferred_element_type=jnp.float32)
    out_ref[...] = (base_ref[...] + adapter_scale * lift).astype(out_ref.dtype)


def on_device(
    tokens,
    base_projection_weight,
    adapter_down_panels,
    adapter_up_panels,
    request_adapter_ids,
    request_token_lengths,
    adapter_store_slot,
):
    groups = lax.axis_size("grp")
    tp = lax.axis_size("tp")
    width, rank = adapter_down_panels.shape[1:]
    columns = base_projection_weight.shape[1]
    tok_all = tokens.shape[1] * tp
    longest = tok_all // 8
    here = groups * longest
    half = width // 2
    in_vmem = pl.BlockSpec(memory_space=pltpu.VMEM)
    in_smem = pl.BlockSpec(memory_space=pltpu.SMEM)
    small = pltpu.CompilerParams(vmem_limit_bytes=16 * 2**20)

    halves = pl.pallas_call(
        halve_kernel,
        out_shape=[jax.ShapeDtypeStruct((tokens.shape[1], half), jnp.bfloat16)] * 2,
        in_specs=[in_vmem],
        out_specs=[in_vmem] * 2,
        compiler_params=small,
        name="halve",
    )(tokens[0])
    rings = [Ring(part, "tp", k == 0) for k, part in enumerate(halves)]
    rings[0].step(1)
    rings[1].step(1)
    piece = jax.ShapeDtypeStruct(halves[0].shape, jnp.bfloat16)

    panels = swapped(adapter_down_panels[0].T, "grp") + swapped(adapter_up_panels[0], "grp")
    rings[1].ahead, down, up = pl.pallas_call(
        functools.partial(stack_kernel, groups),
        out_shape=[
            piece,
            jax.ShapeDtypeStruct((width, groups * rank), jnp.bfloat16),
            jax.ShapeDtypeStruct((groups * rank, tp * columns), jnp.bfloat16),
        ],
        in_specs=[in_vmem] * (1 + len(panels)),
        out_specs=[in_vmem] * 3,
        compiler_params=small,
        name="stack",
    )(rings[1].ahead, *panels)
    rings[0].step(2)
    rings[1].step(2)

    rings[0].ahead, row, column = pl.pallas_call(
        functools.partial(place_kernel, groups, tp),
        out_shape=[
            piece,
            jax.ShapeDtypeStruct((1, tok_all), jnp.int32),
            jax.ShapeDtypeStruct((tok_all, 1), jnp.int32),
        ],
        in_specs=[in_smem] * 3 + [in_vmem],
        out_specs=[in_vmem] * 3,
        compiler_params=small,
        name="place",
    )(request_adapter_ids, request_token_lengths, adapter_store_slot, rings[0].ahead)
    for i in range(3, tp // 2 + 1):
        for ring in rings:
            ring.step(i)
    pieces = rings[0].pieces + rings[1].pieces

    gathered, lifts = pl.pallas_call(
        functools.partial(lift_kernel, groups),
        out_shape=[
            jax.ShapeDtypeStruct((tok_all, width), jnp.bfloat16),
            jax.ShapeDtypeStruct((tp, here, columns), jnp.bfloat16),
        ],
        in_specs=[in_vmem] * (3 + len(pieces)),
        out_specs=[in_vmem] * 2,
        compiler_params=pltpu.CompilerParams(vmem_limit_bytes=24 * 2**20),
        cost_estimate=pl.CostEstimate(
            flops=2 * groups * rank * (tok_all * width + here * tp * columns),
            bytes_accessed=2 * groups * rank * (width + tp * columns),
            transcendentals=0,
        ),
        name="lift",
    )(row, down, up, *pieces)
    lifts = lax.all_to_all(lifts, "tp", split_axis=0, concat_axis=0, tiled=True)

    base = jnp.dot(gathered, base_projection_weight, preferred_element_type=jnp.float32)
    out = pl.pallas_call(
        add_kernel,
        out_shape=jax.ShapeDtypeStruct((tok_all, columns), jnp.bfloat16),
        in_specs=[in_vmem] * 3,
        out_specs=in_vmem,
        compiler_params=small,
        name="add",
    )(column, base, lifts.reshape(tp * here, columns))
    return out[None]


def solution(mesh):
    return jax.shard_map(
        on_device,
        mesh=mesh,
        in_specs=(
            P(("rep", "grp"), "tp", None),
            P(None, "tp"),
            P(("grp", "tp"), None, None),
            P(("grp", "tp"), None, None),
            P("rep", None),
            P(("rep", "grp"), None),
            P(),
        ),
        out_specs=P(("rep", "grp"), None, "tp"),
        check_vma=False,
    )
```

```python
import functools

import jax
import jax.numpy as jnp
from jax import lax
from jax.experimental import pallas as pl
from jax.experimental.pallas import tpu as pltpu
from jax.sharding import PartitionSpec as P

adapter_scale = 1.0


def swapped(x, axis):
    n = lax.axis_size(axis)
    return [x] + [
        lax.ppermute(x, axis, [((i + s) % n, i) for i in range(n)]) for s in range(1, n)
    ]


def ring_of(n):
    return list(range(0, n, 2)) + list(range(1, n, 2))[::-1]


def ring_gather(block, axis, ahead_of_third, ahead_of_last):
    n = lax.axis_size(axis)
    ring = ring_of(n)
    up = [(ring[i], ring[(i + 1) % n]) for i in range(n)]
    down = [(ring[(i + 1) % n], ring[i]) for i in range(n)]
    ahead = behind = block
    pieces = [block]
    for step in range(1, n // 2 + 1):
        if step == n // 2:
            ahead, behind = handed_on((ahead, behind), ahead_of_last, block.shape[1] // 2)
        elif step == 3:
            ahead, behind = handed_on((ahead, behind), ahead_of_third, block.shape[1])
        ahead, behind = lax.ppermute(ahead, axis, up), lax.ppermute(behind, axis, down)
        pieces += [ahead, behind]
    return pieces


def pass_kernel(waits, *refs):
    n = (len(refs) - waits) // 2
    for source, target in zip(refs[:n], refs[-n:]):
        width = target.shape[1]
        start = 0 if source is refs[0] else source.shape[1] - width
        target[...] = source[:, start : start + width]


def handed_on(arrays, values, width):
    in_vmem = pl.BlockSpec(memory_space=pltpu.VMEM)
    return pl.pallas_call(
        functools.partial(pass_kernel, len(values)),
        out_shape=[jax.ShapeDtypeStruct((x.shape[0], width), x.dtype) for x in arrays],
        in_specs=[in_vmem] * len(arrays) + [pl.BlockSpec(memory_space=pl.ANY)] * len(values),
        out_specs=[in_vmem] * len(arrays),
        compiler_params=pltpu.CompilerParams(vmem_limit_bytes=16 * 2**20),
        name="pass",
    )(*arrays, *values)


def ring_sources(axis):
    n = lax.axis_size(axis)
    me = lax.axis_index(axis)
    place = jnp.where(lax.rem(me, 2) == 0, me // 2, n - 1 - me // 2)
    distances = [0] + [d for i in range(1, n // 2) for d in (i, -i)] + [n // 2] * 2
    sources = []
    for distance in distances:
        at = lax.rem(place - distance + n, n)
        sources.append(jnp.where(at < n // 2, 2 * at, 2 * (n - 1 - at) + 1))
    return sources


def stack_kernel(groups, *refs):
    downs, ups, (down_ref, up_ref) = refs[:groups], refs[groups:-2], refs[-2:]
    rank = ups[0].shape[0]
    down_ref[...] = jnp.concatenate([down[...] for down in downs], axis=0).T
    for s, up in enumerate(ups):
        up_ref[s * rank : (s + 1) * rank, :] = up[...]


def place_kernel(groups, tp, ids_ref, lengths_ref, slots_ref, row_ref, column_ref):
    group = lax.axis_index("grp")
    longest = row_ref.shape[1] // 8
    along = lax.broadcasted_iota(jnp.int32, row_ref.shape, 1)
    down = lax.broadcasted_iota(jnp.int32, column_ref.shape, 0)

    def add(request, carry):
        start, row, column = carry
        slot = slots_ref[ids_ref[group, request]]
        end = start + lengths_ref[0, request]
        panel = lax.rem(slot // tp - group + groups, groups)
        first = (lax.rem(slot, tp) * groups + panel) * longest - start
        row = jnp.where((along >= start) & (along < end), first + along, row)
        column = jnp.where((down >= start) & (down < end), first + down, column)
        return end, row, column

    carry = (jnp.int32(0), jnp.zeros_like(along), jnp.zeros_like(down))
    _, row_ref[...], column_ref[...] = lax.fori_loop(0, ids_ref.shape[1], add, carry)


def lift_kernel(groups, place_ref, down_ref, up_ref, *refs):
    pieces, (tokens_ref, out_ref) = refs[:-2], refs[-2:]
    rank = up_ref.shape[0] // groups
    rows = pieces[0].shape[0]
    tok_all = tokens_ref.shape[0]
    parts, slots, columns = out_ref.shape
    for i, (piece, source) in enumerate(zip(pieces, ring_sources("tp"))):
        start = pl.multiple_of(source * rows, rows)
        size = piece.shape[1]
        column = tokens_ref.shape[1] - size if i == len(pieces) - 1 else 0
        tokens_ref[pl.ds(start, rows), column : column + size] = piece[...]
    low = jnp.dot(tokens_ref[...], down_ref[...], preferred_element_type=jnp.float32)
    here = lax.broadcasted_iota(jnp.int32, (slots, tok_all), 0) + lax.axis_index("tp") * slots
    chosen = (here == place_ref[...]).astype(jnp.bfloat16)
    picked = jnp.dot(chosen, low.astype(jnp.bfloat16), preferred_element_type=jnp.float32)
    row_panel = lax.broadcasted_iota(jnp.int32, picked.shape, 0) // (slots // groups)
    rank_panel = lax.broadcasted_iota(jnp.int32, picked.shape, 1) // rank
    picked = jnp.where(row_panel == rank_panel, picked, 0.0).astype(jnp.bfloat16)
    for part in range(parts):
        out_ref[part] = jnp.dot(
            picked,
            up_ref[:, part * columns : (part + 1) * columns],
            preferred_element_type=jnp.float32,
        ).astype(out_ref.dtype)


def add_kernel(place_ref, base_ref, lifts_ref, out_ref):
    place = lax.broadcasted_iota(jnp.int32, (base_ref.shape[0], lifts_ref.shape[0]), 1)
    chosen = (place == place_ref[...]).astype(jnp.bfloat16)
    lift = jnp.dot(chosen, lifts_ref[...], preferred_element_type=jnp.float32)
    out_ref[...] = (base_ref[...] + adapter_scale * lift).astype(out_ref.dtype)


def on_device(
    tokens,
    base_projection_weight,
    adapter_down_panels,
    adapter_up_panels,
    request_adapter_ids,
    request_token_lengths,
    adapter_store_slot,
):
    groups = lax.axis_size("grp")
    tp = lax.axis_size("tp")
    width, rank = adapter_down_panels.shape[1:]
    columns = base_projection_weight.shape[1]
    tok_all = tokens.shape[1] * tp
    longest = tok_all // 8
    here = groups * longest
    in_vmem = pl.BlockSpec(memory_space=pltpu.VMEM)
    in_smem = pl.BlockSpec(memory_space=pltpu.SMEM)
    small = pltpu.CompilerParams(vmem_limit_bytes=16 * 2**20)

    panels = swapped(adapter_down_panels[0].T, "grp") + swapped(adapter_up_panels[0], "grp")
    down, up = pl.pallas_call(
        functools.partial(stack_kernel, groups),
        out_shape=[
            jax.ShapeDtypeStruct((width, groups * rank), jnp.bfloat16),
            jax.ShapeDtypeStruct((groups * rank, tp * columns), jnp.bfloat16),
        ],
        in_specs=[in_vmem] * len(panels),
        out_specs=[in_vmem] * 2,
        compiler_params=small,
        name="stack",
    )(*panels)
    row, column = pl.pallas_call(
        functools.partial(place_kernel, groups, tp),
        out_shape=[
            jax.ShapeDtypeStruct((1, tok_all), jnp.int32),
            jax.ShapeDtypeStruct((tok_all, 1), jnp.int32),
        ],
        in_specs=[in_smem] * 3,
        out_specs=[in_vmem] * 2,
        compiler_params=small,
        name="place",
    )(request_adapter_ids, request_token_lengths, adapter_store_slot)
    pieces = ring_gather(tokens[0], "tp", (down, up), (row, column))

    gathered, lifts = pl.pallas_call(
        functools.partial(lift_kernel, groups),
        out_shape=[
            jax.ShapeDtypeStruct((tok_all, width), jnp.bfloat16),
            jax.ShapeDtypeStruct((tp, here, columns), jnp.bfloat16),
        ],
        in_specs=[in_vmem] * (3 + len(pieces)),
        out_specs=[in_vmem] * 2,
        compiler_params=pltpu.CompilerParams(vmem_limit_bytes=24 * 2**20),
        cost_estimate=pl.CostEstimate(
            flops=2 * groups * rank * (tok_all * width + here * tp * columns),
            bytes_accessed=2 * groups * rank * (width + tp * columns),
            transcendentals=0,
        ),
        name="lift",
    )(row, down, up, *pieces)
    lifts = lax.all_to_all(lifts, "tp", split_axis=0, concat_axis=0, tiled=True)

    base = jnp.dot(gathered, base_projection_weight, preferred_element_type=jnp.float32)
    out = pl.pallas_call(
        add_kernel,
        out_shape=jax.ShapeDtypeStruct((tok_all, columns), jnp.bfloat16),
        in_specs=[in_vmem] * 3,
        out_specs=in_vmem,
        compiler_params=small,
        name="add",
    )(column, base, lifts.reshape(tp * here, columns))
    return out[None]


def solution(mesh):
    return jax.shard_map(
        on_device,
        mesh=mesh,
        in_specs=(
            P(("rep", "grp"), "tp", None),
            P(None, "tp"),
            P(("grp", "tp"), None, None),
            P(("grp", "tp"), None, None),
            P("rep", None),
            P(("rep", "grp"), None),
            P(),
        ),
        out_specs=P(("rep", "grp"), None, "tp"),
        check_vma=False,
    )
```

```python
import functools

import jax
import jax.numpy as jnp
from jax import lax
from jax.experimental import pallas as pl
from jax.experimental.pallas import tpu as pltpu
from jax.sharding import PartitionSpec as P

adapter_scale = 1.0


def swapped(x, axis):
    n = lax.axis_size(axis)
    return [x] + [
        lax.ppermute(x, axis, [((i + s) % n, i) for i in range(n)]) for s in range(1, n)
    ]


def ring_of(n):
    return list(range(0, n, 2)) + list(range(1, n, 2))[::-1]


def ring_gather(block, axis, first):
    n = lax.axis_size(axis)
    ring = ring_of(n)
    up = [(ring[i], ring[(i + 1) % n]) for i in range(n)]
    down = [(ring[(i + 1) % n], ring[i]) for i in range(n)]
    half = block.shape[1] // 2
    neighbours = lax.ppermute(block, axis, up), lax.ppermute(block, axis, down)
    cuts = [(0, 0), (1, 0), (0, half), (1, half)]
    streams = handed_on(neighbours, first, cuts, half)
    pieces = [block, *neighbours]
    for step in range(2, n // 2):
        streams = [lax.ppermute(x, axis, way) for x, way in zip(streams, (up, down) * 2)]
        pieces += streams
    return pieces + [lax.ppermute(streams[0], axis, up), lax.ppermute(streams[3], axis, down)]


def pass_kernel(cuts, *refs):
    for (i, start), target in zip(cuts, refs[-len(cuts) :]):
        target[...] = refs[i][:, start : start + target.shape[1]]


def handed_on(arrays, values, cuts, width):
    in_vmem = pl.BlockSpec(memory_space=pltpu.VMEM)
    return pl.pallas_call(
        functools.partial(pass_kernel, cuts),
        out_shape=[jax.ShapeDtypeStruct((arrays[0].shape[0], width), arrays[0].dtype)] * len(cuts),
        in_specs=[in_vmem] * len(arrays) + [pl.BlockSpec(memory_space=pl.ANY)] * len(values),
        out_specs=[in_vmem] * len(cuts),
        compiler_params=pltpu.CompilerParams(vmem_limit_bytes=16 * 2**20),
        name="pass",
    )(*arrays, *values)


def ring_sources(axis, half):
    n = lax.axis_size(axis)
    me = lax.axis_index(axis)
    place = jnp.where(lax.rem(me, 2) == 0, me // 2, n - 1 - me // 2)
    found = [(0, 0), (1, 0), (-1, 0)]
    for i in range(2, n // 2):
        found += [(i, 0), (-i, 0), (i, half), (-i, half)]
    found += [(n // 2, 0), (n // 2, half)]
    sources = []
    for distance, column in found:
        at = lax.rem(place - distance + n, n)
        sources.append((jnp.where(at < n // 2, 2 * at, 2 * (n - 1 - at) + 1), column))
    return sources


def stack_kernel(groups, *refs):
    downs, ups, (down_ref, up_ref) = refs[:groups], refs[groups:-2], refs[-2:]
    rank = ups[0].shape[0]
    down_ref[...] = jnp.concatenate([down[...] for down in downs], axis=0).T
    for s, up in enumerate(ups):
        up_ref[s * rank : (s + 1) * rank, :] = up[...]


def place_kernel(groups, tp, ids_ref, lengths_ref, slots_ref, row_ref, column_ref):
    group = lax.axis_index("grp")
    longest = row_ref.shape[1] // 8
    along = lax.broadcasted_iota(jnp.int32, row_ref.shape, 1)
    down = lax.broadcasted_iota(jnp.int32, column_ref.shape, 0)

    def add(request, carry):
        start, row, column = carry
        slot = slots_ref[ids_ref[group, request]]
        end = start + lengths_ref[0, request]
        panel = lax.rem(slot // tp - group + groups, groups)
        first = (lax.rem(slot, tp) * groups + panel) * longest - start
        row = jnp.where((along >= start) & (along < end), first + along, row)
        column = jnp.where((down >= start) & (down < end), first + down, column)
        return end, row, column

    carry = (jnp.int32(0), jnp.zeros_like(along), jnp.zeros_like(down))
    _, row_ref[...], column_ref[...] = lax.fori_loop(0, ids_ref.shape[1], add, carry)


def lift_kernel(groups, place_ref, down_ref, up_ref, *refs):
    pieces, (tokens_ref, out_ref) = refs[:-2], refs[-2:]
    rank = up_ref.shape[0] // groups
    rows = pieces[0].shape[0]
    tok_all = tokens_ref.shape[0]
    parts, slots, columns = out_ref.shape
    for piece, (source, column) in zip(pieces, ring_sources("tp", pieces[-1].shape[1])):
        start = pl.multiple_of(source * rows, rows)
        tokens_ref[pl.ds(start, rows), column : column + piece.shape[1]] = piece[...]
    low = jnp.dot(tokens_ref[...], down_ref[...], preferred_element_type=jnp.float32)
    here = lax.broadcasted_iota(jnp.int32, (slots, tok_all), 0) + lax.axis_index("tp") * slots
    chosen = (here == place_ref[...]).astype(jnp.bfloat16)
    picked = jnp.dot(chosen, low.astype(jnp.bfloat16), preferred_element_type=jnp.float32)
    row_panel = lax.broadcasted_iota(jnp.int32, picked.shape, 0) // (slots // groups)
    rank_panel = lax.broadcasted_iota(jnp.int32, picked.shape, 1) // rank
    picked = jnp.where(row_panel == rank_panel, picked, 0.0).astype(jnp.bfloat16)
    for part in range(parts):
        out_ref[part] = jnp.dot(
            picked,
            up_ref[:, part * columns : (part + 1) * columns],
            preferred_element_type=jnp.float32,
        ).astype(out_ref.dtype)


def add_kernel(place_ref, base_ref, lifts_ref, out_ref):
    place = lax.broadcasted_iota(jnp.int32, (base_ref.shape[0], lifts_ref.shape[0]), 1)
    chosen = (place == place_ref[...]).astype(jnp.bfloat16)
    lift = jnp.dot(chosen, lifts_ref[...], preferred_element_type=jnp.float32)
    out_ref[...] = (base_ref[...] + adapter_scale * lift).astype(out_ref.dtype)


def on_device(
    tokens,
    base_projection_weight,
    adapter_down_panels,
    adapter_up_panels,
    request_adapter_ids,
    request_token_lengths,
    adapter_store_slot,
):
    groups = lax.axis_size("grp")
    tp = lax.axis_size("tp")
    width, rank = adapter_down_panels.shape[1:]
    columns = base_projection_weight.shape[1]
    tok_all = tokens.shape[1] * tp
    longest = tok_all // 8
    here = groups * longest
    in_vmem = pl.BlockSpec(memory_space=pltpu.VMEM)
    in_smem = pl.BlockSpec(memory_space=pltpu.SMEM)
    small = pltpu.CompilerParams(vmem_limit_bytes=16 * 2**20)

    panels = swapped(adapter_down_panels[0].T, "grp") + swapped(adapter_up_panels[0], "grp")
    down, up = pl.pallas_call(
        functools.partial(stack_kernel, groups),
        out_shape=[
            jax.ShapeDtypeStruct((width, groups * rank), jnp.bfloat16),
            jax.ShapeDtypeStruct((groups * rank, tp * columns), jnp.bfloat16),
        ],
        in_specs=[in_vmem] * len(panels),
        out_specs=[in_vmem] * 2,
        compiler_params=small,
        name="stack",
    )(*panels)
    row, column = pl.pallas_call(
        functools.partial(place_kernel, groups, tp),
        out_shape=[
            jax.ShapeDtypeStruct((1, tok_all), jnp.int32),
            jax.ShapeDtypeStruct((tok_all, 1), jnp.int32),
        ],
        in_specs=[in_smem] * 3,
        out_specs=[in_vmem] * 2,
        compiler_params=small,
        name="place",
    )(request_adapter_ids, request_token_lengths, adapter_store_slot)
    pieces = ring_gather(tokens[0], "tp", (down, up, row, column))

    gathered, lifts = pl.pallas_call(
        functools.partial(lift_kernel, groups),
        out_shape=[
            jax.ShapeDtypeStruct((tok_all, width), jnp.bfloat16),
            jax.ShapeDtypeStruct((tp, here, columns), jnp.bfloat16),
        ],
        in_specs=[in_vmem] * (3 + len(pieces)),
        out_specs=[in_vmem] * 2,
        compiler_params=pltpu.CompilerParams(vmem_limit_bytes=24 * 2**20),
        cost_estimate=pl.CostEstimate(
            flops=2 * groups * rank * (tok_all * width + here * tp * columns),
            bytes_accessed=2 * groups * rank * (width + tp * columns),
            transcendentals=0,
        ),
        name="lift",
    )(row, down, up, *pieces)
    lifts = lax.all_to_all(lifts, "tp", split_axis=0, concat_axis=0, tiled=True)

    base = jnp.dot(gathered, base_projection_weight, preferred_element_type=jnp.float32)
    out = pl.pallas_call(
        add_kernel,
        out_shape=jax.ShapeDtypeStruct((tok_all, columns), jnp.bfloat16),
        in_specs=[in_vmem] * 3,
        out_specs=in_vmem,
        compiler_params=small,
        name="add",
    )(column, base, lifts.reshape(tp * here, columns))
    return out[None]


def solution(mesh):
    return jax.shard_map(
        on_device,
        mesh=mesh,
        in_specs=(
            P(("rep", "grp"), "tp", None),
            P(None, "tp"),
            P(("grp", "tp"), None, None),
            P(("grp", "tp"), None, None),
            P("rep", None),
            P(("rep", "grp"), None),
            P(),
        ),
        out_specs=P(("rep", "grp"), None, "tp"),
        check_vma=False,
    )
```

```python
import functools

import jax
import jax.numpy as jnp
from jax import lax
from jax.experimental import pallas as pl
from jax.experimental.pallas import tpu as pltpu
from jax.sharding import PartitionSpec as P

adapter_scale = 1.0


def swapped(x, axis):
    n = lax.axis_size(axis)
    return [x] + [
        lax.ppermute(x, axis, [((i + s) % n, i) for i in range(n)]) for s in range(1, n)
    ]


def ring_of(n):
    return list(range(0, n, 2)) + list(range(1, n, 2))[::-1]


def ring_gather(block, axis, first):
    n = lax.axis_size(axis)
    ring = ring_of(n)
    up = [(ring[i], ring[(i + 1) % n]) for i in range(n)]
    down = [(ring[(i + 1) % n], ring[i]) for i in range(n)]
    half = block.shape[1] // 2
    neighbours = lax.ppermute(block, axis, up), lax.ppermute(block, axis, down)
    cuts = [(0, 0), (1, 0), (0, half), (1, half)]
    streams = handed_on(neighbours, first, cuts, half)
    pieces = [block, *neighbours]
    for step in range(2, n // 2):
        streams = [lax.ppermute(x, axis, way) for x, way in zip(streams, (up, down) * 2)]
        pieces += streams
    return pieces + [lax.ppermute(streams[0], axis, up), lax.ppermute(streams[3], axis, down)]


def pass_kernel(cuts, *refs):
    for (i, start), target in zip(cuts, refs[-len(cuts) :]):
        target[...] = refs[i][:, start : start + target.shape[1]]


def handed_on(arrays, values, cuts, width):
    in_vmem = pl.BlockSpec(memory_space=pltpu.VMEM)
    return pl.pallas_call(
        functools.partial(pass_kernel, cuts),
        out_shape=[jax.ShapeDtypeStruct((arrays[0].shape[0], width), arrays[0].dtype)] * len(cuts),
        in_specs=[in_vmem] * len(arrays) + [pl.BlockSpec(memory_space=pl.ANY)] * len(values),
        out_specs=[in_vmem] * len(cuts),
        compiler_params=pltpu.CompilerParams(vmem_limit_bytes=16 * 2**20),
        name="pass",
    )(*arrays, *values)


def ring_place(i, n):
    return jnp.where(lax.rem(i, 2) == 0, i // 2, n - 1 - i // 2)


def ring_sources(axis, half):
    n = lax.axis_size(axis)
    place = ring_place(lax.axis_index(axis), n)
    found = [(0, 0), (1, 0), (-1, 0)]
    for i in range(2, n // 2):
        found += [(i, 0), (-i, 0), (i, half), (-i, half)]
    found += [(n // 2, 0), (n // 2, half)]
    sources = []
    for distance, column in found:
        at = lax.rem(place - distance + n, n)
        sources.append((jnp.where(at < n // 2, 2 * at, 2 * (n - 1 - at) + 1), column))
    return sources


def stack_kernel(groups, *refs):
    downs, ups, (down_ref, up_ref) = refs[:groups], refs[groups:-2], refs[-2:]
    rank = ups[0].shape[0]
    down_ref[...] = jnp.concatenate([down[...] for down in downs], axis=0).T
    for s, up in enumerate(ups):
        up_ref[s * rank : (s + 1) * rank, :] = up[...]


def place_kernel(groups, tp, ids_ref, lengths_ref, slots_ref, row_ref, column_ref):
    group = lax.axis_index("grp")
    longest = row_ref.shape[1] // 8
    along = lax.broadcasted_iota(jnp.int32, row_ref.shape, 1)
    down = lax.broadcasted_iota(jnp.int32, column_ref.shape, 0)

    def add(request, carry):
        start, row, column = carry
        slot = slots_ref[ids_ref[group, request]]
        end = start + lengths_ref[0, request]
        panel = lax.rem(slot // tp - group + groups, groups)
        first = (ring_place(lax.rem(slot, tp), tp) * groups + panel) * longest - start
        row = jnp.where((along >= start) & (along < end), first + along, row)
        column = jnp.where((down >= start) & (down < end), first + down, column)
        return end, row, column

    carry = (jnp.int32(0), jnp.zeros_like(along), jnp.zeros_like(down))
    _, row_ref[...], column_ref[...] = lax.fori_loop(0, ids_ref.shape[1], add, carry)


def lift_kernel(groups, place_ref, down_ref, up_ref, *refs):
    pieces, (tokens_ref, out_ref) = refs[:-2], refs[-2:]
    rank = up_ref.shape[0] // groups
    rows = pieces[0].shape[0]
    tok_all = tokens_ref.shape[0]
    parts, slots, columns = out_ref.shape
    for piece, (source, column) in zip(pieces, ring_sources("tp", pieces[-1].shape[1])):
        start = pl.multiple_of(source * rows, rows)
        tokens_ref[pl.ds(start, rows), column : column + piece.shape[1]] = piece[...]
    low = jnp.dot(tokens_ref[...], down_ref[...], preferred_element_type=jnp.float32)
    place = ring_place(lax.axis_index("tp"), parts)
    here = lax.broadcasted_iota(jnp.int32, (slots, tok_all), 0) + place * slots
    chosen = (here == place_ref[...]).astype(jnp.bfloat16)
    picked = jnp.dot(chosen, low.astype(jnp.bfloat16), preferred_element_type=jnp.float32)
    row_panel = lax.broadcasted_iota(jnp.int32, picked.shape, 0) // (slots // groups)
    rank_panel = lax.broadcasted_iota(jnp.int32, picked.shape, 1) // rank
    picked = jnp.where(row_panel == rank_panel, picked, 0.0).astype(jnp.bfloat16)
    for part, owner in enumerate(ring_of(parts)):
        out_ref[part] = jnp.dot(
            picked,
            up_ref[:, owner * columns : (owner + 1) * columns],
            preferred_element_type=jnp.float32,
        ).astype(out_ref.dtype)


def add_kernel(place_ref, base_ref, lifts_ref, out_ref):
    place = lax.broadcasted_iota(jnp.int32, (base_ref.shape[0], lifts_ref.shape[0]), 1)
    chosen = (place == place_ref[...]).astype(jnp.bfloat16)
    lift = jnp.dot(chosen, lifts_ref[...], preferred_element_type=jnp.float32)
    out_ref[...] = (base_ref[...] + adapter_scale * lift).astype(out_ref.dtype)


def on_device(
    tokens,
    base_projection_weight,
    adapter_down_panels,
    adapter_up_panels,
    request_adapter_ids,
    request_token_lengths,
    adapter_store_slot,
):
    groups = lax.axis_size("grp")
    tp = lax.axis_size("tp")
    width, rank = adapter_down_panels.shape[1:]
    columns = base_projection_weight.shape[1]
    tok_all = tokens.shape[1] * tp
    longest = tok_all // 8
    here = groups * longest
    in_vmem = pl.BlockSpec(memory_space=pltpu.VMEM)
    in_smem = pl.BlockSpec(memory_space=pltpu.SMEM)
    small = pltpu.CompilerParams(vmem_limit_bytes=16 * 2**20)

    panels = swapped(adapter_down_panels[0].T, "grp") + swapped(adapter_up_panels[0], "grp")
    down, up = pl.pallas_call(
        functools.partial(stack_kernel, groups),
        out_shape=[
            jax.ShapeDtypeStruct((width, groups * rank), jnp.bfloat16),
            jax.ShapeDtypeStruct((groups * rank, tp * columns), jnp.bfloat16),
        ],
        in_specs=[in_vmem] * len(panels),
        out_specs=[in_vmem] * 2,
        compiler_params=small,
        name="stack",
    )(*panels)
    row, column = pl.pallas_call(
        functools.partial(place_kernel, groups, tp),
        out_shape=[
            jax.ShapeDtypeStruct((1, tok_all), jnp.int32),
            jax.ShapeDtypeStruct((tok_all, 1), jnp.int32),
        ],
        in_specs=[in_smem] * 3,
        out_specs=[in_vmem] * 2,
        compiler_params=small,
        name="place",
    )(request_adapter_ids, request_token_lengths, adapter_store_slot)
    pieces = ring_gather(tokens[0], "tp", (down, up, row, column))

    gathered, lifts = pl.pallas_call(
        functools.partial(lift_kernel, groups),
        out_shape=[
            jax.ShapeDtypeStruct((tok_all, width), jnp.bfloat16),
            jax.ShapeDtypeStruct((tp, here, columns), jnp.bfloat16),
        ],
        in_specs=[in_vmem] * (3 + len(pieces)),
        out_specs=[in_vmem] * 2,
        compiler_params=pltpu.CompilerParams(vmem_limit_bytes=24 * 2**20),
        cost_estimate=pl.CostEstimate(
            flops=2 * groups * rank * (tok_all * width + here * tp * columns),
            bytes_accessed=2 * groups * rank * (width + tp * columns),
            transcendentals=0,
        ),
        name="lift",
    )(row, down, up, *pieces)
    lifts = lax.all_to_all(
        lifts, "tp", split_axis=0, concat_axis=0, axis_index_groups=[ring_of(tp)], tiled=True
    )

    base = jnp.dot(gathered, base_projection_weight, preferred_element_type=jnp.float32)
    out = pl.pallas_call(
        add_kernel,
        out_shape=jax.ShapeDtypeStruct((tok_all, columns), jnp.bfloat16),
        in_specs=[in_vmem] * 3,
        out_specs=in_vmem,
        compiler_params=small,
        name="add",
    )(column, base, lifts.reshape(tp * here, columns))
    return out[None]


def solution(mesh):
    return jax.shard_map(
        on_device,
        mesh=mesh,
        in_specs=(
            P(("rep", "grp"), "tp", None),
            P(None, "tp"),
            P(("grp", "tp"), None, None),
            P(("grp", "tp"), None, None),
            P("rep", None),
            P(("rep", "grp"), None),
            P(),
        ),
        out_specs=P(("rep", "grp"), None, "tp"),
        check_vma=False,
    )
```

```python
import functools

import jax
import jax.numpy as jnp
from jax import lax
from jax.experimental import pallas as pl
from jax.experimental.pallas import tpu as pltpu
from jax.sharding import PartitionSpec as P

adapter_scale = 1.0


def swapped(x, axis):
    n = lax.axis_size(axis)
    return [x] + [
        lax.ppermute(x, axis, [((i + s) % n, i) for i in range(n)]) for s in range(1, n)
    ]


def ring_of(n):
    return list(range(0, n, 2)) + list(range(1, n, 2))[::-1]


def ring_gather(block, axis, first):
    n = lax.axis_size(axis)
    ring = ring_of(n)
    up = [(ring[i], ring[(i + 1) % n]) for i in range(n)]
    down = [(ring[(i + 1) % n], ring[i]) for i in range(n)]
    half = block.shape[1] // 2
    neighbours = lax.ppermute(block, axis, up), lax.ppermute(block, axis, down)
    cuts = [(0, 0), (1, 0), (0, half), (1, half)]
    streams = handed_on(neighbours, first, cuts, half)
    pieces = [block, *neighbours]
    for step in range(2, n // 2):
        streams = [lax.ppermute(x, axis, way) for x, way in zip(streams, (up, down) * 2)]
        pieces += streams
    return pieces + [lax.ppermute(streams[0], axis, up), lax.ppermute(streams[3], axis, down)]


def pass_kernel(cuts, *refs):
    for (i, start), target in zip(cuts, refs[-len(cuts) :]):
        target[...] = refs[i][:, start : start + target.shape[1]]


def handed_on(arrays, values, cuts, width):
    in_vmem = pl.BlockSpec(memory_space=pltpu.VMEM)
    return pl.pallas_call(
        functools.partial(pass_kernel, cuts),
        out_shape=[jax.ShapeDtypeStruct((arrays[0].shape[0], width), arrays[0].dtype)] * len(cuts),
        in_specs=[in_vmem] * len(arrays) + [pl.BlockSpec(memory_space=pl.ANY)] * len(values),
        out_specs=[in_vmem] * len(cuts),
        compiler_params=pltpu.CompilerParams(vmem_limit_bytes=16 * 2**20),
        name="pass",
    )(*arrays, *values)


def listed(n):
    return [i // 2 + i % 2 * (n // 2) for i in range(n)]


def listed_place(i, n):
    return jnp.where(i < n // 2, 2 * i, 2 * i - n + 1)


def ring_place(i, n):
    return jnp.where(lax.rem(i, 2) == 0, i // 2, n - 1 - i // 2)


def ring_sources(axis, half):
    n = lax.axis_size(axis)
    place = ring_place(lax.axis_index(axis), n)
    found = [(0, 0), (1, 0), (-1, 0)]
    for i in range(2, n // 2):
        found += [(i, 0), (-i, 0), (i, half), (-i, half)]
    found += [(n // 2, 0), (n // 2, half)]
    sources = []
    for distance, column in found:
        at = lax.rem(place - distance + n, n)
        sources.append((jnp.where(at < n // 2, 2 * at, 2 * (n - 1 - at) + 1), column))
    return sources


def stack_kernel(groups, *refs):
    downs, ups, (down_ref, up_ref) = refs[:groups], refs[groups:-2], refs[-2:]
    rank = ups[0].shape[0]
    down_ref[...] = jnp.concatenate([down[...] for down in downs], axis=0).T
    for s, up in enumerate(ups):
        up_ref[s * rank : (s + 1) * rank, :] = up[...]


def place_kernel(groups, tp, ids_ref, lengths_ref, slots_ref, row_ref, column_ref):
    group = lax.axis_index("grp")
    longest = row_ref.shape[1] // 8
    along = lax.broadcasted_iota(jnp.int32, row_ref.shape, 1)
    down = lax.broadcasted_iota(jnp.int32, column_ref.shape, 0)

    def add(request, carry):
        start, row, column = carry
        slot = slots_ref[ids_ref[group, request]]
        end = start + lengths_ref[0, request]
        panel = lax.rem(slot // tp - group + groups, groups)
        first = (listed_place(lax.rem(slot, tp), tp) * groups + panel) * longest - start
        row = jnp.where((along >= start) & (along < end), first + along, row)
        column = jnp.where((down >= start) & (down < end), first + down, column)
        return end, row, column

    carry = (jnp.int32(0), jnp.zeros_like(along), jnp.zeros_like(down))
    _, row_ref[...], column_ref[...] = lax.fori_loop(0, ids_ref.shape[1], add, carry)


def lift_kernel(groups, place_ref, down_ref, up_ref, *refs):
    pieces, (tokens_ref, out_ref) = refs[:-2], refs[-2:]
    rank = up_ref.shape[0] // groups
    rows = pieces[0].shape[0]
    tok_all = tokens_ref.shape[0]
    parts, slots, columns = out_ref.shape
    for piece, (source, column) in zip(pieces, ring_sources("tp", pieces[-1].shape[1])):
        start = pl.multiple_of(source * rows, rows)
        tokens_ref[pl.ds(start, rows), column : column + piece.shape[1]] = piece[...]
    low = jnp.dot(tokens_ref[...], down_ref[...], preferred_element_type=jnp.float32)
    place = listed_place(lax.axis_index("tp"), parts)
    here = lax.broadcasted_iota(jnp.int32, (slots, tok_all), 0) + place * slots
    chosen = (here == place_ref[...]).astype(jnp.bfloat16)
    picked = jnp.dot(chosen, low.astype(jnp.bfloat16), preferred_element_type=jnp.float32)
    row_panel = lax.broadcasted_iota(jnp.int32, picked.shape, 0) // (slots // groups)
    rank_panel = lax.broadcasted_iota(jnp.int32, picked.shape, 1) // rank
    picked = jnp.where(row_panel == rank_panel, picked, 0.0).astype(jnp.bfloat16)
    for part, owner in enumerate(listed(parts)):
        out_ref[part] = jnp.dot(
            picked,
            up_ref[:, owner * columns : (owner + 1) * columns],
            preferred_element_type=jnp.float32,
        ).astype(out_ref.dtype)


def add_kernel(place_ref, base_ref, lifts_ref, out_ref):
    place = lax.broadcasted_iota(jnp.int32, (base_ref.shape[0], lifts_ref.shape[0]), 1)
    chosen = (place == place_ref[...]).astype(jnp.bfloat16)
    lift = jnp.dot(chosen, lifts_ref[...], preferred_element_type=jnp.float32)
    out_ref[...] = (base_ref[...] + adapter_scale * lift).astype(out_ref.dtype)


def on_device(
    tokens,
    base_projection_weight,
    adapter_down_panels,
    adapter_up_panels,
    request_adapter_ids,
    request_token_lengths,
    adapter_store_slot,
):
    groups = lax.axis_size("grp")
    tp = lax.axis_size("tp")
    width, rank = adapter_down_panels.shape[1:]
    columns = base_projection_weight.shape[1]
    tok_all = tokens.shape[1] * tp
    longest = tok_all // 8
    here = groups * longest
    in_vmem = pl.BlockSpec(memory_space=pltpu.VMEM)
    in_smem = pl.BlockSpec(memory_space=pltpu.SMEM)
    small = pltpu.CompilerParams(vmem_limit_bytes=16 * 2**20)

    panels = swapped(adapter_down_panels[0].T, "grp") + swapped(adapter_up_panels[0], "grp")
    down, up = pl.pallas_call(
        functools.partial(stack_kernel, groups),
        out_shape=[
            jax.ShapeDtypeStruct((width, groups * rank), jnp.bfloat16),
            jax.ShapeDtypeStruct((groups * rank, tp * columns), jnp.bfloat16),
        ],
        in_specs=[in_vmem] * len(panels),
        out_specs=[in_vmem] * 2,
        compiler_params=small,
        name="stack",
    )(*panels)
    row, column = pl.pallas_call(
        functools.partial(place_kernel, groups, tp),
        out_shape=[
            jax.ShapeDtypeStruct((1, tok_all), jnp.int32),
            jax.ShapeDtypeStruct((tok_all, 1), jnp.int32),
        ],
        in_specs=[in_smem] * 3,
        out_specs=[in_vmem] * 2,
        compiler_params=small,
        name="place",
    )(request_adapter_ids, request_token_lengths, adapter_store_slot)
    pieces = ring_gather(tokens[0], "tp", (down, up, row, column))

    gathered, lifts = pl.pallas_call(
        functools.partial(lift_kernel, groups),
        out_shape=[
            jax.ShapeDtypeStruct((tok_all, width), jnp.bfloat16),
            jax.ShapeDtypeStruct((tp, here, columns), jnp.bfloat16),
        ],
        in_specs=[in_vmem] * (3 + len(pieces)),
        out_specs=[in_vmem] * 2,
        compiler_params=pltpu.CompilerParams(vmem_limit_bytes=24 * 2**20),
        cost_estimate=pl.CostEstimate(
            flops=2 * groups * rank * (tok_all * width + here * tp * columns),
            bytes_accessed=2 * groups * rank * (width + tp * columns),
            transcendentals=0,
        ),
        name="lift",
    )(row, down, up, *pieces)
    lifts = lax.all_to_all(
        lifts, "tp", split_axis=0, concat_axis=0, axis_index_groups=[listed(tp)], tiled=True
    )

    base = jnp.dot(gathered, base_projection_weight, preferred_element_type=jnp.float32)
    out = pl.pallas_call(
        add_kernel,
        out_shape=jax.ShapeDtypeStruct((tok_all, columns), jnp.bfloat16),
        in_specs=[in_vmem] * 3,
        out_specs=in_vmem,
        compiler_params=small,
        name="add",
    )(column, base, lifts.reshape(tp * here, columns))
    return out[None]


def solution(mesh):
    return jax.shard_map(
        on_device,
        mesh=mesh,
        in_specs=(
            P(("rep", "grp"), "tp", None),
            P(None, "tp"),
            P(("grp", "tp"), None, None),
            P(("grp", "tp"), None, None),
            P("rep", None),
            P(("rep", "grp"), None),
            P(),
        ),
        out_specs=P(("rep", "grp"), None, "tp"),
        check_vma=False,
    )
```

```python
import functools

import jax
import jax.numpy as jnp
from jax import lax
from jax.experimental import pallas as pl
from jax.experimental.pallas import tpu as pltpu
from jax.sharding import PartitionSpec as P

adapter_scale = 1.0


def swapped(x, axis):
    n = lax.axis_size(axis)
    return [x] + [
        lax.ppermute(x, axis, [((i + s) % n, i) for i in range(n)]) for s in range(1, n)
    ]


def ring_of(n):
    return list(range(0, n, 2)) + list(range(1, n, 2))[::-1]


def ring_gather(block, axis, first):
    n = lax.axis_size(axis)
    ring = ring_of(n)
    up = [(ring[i], ring[(i + 1) % n]) for i in range(n)]
    down = [(ring[(i + 1) % n], ring[i]) for i in range(n)]
    half = block.shape[1] // 2
    neighbours = lax.ppermute(block, axis, up), lax.ppermute(block, axis, down)
    cuts = [(0, 0), (1, 0), (0, half), (1, half)]
    streams = handed_on(neighbours, first, cuts, half)
    pieces = [block, *neighbours]
    for step in range(2, n // 2):
        streams = [lax.ppermute(x, axis, way) for x, way in zip(streams, (up, down) * 2)]
        pieces += streams
    return pieces + [lax.ppermute(streams[0], axis, up), lax.ppermute(streams[3], axis, down)]


def pass_kernel(cuts, *refs):
    for (i, start), target in zip(cuts, refs[-len(cuts) :]):
        target[...] = refs[i][:, start : start + target.shape[1]]


def handed_on(arrays, values, cuts, width):
    in_vmem = pl.BlockSpec(memory_space=pltpu.VMEM)
    return pl.pallas_call(
        functools.partial(pass_kernel, cuts),
        out_shape=[jax.ShapeDtypeStruct((arrays[0].shape[0], width), arrays[0].dtype)] * len(cuts),
        in_specs=[in_vmem] * len(arrays) + [pl.BlockSpec(memory_space=pl.ANY)] * len(values),
        out_specs=[in_vmem] * len(cuts),
        compiler_params=pltpu.CompilerParams(vmem_limit_bytes=16 * 2**20),
        name="pass",
    )(*arrays, *values)


def ring_place(i, n):
    return jnp.where(lax.rem(i, 2) == 0, i // 2, n - 1 - i // 2)


def exchange_groups(groups, n):
    ring = ring_of(n)
    return [[g * n + ring[-p if g % 2 else p] for p in range(n)] for g in range(groups)]


def exchange_place(i, n):
    place = ring_place(i, n)
    return jnp.where(lax.rem(lax.axis_index("grp"), 2) == 0, place, lax.rem(n - place, n))


def ring_sources(axis, half):
    n = lax.axis_size(axis)
    place = ring_place(lax.axis_index(axis), n)
    found = [(0, 0), (1, 0), (-1, 0)]
    for i in range(2, n // 2):
        found += [(i, 0), (-i, 0), (i, half), (-i, half)]
    found += [(n // 2, 0), (n // 2, half)]
    sources = []
    for distance, column in found:
        at = lax.rem(place - distance + n, n)
        sources.append((jnp.where(at < n // 2, 2 * at, 2 * (n - 1 - at) + 1), column))
    return sources


def stack_kernel(groups, *refs):
    downs, ups, (down_ref, up_ref) = refs[:groups], refs[groups:-2], refs[-2:]
    rank = ups[0].shape[0]
    down_ref[...] = jnp.concatenate([down[...] for down in downs], axis=0).T
    for s, up in enumerate(ups):
        up_ref[s * rank : (s + 1) * rank, :] = up[...]


def place_kernel(groups, tp, ids_ref, lengths_ref, slots_ref, row_ref, column_ref):
    group = lax.axis_index("grp")
    longest = row_ref.shape[1] // 8
    along = lax.broadcasted_iota(jnp.int32, row_ref.shape, 1)
    down = lax.broadcasted_iota(jnp.int32, column_ref.shape, 0)

    def add(request, carry):
        start, row, column = carry
        slot = slots_ref[ids_ref[group, request]]
        end = start + lengths_ref[0, request]
        panel = lax.rem(slot // tp - group + groups, groups)
        first = (exchange_place(lax.rem(slot, tp), tp) * groups + panel) * longest - start
        row = jnp.where((along >= start) & (along < end), first + along, row)
        column = jnp.where((down >= start) & (down < end), first + down, column)
        return end, row, column

    carry = (jnp.int32(0), jnp.zeros_like(along), jnp.zeros_like(down))
    _, row_ref[...], column_ref[...] = lax.fori_loop(0, ids_ref.shape[1], add, carry)


def lift_kernel(groups, place_ref, down_ref, up_ref, *refs):
    pieces, (tokens_ref, out_ref) = refs[:-2], refs[-2:]
    rank = up_ref.shape[0] // groups
    rows = pieces[0].shape[0]
    tok_all = tokens_ref.shape[0]
    parts, slots, columns = out_ref.shape
    for piece, (source, column) in zip(pieces, ring_sources("tp", pieces[-1].shape[1])):
        start = pl.multiple_of(source * rows, rows)
        tokens_ref[pl.ds(start, rows), column : column + piece.shape[1]] = piece[...]
    low = jnp.dot(tokens_ref[...], down_ref[...], preferred_element_type=jnp.float32)
    place = exchange_place(lax.axis_index("tp"), parts)
    here = lax.broadcasted_iota(jnp.int32, (slots, tok_all), 0) + place * slots
    chosen = (here == place_ref[...]).astype(jnp.bfloat16)
    picked = jnp.dot(chosen, low.astype(jnp.bfloat16), preferred_element_type=jnp.float32)
    row_panel = lax.broadcasted_iota(jnp.int32, picked.shape, 0) // (slots // groups)
    rank_panel = lax.broadcasted_iota(jnp.int32, picked.shape, 1) // rank
    picked = jnp.where(row_panel == rank_panel, picked, 0.0).astype(jnp.bfloat16)
    for owner in range(parts):
        out_ref[exchange_place(jnp.int32(owner), parts)] = jnp.dot(
            picked,
            up_ref[:, owner * columns : (owner + 1) * columns],
            preferred_element_type=jnp.float32,
        ).astype(out_ref.dtype)


def add_kernel(place_ref, base_ref, lifts_ref, out_ref):
    place = lax.broadcasted_iota(jnp.int32, (base_ref.shape[0], lifts_ref.shape[0]), 1)
    chosen = (place == place_ref[...]).astype(jnp.bfloat16)
    lift = jnp.dot(chosen, lifts_ref[...], preferred_element_type=jnp.float32)
    out_ref[...] = (base_ref[...] + adapter_scale * lift).astype(out_ref.dtype)


def on_device(
    tokens,
    base_projection_weight,
    adapter_down_panels,
    adapter_up_panels,
    request_adapter_ids,
    request_token_lengths,
    adapter_store_slot,
):
    groups = lax.axis_size("grp")
    tp = lax.axis_size("tp")
    width, rank = adapter_down_panels.shape[1:]
    columns = base_projection_weight.shape[1]
    tok_all = tokens.shape[1] * tp
    longest = tok_all // 8
    here = groups * longest
    in_vmem = pl.BlockSpec(memory_space=pltpu.VMEM)
    in_smem = pl.BlockSpec(memory_space=pltpu.SMEM)
    small = pltpu.CompilerParams(vmem_limit_bytes=16 * 2**20)

    panels = swapped(adapter_down_panels[0].T, "grp") + swapped(adapter_up_panels[0], "grp")
    down, up = pl.pallas_call(
        functools.partial(stack_kernel, groups),
        out_shape=[
            jax.ShapeDtypeStruct((width, groups * rank), jnp.bfloat16),
            jax.ShapeDtypeStruct((groups * rank, tp * columns), jnp.bfloat16),
        ],
        in_specs=[in_vmem] * len(panels),
        out_specs=[in_vmem] * 2,
        compiler_params=small,
        name="stack",
    )(*panels)
    row, column = pl.pallas_call(
        functools.partial(place_kernel, groups, tp),
        out_shape=[
            jax.ShapeDtypeStruct((1, tok_all), jnp.int32),
            jax.ShapeDtypeStruct((tok_all, 1), jnp.int32),
        ],
        in_specs=[in_smem] * 3,
        out_specs=[in_vmem] * 2,
        compiler_params=small,
        name="place",
    )(request_adapter_ids, request_token_lengths, adapter_store_slot)
    pieces = ring_gather(tokens[0], "tp", (down, up, row, column))

    gathered, lifts = pl.pallas_call(
        functools.partial(lift_kernel, groups),
        out_shape=[
            jax.ShapeDtypeStruct((tok_all, width), jnp.bfloat16),
            jax.ShapeDtypeStruct((tp, here, columns), jnp.bfloat16),
        ],
        in_specs=[in_vmem] * (3 + len(pieces)),
        out_specs=[in_vmem] * 2,
        compiler_params=pltpu.CompilerParams(vmem_limit_bytes=24 * 2**20),
        cost_estimate=pl.CostEstimate(
            flops=2 * groups * rank * (tok_all * width + here * tp * columns),
            bytes_accessed=2 * groups * rank * (width + tp * columns),
            transcendentals=0,
        ),
        name="lift",
    )(row, down, up, *pieces)
    lifts = lax.all_to_all(
        lifts,
        ("grp", "tp"),
        split_axis=0,
        concat_axis=0,
        axis_index_groups=exchange_groups(groups, tp),
        tiled=True,
    )

    base = jnp.dot(gathered, base_projection_weight, preferred_element_type=jnp.float32)
    out = pl.pallas_call(
        add_kernel,
        out_shape=jax.ShapeDtypeStruct((tok_all, columns), jnp.bfloat16),
        in_specs=[in_vmem] * 3,
        out_specs=in_vmem,
        compiler_params=small,
        name="add",
    )(column, base, lifts.reshape(tp * here, columns))
    return out[None]


def solution(mesh):
    return jax.shard_map(
        on_device,
        mesh=mesh,
        in_specs=(
            P(("rep", "grp"), "tp", None),
            P(None, "tp"),
            P(("grp", "tp"), None, None),
            P(("grp", "tp"), None, None),
            P("rep", None),
            P(("rep", "grp"), None),
            P(),
        ),
        out_specs=P(("rep", "grp"), None, "tp"),
        check_vma=False,
    )
```

```python
import functools

import jax
import jax.numpy as jnp
from jax import lax
from jax.experimental import pallas as pl
from jax.experimental.pallas import tpu as pltpu
from jax.sharding import PartitionSpec as P

adapter_scale = 1.0


def swapped(x, axis):
    n = lax.axis_size(axis)
    return [x] + [
        lax.ppermute(x, axis, [((i + s) % n, i) for i in range(n)]) for s in range(1, n)
    ]


def ring_of(n):
    return list(range(0, n, 2)) + list(range(1, n, 2))[::-1]


def ring_gather(block, axis, first):
    n = lax.axis_size(axis)
    ring = ring_of(n)
    up = [(ring[i], ring[(i + 1) % n]) for i in range(n)]
    down = [(ring[(i + 1) % n], ring[i]) for i in range(n)]
    half = block.shape[1] // 2
    neighbours = lax.ppermute(block, axis, up), lax.ppermute(block, axis, down)
    cuts = [(0, 0), (1, 0), (0, half), (1, half)]
    streams = handed_on(neighbours, first, cuts, half)
    pieces = [block, *neighbours]
    for step in range(2, n // 2):
        streams = [lax.ppermute(x, axis, way) for x, way in zip(streams, (up, down) * 2)]
        pieces += streams
    return pieces + [lax.ppermute(streams[0], axis, up), lax.ppermute(streams[3], axis, down)]


def pass_kernel(cuts, *refs):
    for (i, start), target in zip(cuts, refs[-len(cuts) :]):
        target[...] = refs[i][:, start : start + target.shape[1]]


def handed_on(arrays, values, cuts, width):
    in_vmem = pl.BlockSpec(memory_space=pltpu.VMEM)
    return pl.pallas_call(
        functools.partial(pass_kernel, cuts),
        out_shape=[jax.ShapeDtypeStruct((arrays[0].shape[0], width), arrays[0].dtype)] * len(cuts),
        in_specs=[in_vmem] * len(arrays) + [pl.BlockSpec(memory_space=pl.ANY)] * len(values),
        out_specs=[in_vmem] * len(cuts),
        compiler_params=pltpu.CompilerParams(vmem_limit_bytes=16 * 2**20),
        name="pass",
    )(*arrays, *values)


def ring_sources(axis, half):
    n = lax.axis_size(axis)
    me = lax.axis_index(axis)
    place = jnp.where(lax.rem(me, 2) == 0, me // 2, n - 1 - me // 2)
    found = [(0, 0), (1, 0), (-1, 0)]
    for i in range(2, n // 2):
        found += [(i, 0), (-i, 0), (i, half), (-i, half)]
    found += [(n // 2, 0), (n // 2, half)]
    sources = []
    for distance, column in found:
        at = lax.rem(place - distance + n, n)
        sources.append((jnp.where(at < n // 2, 2 * at, 2 * (n - 1 - at) + 1), column))
    return sources


def stack_kernel(groups, *refs):
    downs, ups, (down_ref, up_ref) = refs[:groups], refs[groups:-2], refs[-2:]
    rank = ups[0].shape[0]
    down_ref[...] = jnp.concatenate([down[...] for down in downs], axis=0).T
    for s, up in enumerate(ups):
        up_ref[s * rank : (s + 1) * rank, :] = up[...]


def place_kernel(groups, tp, ids_ref, lengths_ref, slots_ref, row_ref, column_ref):
    group = lax.axis_index("grp")
    longest = row_ref.shape[1] // 8
    along = lax.broadcasted_iota(jnp.int32, row_ref.shape, 1)
    down = lax.broadcasted_iota(jnp.int32, column_ref.shape, 0)

    def add(request, carry):
        start, row, column = carry
        slot = slots_ref[ids_ref[group, request]]
        end = start + lengths_ref[0, request]
        panel = lax.rem(slot // tp - group + groups, groups)
        chip = lax.rem(slot, tp)
        other_row = lax.rem(chip + lax.axis_index("tp"), 2)
        chip = other_row * (tp // 2) + chip // 2
        first = (chip * groups + panel) * longest - start
        row = jnp.where((along >= start) & (along < end), first + along, row)
        column = jnp.where((down >= start) & (down < end), first + down, column)
        return end, row, column

    carry = (jnp.int32(0), jnp.zeros_like(along), jnp.zeros_like(down))
    _, row_ref[...], column_ref[...] = lax.fori_loop(0, ids_ref.shape[1], add, carry)


def lift_kernel(groups, place_ref, down_ref, up_ref, *refs):
    pieces, (tokens_ref, *out_refs) = refs[:-3], refs[-3:]
    rank = up_ref.shape[0] // groups
    rows = pieces[0].shape[0]
    tok_all = tokens_ref.shape[0]
    parts, slots, columns = out_refs[0].shape
    for piece, (source, column) in zip(pieces, ring_sources("tp", pieces[-1].shape[1])):
        start = pl.multiple_of(source * rows, rows)
        tokens_ref[pl.ds(start, rows), column : column + piece.shape[1]] = piece[...]
    low = jnp.dot(tokens_ref[...], down_ref[...], preferred_element_type=jnp.float32)
    me = lax.axis_index("tp")
    here = lax.broadcasted_iota(jnp.int32, (slots, tok_all), 0) + me // 2 * slots
    chosen = (here == place_ref[...]).astype(jnp.bfloat16)
    picked = jnp.dot(chosen, low.astype(jnp.bfloat16), preferred_element_type=jnp.float32)
    row_panel = lax.broadcasted_iota(jnp.int32, picked.shape, 0) // (slots // groups)
    rank_panel = lax.broadcasted_iota(jnp.int32, picked.shape, 1) // rank
    picked = jnp.where(row_panel == rank_panel, picked, 0.0).astype(jnp.bfloat16)
    for owner in range(2 * parts):
        lifts = jnp.dot(
            picked,
            up_ref[:, owner * columns : (owner + 1) * columns],
            preferred_element_type=jnp.float32,
        ).astype(out_refs[0].dtype)
        for other_row, out_ref in enumerate(out_refs):

            @pl.when(lax.rem(me + owner, 2) == other_row)
            def _():
                out_ref[owner // 2] = lifts


def add_kernel(place_ref, base_ref, *refs):
    parts, (out_ref, lifts_ref) = refs[:-2], refs[-2:]
    rows = parts[0].shape[0]
    for i, part in enumerate(parts):
        lifts_ref[i * rows : (i + 1) * rows, :] = part[...]
    place = lax.broadcasted_iota(jnp.int32, (base_ref.shape[0], lifts_ref.shape[0]), 1)
    chosen = (place == place_ref[...]).astype(jnp.bfloat16)
    lift = jnp.dot(chosen, lifts_ref[...], preferred_element_type=jnp.float32)
    out_ref[...] = (base_ref[...] + adapter_scale * lift).astype(out_ref.dtype)


def on_device(
    tokens,
    base_projection_weight,
    adapter_down_panels,
    adapter_up_panels,
    request_adapter_ids,
    request_token_lengths,
    adapter_store_slot,
):
    groups = lax.axis_size("grp")
    tp = lax.axis_size("tp")
    width, rank = adapter_down_panels.shape[1:]
    columns = base_projection_weight.shape[1]
    tok_all = tokens.shape[1] * tp
    longest = tok_all // 8
    here = groups * longest
    in_vmem = pl.BlockSpec(memory_space=pltpu.VMEM)
    in_smem = pl.BlockSpec(memory_space=pltpu.SMEM)
    small = pltpu.CompilerParams(vmem_limit_bytes=16 * 2**20)

    panels = swapped(adapter_down_panels[0].T, "grp") + swapped(adapter_up_panels[0], "grp")
    down, up = pl.pallas_call(
        functools.partial(stack_kernel, groups),
        out_shape=[
            jax.ShapeDtypeStruct((width, groups * rank), jnp.bfloat16),
            jax.ShapeDtypeStruct((groups * rank, tp * columns), jnp.bfloat16),
        ],
        in_specs=[in_vmem] * len(panels),
        out_specs=[in_vmem] * 2,
        compiler_params=small,
        name="stack",
    )(*panels)
    row, column = pl.pallas_call(
        functools.partial(place_kernel, groups, tp),
        out_shape=[
            jax.ShapeDtypeStruct((1, tok_all), jnp.int32),
            jax.ShapeDtypeStruct((tok_all, 1), jnp.int32),
        ],
        in_specs=[in_smem] * 3,
        out_specs=[in_vmem] * 2,
        compiler_params=small,
        name="place",
    )(request_adapter_ids, request_token_lengths, adapter_store_slot)
    pieces = ring_gather(tokens[0], "tp", (down, up, row, column))

    gathered, *lifts = pl.pallas_call(
        functools.partial(lift_kernel, groups),
        out_shape=[
            jax.ShapeDtypeStruct((tok_all, width), jnp.bfloat16),
            jax.ShapeDtypeStruct((tp // 2, here, columns), jnp.bfloat16),
            jax.ShapeDtypeStruct((tp // 2, here, columns), jnp.bfloat16),
        ],
        in_specs=[in_vmem] * (3 + len(pieces)),
        out_specs=[in_vmem] * 3,
        compiler_params=pltpu.CompilerParams(vmem_limit_bytes=24 * 2**20),
        cost_estimate=pl.CostEstimate(
            flops=2 * groups * rank * (tok_all * width + here * tp * columns),
            bytes_accessed=2 * groups * rank * (width + tp * columns),
            transcendentals=0,
        ),
        name="lift",
    )(row, down, up, *pieces)
    lifts[1] = lax.ppermute(lifts[1], "tp", [(i, i ^ 1) for i in range(tp)])
    rows = [list(range(row, tp, 2)) for row in range(2)]
    lifts = [
        lax.all_to_all(
            x, "tp", split_axis=0, concat_axis=0, axis_index_groups=rows, tiled=True
        ).reshape(tp // 2 * here, columns)
        for x in lifts
    ]

    base = jnp.dot(gathered, base_projection_weight, preferred_element_type=jnp.float32)
    out = pl.pallas_call(
        add_kernel,
        out_shape=jax.ShapeDtypeStruct((tok_all, columns), jnp.bfloat16),
        in_specs=[in_vmem] * 4,
        out_specs=in_vmem,
        scratch_shapes=[pltpu.VMEM((tp * here, columns), jnp.bfloat16)],
        compiler_params=small,
        name="add",
    )(column, base, *lifts)
    return out[None]


def solution(mesh):
    return jax.shard_map(
        on_device,
        mesh=mesh,
        in_specs=(
            P(("rep", "grp"), "tp", None),
            P(None, "tp"),
            P(("grp", "tp"), None, None),
            P(("grp", "tp"), None, None),
            P("rep", None),
            P(("rep", "grp"), None),
            P(),
        ),
        out_specs=P(("rep", "grp"), None, "tp"),
        check_vma=False,
    )
```

```python
import functools

import jax
import jax.numpy as jnp
from jax import lax
from jax.experimental import pallas as pl
from jax.experimental.pallas import tpu as pltpu
from jax.sharding import PartitionSpec as P

adapter_scale = 1.0


def swapped(x, axis):
    n = lax.axis_size(axis)
    return [x] + [
        lax.ppermute(x, axis, [((i + s) % n, i) for i in range(n)]) for s in range(1, n)
    ]


def ring_of(n):
    return list(range(0, n, 2)) + list(range(1, n, 2))[::-1]


def ring_gather(block, axis, first):
    n = lax.axis_size(axis)
    ring = ring_of(n)
    up = [(ring[i], ring[(i + 1) % n]) for i in range(n)]
    down = [(ring[(i + 1) % n], ring[i]) for i in range(n)]
    half = block.shape[1] // 2
    neighbours = lax.ppermute(block, axis, up), lax.ppermute(block, axis, down)
    cuts = [(0, 0), (1, 0), (0, half), (1, half)]
    streams = handed_on(neighbours, first, cuts, half)
    pieces = [block, *neighbours]
    for step in range(2, n // 2):
        streams = [lax.ppermute(x, axis, way) for x, way in zip(streams, (up, down) * 2)]
        pieces += streams
    return pieces + [lax.ppermute(streams[0], axis, up), lax.ppermute(streams[3], axis, down)]


def pass_kernel(cuts, *refs):
    for (i, start), target in zip(cuts, refs[-len(cuts) :]):
        target[...] = refs[i][:, start : start + target.shape[1]]


def handed_on(arrays, values, cuts, width):
    in_vmem = pl.BlockSpec(memory_space=pltpu.VMEM)
    return pl.pallas_call(
        functools.partial(pass_kernel, cuts),
        out_shape=[jax.ShapeDtypeStruct((arrays[0].shape[0], width), arrays[0].dtype)] * len(cuts),
        in_specs=[in_vmem] * len(arrays) + [pl.BlockSpec(memory_space=pl.ANY)] * len(values),
        out_specs=[in_vmem] * len(cuts),
        compiler_params=pltpu.CompilerParams(vmem_limit_bytes=16 * 2**20),
        name="pass",
    )(*arrays, *values)


def ring_place(i, n):
    return jnp.where(lax.rem(i, 2) == 0, i // 2, n - 1 - i // 2)


def exchange_order(n):
    ring = ring_of(n)
    return ring[n // 2 :] + ring[: n // 2]


def exchange_place(i, n):
    return lax.rem(ring_place(i, n) + n // 2, n)


def ring_sources(axis, half):
    n = lax.axis_size(axis)
    place = ring_place(lax.axis_index(axis), n)
    found = [(0, 0), (1, 0), (-1, 0)]
    for i in range(2, n // 2):
        found += [(i, 0), (-i, 0), (i, half), (-i, half)]
    found += [(n // 2, 0), (n // 2, half)]
    sources = []
    for distance, column in found:
        at = lax.rem(place - distance + n, n)
        sources.append((jnp.where(at < n // 2, 2 * at, 2 * (n - 1 - at) + 1), column))
    return sources


def stack_kernel(groups, *refs):
    downs, ups, (down_ref, up_ref) = refs[:groups], refs[groups:-2], refs[-2:]
    rank = ups[0].shape[0]
    down_ref[...] = jnp.concatenate([down[...] for down in downs], axis=0).T
    for s, up in enumerate(ups):
        up_ref[s * rank : (s + 1) * rank, :] = up[...]


def place_kernel(groups, tp, ids_ref, lengths_ref, slots_ref, row_ref, column_ref):
    group = lax.axis_index("grp")
    longest = row_ref.shape[1] // 8
    along = lax.broadcasted_iota(jnp.int32, row_ref.shape, 1)
    down = lax.broadcasted_iota(jnp.int32, column_ref.shape, 0)

    def add(request, carry):
        start, row, column = carry
        slot = slots_ref[ids_ref[group, request]]
        end = start + lengths_ref[0, request]
        panel = lax.rem(slot // tp - group + groups, groups)
        first = (exchange_place(lax.rem(slot, tp), tp) * groups + panel) * longest - start
        row = jnp.where((along >= start) & (along < end), first + along, row)
        column = jnp.where((down >= start) & (down < end), first + down, column)
        return end, row, column

    carry = (jnp.int32(0), jnp.zeros_like(along), jnp.zeros_like(down))
    _, row_ref[...], column_ref[...] = lax.fori_loop(0, ids_ref.shape[1], add, carry)


def lift_kernel(groups, place_ref, down_ref, up_ref, *refs):
    pieces, (tokens_ref, out_ref, made_ref, sems) = refs[:-4], refs[-4:]
    rank = up_ref.shape[0] // groups
    rows = pieces[0].shape[0]
    tok_all = tokens_ref.shape[0]
    parts, slots, columns = out_ref.shape
    for piece, (source, column) in zip(pieces, ring_sources("tp", pieces[-1].shape[1])):
        start = pl.multiple_of(source * rows, rows)
        tokens_ref[pl.ds(start, rows), column : column + piece.shape[1]] = piece[...]
    low = jnp.dot(tokens_ref[...], down_ref[...], preferred_element_type=jnp.float32)
    place = exchange_place(lax.axis_index("tp"), parts)
    here = lax.broadcasted_iota(jnp.int32, (slots, tok_all), 0) + place * slots
    chosen = (here == place_ref[...]).astype(jnp.bfloat16)
    picked = jnp.dot(chosen, low.astype(jnp.bfloat16), preferred_element_type=jnp.float32)
    row_panel = lax.broadcasted_iota(jnp.int32, picked.shape, 0) // (slots // groups)
    rank_panel = lax.broadcasted_iota(jnp.int32, picked.shape, 1) // rank
    picked = jnp.where(row_panel == rank_panel, picked, 0.0).astype(jnp.bfloat16)
    copies = []
    for part, owner in enumerate(exchange_order(parts)):
        made_ref[part] = jnp.dot(
            picked,
            up_ref[:, owner * columns : (owner + 1) * columns],
            preferred_element_type=jnp.float32,
        ).astype(made_ref.dtype)
        copies.append(
            pltpu.make_async_copy(made_ref.at[part], out_ref.at[part], sems.at[part])
        )
        copies[-1].start()
    for copy in copies:
        copy.wait()


def add_kernel(place_ref, base_ref, lifts_ref, out_ref):
    place = lax.broadcasted_iota(jnp.int32, (base_ref.shape[0], lifts_ref.shape[0]), 1)
    chosen = (place == place_ref[...]).astype(jnp.bfloat16)
    lift = jnp.dot(chosen, lifts_ref[...], preferred_element_type=jnp.float32)
    out_ref[...] = (base_ref[...] + adapter_scale * lift).astype(out_ref.dtype)


def on_device(
    tokens,
    base_projection_weight,
    adapter_down_panels,
    adapter_up_panels,
    request_adapter_ids,
    request_token_lengths,
    adapter_store_slot,
):
    groups = lax.axis_size("grp")
    tp = lax.axis_size("tp")
    width, rank = adapter_down_panels.shape[1:]
    columns = base_projection_weight.shape[1]
    tok_all = tokens.shape[1] * tp
    longest = tok_all // 8
    here = groups * longest
    in_vmem = pl.BlockSpec(memory_space=pltpu.VMEM)
    in_smem = pl.BlockSpec(memory_space=pltpu.SMEM)
    small = pltpu.CompilerParams(vmem_limit_bytes=16 * 2**20)

    panels = swapped(adapter_down_panels[0].T, "grp") + swapped(adapter_up_panels[0], "grp")
    down, up = pl.pallas_call(
        functools.partial(stack_kernel, groups),
        out_shape=[
            jax.ShapeDtypeStruct((width, groups * rank), jnp.bfloat16),
            jax.ShapeDtypeStruct((groups * rank, tp * columns), jnp.bfloat16),
        ],
        in_specs=[in_vmem] * len(panels),
        out_specs=[in_vmem] * 2,
        compiler_params=small,
        name="stack",
    )(*panels)
    row, column = pl.pallas_call(
        functools.partial(place_kernel, groups, tp),
        out_shape=[
            jax.ShapeDtypeStruct((1, tok_all), jnp.int32),
            jax.ShapeDtypeStruct((tok_all, 1), jnp.int32),
        ],
        in_specs=[in_smem] * 3,
        out_specs=[in_vmem] * 2,
        compiler_params=small,
        name="place",
    )(request_adapter_ids, request_token_lengths, adapter_store_slot)
    pieces = ring_gather(tokens[0], "tp", (down, up, row, column))

    gathered, lifts = pl.pallas_call(
        functools.partial(lift_kernel, groups),
        out_shape=[
            jax.ShapeDtypeStruct((tok_all, width), jnp.bfloat16),
            jax.ShapeDtypeStruct((tp, here, columns), jnp.bfloat16),
        ],
        in_specs=[in_vmem] * (3 + len(pieces)),
        out_specs=[in_vmem, pl.BlockSpec(memory_space=pl.ANY)],
        scratch_shapes=[
            pltpu.VMEM((tp, here, columns), jnp.bfloat16),
            pltpu.SemaphoreType.DMA((tp,)),
        ],
        compiler_params=pltpu.CompilerParams(vmem_limit_bytes=24 * 2**20),
        cost_estimate=pl.CostEstimate(
            flops=2 * groups * rank * (tok_all * width + here * tp * columns),
            bytes_accessed=2 * groups * rank * (width + tp * columns),
            transcendentals=0,
        ),
        name="lift",
    )(row, down, up, *pieces)
    lifts = lax.all_to_all(
        lifts, "tp", split_axis=0, concat_axis=0, axis_index_groups=[exchange_order(tp)], tiled=True
    )

    base = jnp.dot(gathered, base_projection_weight, preferred_element_type=jnp.float32)
    out = pl.pallas_call(
        add_kernel,
        out_shape=jax.ShapeDtypeStruct((tok_all, columns), jnp.bfloat16),
        in_specs=[in_vmem] * 3,
        out_specs=in_vmem,
        compiler_params=small,
        name="add",
    )(column, base, lifts.reshape(tp * here, columns))
    return out[None]


def solution(mesh):
    return jax.shard_map(
        on_device,
        mesh=mesh,
        in_specs=(
            P(("rep", "grp"), "tp", None),
            P(None, "tp"),
            P(("grp", "tp"), None, None),
            P(("grp", "tp"), None, None),
            P("rep", None),
            P(("rep", "grp"), None),
            P(),
        ),
        out_specs=P(("rep", "grp"), None, "tp"),
        check_vma=False,
    )
```

```python
import functools

import jax
import jax.numpy as jnp
from jax import lax
from jax.experimental import pallas as pl
from jax.experimental.pallas import tpu as pltpu
from jax.sharding import PartitionSpec as P

adapter_scale = 1.0


def swapped(x, axis):
    n = lax.axis_size(axis)
    return [x] + [
        lax.ppermute(x, axis, [((i + s) % n, i) for i in range(n)]) for s in range(1, n)
    ]


def ring_of(n):
    return list(range(0, n, 2)) + list(range(1, n, 2))[::-1]


def ring_gather(block, axis, first):
    n = lax.axis_size(axis)
    ring = ring_of(n)
    up = [(ring[i], ring[(i + 1) % n]) for i in range(n)]
    down = [(ring[(i + 1) % n], ring[i]) for i in range(n)]
    half = block.shape[1] // 2
    neighbours = lax.ppermute(block, axis, up), lax.ppermute(block, axis, down)
    cuts = [(0, 0), (1, 0), (0, half), (1, half)]
    streams = handed_on(neighbours, first, cuts, half)
    pieces = [block, *neighbours]
    for step in range(2, n // 2):
        streams = [lax.ppermute(x, axis, way) for x, way in zip(streams, (up, down) * 2)]
        pieces += streams
    return pieces + [lax.ppermute(streams[0], axis, up), lax.ppermute(streams[3], axis, down)]


def pass_kernel(cuts, *refs):
    for (i, start), target in zip(cuts, refs[-len(cuts) :]):
        target[...] = refs[i][:, start : start + target.shape[1]]


def handed_on(arrays, values, cuts, width):
    in_vmem = pl.BlockSpec(memory_space=pltpu.VMEM)
    return pl.pallas_call(
        functools.partial(pass_kernel, cuts),
        out_shape=[jax.ShapeDtypeStruct((arrays[0].shape[0], width), arrays[0].dtype)] * len(cuts),
        in_specs=[in_vmem] * len(arrays) + [pl.BlockSpec(memory_space=pl.ANY)] * len(values),
        out_specs=[in_vmem] * len(cuts),
        compiler_params=pltpu.CompilerParams(vmem_limit_bytes=16 * 2**20),
        name="pass",
    )(*arrays, *values)


def ring_place(i, n):
    return jnp.where(lax.rem(i, 2) == 0, i // 2, n - 1 - i // 2)


def exchange_order(n):
    ring = ring_of(n)
    return ring[1:] + ring[:1]


def exchange_place(i, n):
    return lax.rem(ring_place(i, n) + n - 1, n)


def ring_sources(axis, half):
    n = lax.axis_size(axis)
    place = ring_place(lax.axis_index(axis), n)
    found = [(0, 0), (1, 0), (-1, 0)]
    for i in range(2, n // 2):
        found += [(i, 0), (-i, 0), (i, half), (-i, half)]
    found += [(n // 2, 0), (n // 2, half)]
    sources = []
    for distance, column in found:
        at = lax.rem(place - distance + n, n)
        sources.append((jnp.where(at < n // 2, 2 * at, 2 * (n - 1 - at) + 1), column))
    return sources


def stack_kernel(groups, *refs):
    downs, ups, (down_ref, up_ref) = refs[:groups], refs[groups:-2], refs[-2:]
    rank = ups[0].shape[0]
    down_ref[...] = jnp.concatenate([down[...] for down in downs], axis=0).T
    for s, up in enumerate(ups):
        up_ref[s * rank : (s + 1) * rank, :] = up[...]


def place_kernel(groups, tp, segs, lists_ref, row_ref, column_ref):
    group = lax.axis_index("grp")
    longest = row_ref.shape[1] // 8
    along = lax.broadcasted_iota(jnp.int32, row_ref.shape, 1)
    down = lax.broadcasted_iota(jnp.int32, column_ref.shape, 0)

    def add(request, carry):
        start, row, column = carry
        adapter = lists_ref[group * segs + request]
        slot = lists_ref[(groups + 1) * segs + adapter]
        end = start + lists_ref[groups * segs + request]
        panel = lax.rem(slot // tp - group + groups, groups)
        first = (exchange_place(lax.rem(slot, tp), tp) * groups + panel) * longest - start
        row = jnp.where((along >= start) & (along < end), first + along, row)
        column = jnp.where((down >= start) & (down < end), first + down, column)
        return end, row, column

    carry = (jnp.int32(0), jnp.zeros_like(along), jnp.zeros_like(down))
    _, row_ref[...], column_ref[...] = lax.fori_loop(0, segs, add, carry)


def lift_kernel(groups, place_ref, down_ref, up_ref, *refs):
    pieces, (tokens_ref, out_ref, made_ref, sems) = refs[:-4], refs[-4:]
    rank = up_ref.shape[0] // groups
    rows = pieces[0].shape[0]
    tok_all = tokens_ref.shape[0]
    parts, slots, columns = out_ref.shape
    for piece, (source, column) in zip(pieces, ring_sources("tp", pieces[-1].shape[1])):
        start = pl.multiple_of(source * rows, rows)
        tokens_ref[pl.ds(start, rows), column : column + piece.shape[1]] = piece[...]
    low = jnp.dot(tokens_ref[...], down_ref[...], preferred_element_type=jnp.float32)
    place = exchange_place(lax.axis_index("tp"), parts)
    here = lax.broadcasted_iota(jnp.int32, (slots, tok_all), 0) + place * slots
    chosen = (here == place_ref[...]).astype(jnp.bfloat16)
    picked = jnp.dot(chosen, low.astype(jnp.bfloat16), preferred_element_type=jnp.float32)
    row_panel = lax.broadcasted_iota(jnp.int32, picked.shape, 0) // (slots // groups)
    rank_panel = lax.broadcasted_iota(jnp.int32, picked.shape, 1) // rank
    picked = jnp.where(row_panel == rank_panel, picked, 0.0).astype(jnp.bfloat16)
    copies = []
    for part, owner in enumerate(exchange_order(parts)):
        made_ref[part] = jnp.dot(
            picked,
            up_ref[:, owner * columns : (owner + 1) * columns],
            preferred_element_type=jnp.float32,
        ).astype(made_ref.dtype)
        copies.append(
            pltpu.make_async_copy(made_ref.at[part], out_ref.at[part], sems.at[part])
        )
        copies[-1].start()
    for copy in copies:
        copy.wait()


def add_kernel(place_ref, base_ref, lifts_ref, out_ref):
    place = lax.broadcasted_iota(jnp.int32, (base_ref.shape[0], lifts_ref.shape[0]), 1)
    chosen = (place == place_ref[...]).astype(jnp.bfloat16)
    lift = jnp.dot(chosen, lifts_ref[...], preferred_element_type=jnp.float32)
    out_ref[...] = (base_ref[...] + adapter_scale * lift).astype(out_ref.dtype)


def on_device(
    tokens,
    base_projection_weight,
    adapter_down_panels,
    adapter_up_panels,
    request_adapter_ids,
    request_token_lengths,
    adapter_store_slot,
):
    groups = lax.axis_size("grp")
    tp = lax.axis_size("tp")
    width, rank = adapter_down_panels.shape[1:]
    columns = base_projection_weight.shape[1]
    tok_all = tokens.shape[1] * tp
    longest = tok_all // 8
    here = groups * longest
    in_vmem = pl.BlockSpec(memory_space=pltpu.VMEM)
    in_smem = pl.BlockSpec(memory_space=pltpu.SMEM)
    small = pltpu.CompilerParams(vmem_limit_bytes=16 * 2**20)

    panels = swapped(adapter_down_panels[0].T, "grp") + swapped(adapter_up_panels[0], "grp")
    down, up = pl.pallas_call(
        functools.partial(stack_kernel, groups),
        out_shape=[
            jax.ShapeDtypeStruct((width, groups * rank), jnp.bfloat16),
            jax.ShapeDtypeStruct((groups * rank, tp * columns), jnp.bfloat16),
        ],
        in_specs=[in_vmem] * len(panels),
        out_specs=[in_vmem] * 2,
        compiler_params=small,
        name="stack",
    )(*panels)
    lists = jnp.concatenate(
        [request_adapter_ids.reshape(-1), request_token_lengths.reshape(-1), adapter_store_slot]
    )
    row, column = pl.pallas_call(
        functools.partial(place_kernel, groups, tp, request_adapter_ids.shape[1]),
        out_shape=[
            jax.ShapeDtypeStruct((1, tok_all), jnp.int32),
            jax.ShapeDtypeStruct((tok_all, 1), jnp.int32),
        ],
        in_specs=[in_smem],
        out_specs=[in_vmem] * 2,
        compiler_params=small,
        name="place",
    )(lists)
    pieces = ring_gather(tokens[0], "tp", (down, up, row, column))

    gathered, lifts = pl.pallas_call(
        functools.partial(lift_kernel, groups),
        out_shape=[
            jax.ShapeDtypeStruct((tok_all, width), jnp.bfloat16),
            jax.ShapeDtypeStruct((tp, here, columns), jnp.bfloat16),
        ],
        in_specs=[in_vmem] * (3 + len(pieces)),
        out_specs=[in_vmem, pl.BlockSpec(memory_space=pl.ANY)],
        scratch_shapes=[
            pltpu.VMEM((tp, here, columns), jnp.bfloat16),
            pltpu.SemaphoreType.DMA((tp,)),
        ],
        compiler_params=pltpu.CompilerParams(vmem_limit_bytes=24 * 2**20),
        cost_estimate=pl.CostEstimate(
            flops=2 * groups * rank * (tok_all * width + here * tp * columns),
            bytes_accessed=2 * groups * rank * (width + tp * columns),
            transcendentals=0,
        ),
        name="lift",
    )(row, down, up, *pieces)
    lifts = lax.all_to_all(
        lifts, "tp", split_axis=0, concat_axis=0, axis_index_groups=[exchange_order(tp)], tiled=True
    )

    base = jnp.dot(gathered, base_projection_weight, preferred_element_type=jnp.float32)
    out = pl.pallas_call(
        add_kernel,
        out_shape=jax.ShapeDtypeStruct((tok_all, columns), jnp.bfloat16),
        in_specs=[in_vmem] * 3,
        out_specs=in_vmem,
        compiler_params=small,
        name="add",
    )(column, base, lifts.reshape(tp * here, columns))
    return out[None]


def solution(mesh):
    return jax.shard_map(
        on_device,
        mesh=mesh,
        in_specs=(
            P(("rep", "grp"), "tp", None),
            P(None, "tp"),
            P(("grp", "tp"), None, None),
            P(("grp", "tp"), None, None),
            P("rep", None),
            P(("rep", "grp"), None),
            P(),
        ),
        out_specs=P(("rep", "grp"), None, "tp"),
        check_vma=False,
    )
```

```python
import functools

import jax
import jax.numpy as jnp
from jax import lax
from jax.experimental import pallas as pl
from jax.experimental.pallas import tpu as pltpu
from jax.sharding import PartitionSpec as P

adapter_scale = 1.0


def swapped(x, axis):
    n = lax.axis_size(axis)
    return [x] + [
        lax.ppermute(x, axis, [((i + s) % n, i) for i in range(n)]) for s in range(1, n)
    ]


def ring_of(n):
    return list(range(0, n, 2)) + list(range(1, n, 2))[::-1]


def ring_gather(block, axis, first):
    n = lax.axis_size(axis)
    ring = ring_of(n)
    up = [(ring[i], ring[(i + 1) % n]) for i in range(n)]
    down = [(ring[(i + 1) % n], ring[i]) for i in range(n)]
    half = block.shape[1] // 2
    neighbours = lax.ppermute(block, axis, up), lax.ppermute(block, axis, down)
    cuts = [(0, 0), (1, 0), (0, half), (1, half)]
    streams = handed_on(neighbours, first, cuts, half)
    pieces = [block, *neighbours]
    for step in range(2, n // 2):
        streams = [lax.ppermute(x, axis, way) for x, way in zip(streams, (up, down) * 2)]
        pieces += streams
    return pieces + [lax.ppermute(streams[0], axis, up), lax.ppermute(streams[3], axis, down)]


def pass_kernel(cuts, *refs):
    for (i, start), target in zip(cuts, refs[-len(cuts) :]):
        target[...] = refs[i][:, start : start + target.shape[1]]


def handed_on(arrays, values, cuts, width):
    in_vmem = pl.BlockSpec(memory_space=pltpu.VMEM)
    return pl.pallas_call(
        functools.partial(pass_kernel, cuts),
        out_shape=[jax.ShapeDtypeStruct((arrays[0].shape[0], width), arrays[0].dtype)] * len(cuts),
        in_specs=[in_vmem] * len(arrays) + [pl.BlockSpec(memory_space=pl.ANY)] * len(values),
        out_specs=[in_vmem] * len(cuts),
        compiler_params=pltpu.CompilerParams(vmem_limit_bytes=16 * 2**20),
        name="pass",
    )(*arrays, *values)


def ring_place(i, n):
    return jnp.where(lax.rem(i, 2) == 0, i // 2, n - 1 - i // 2)


def exchange_order(n):
    ring = ring_of(n)
    return ring[1:] + ring[:1]


def exchange_place(i, n):
    return lax.rem(ring_place(i, n) + n - 1, n)


def ring_sources(axis, half):
    n = lax.axis_size(axis)
    place = ring_place(lax.axis_index(axis), n)
    found = [(0, 0), (1, 0), (-1, 0)]
    for i in range(2, n // 2):
        found += [(i, 0), (-i, 0), (i, half), (-i, half)]
    found += [(n // 2, 0), (n // 2, half)]
    sources = []
    for distance, column in found:
        at = lax.rem(place - distance + n, n)
        sources.append((jnp.where(at < n // 2, 2 * at, 2 * (n - 1 - at) + 1), column))
    return sources


def stack_kernel(groups, *refs):
    downs, ups, (down_ref, up_ref) = refs[:groups], refs[groups:-2], refs[-2:]
    rank = ups[0].shape[0]
    down_ref[...] = jnp.concatenate([down[...] for down in downs], axis=0).T
    for s, up in enumerate(ups):
        up_ref[s * rank : (s + 1) * rank, :] = up[...]


def place_kernel(groups, tp, ids_ref, lengths_ref, slots_ref, row_ref, column_ref):
    group = lax.axis_index("grp")
    longest = row_ref.shape[1] // 8
    along = lax.broadcasted_iota(jnp.int32, row_ref.shape, 1)
    down = lax.broadcasted_iota(jnp.int32, column_ref.shape, 0)

    def add(request, carry):
        start, row, column = carry
        slot = slots_ref[ids_ref[group, request]]
        end = start + lengths_ref[0, request]
        panel = lax.rem(slot // tp - group + groups, groups)
        first = (exchange_place(lax.rem(slot, tp), tp) * groups + panel) * longest - start
        row = jnp.where((along >= start) & (along < end), first + along, row)
        column = jnp.where((down >= start) & (down < end), first + down, column)
        return end, row, column

    carry = (jnp.int32(0), jnp.zeros_like(along), jnp.zeros_like(down))
    _, row_ref[...], column_ref[...] = lax.fori_loop(0, ids_ref.shape[1], add, carry)


def lift_kernel(groups, place_ref, down_ref, up_ref, *refs):
    pieces, (tokens_ref, out_ref, made_ref, sems) = refs[:-4], refs[-4:]
    rank = up_ref.shape[0] // groups
    rows = pieces[0].shape[0]
    tok_all = tokens_ref.shape[0]
    parts, slots, columns = out_ref.shape
    for piece, (source, column) in zip(pieces, ring_sources("tp", pieces[-1].shape[1])):
        start = pl.multiple_of(source * rows, rows)
        tokens_ref[pl.ds(start, rows), column : column + piece.shape[1]] = piece[...]
    low = jnp.dot(tokens_ref[...], down_ref[...], preferred_element_type=jnp.float32)
    place = exchange_place(lax.axis_index("tp"), parts)
    here = lax.broadcasted_iota(jnp.int32, (slots, tok_all), 0) + place * slots
    chosen = (here == place_ref[...]).astype(jnp.bfloat16)
    picked = jnp.dot(chosen, low.astype(jnp.bfloat16), preferred_element_type=jnp.float32)
    row_panel = lax.broadcasted_iota(jnp.int32, picked.shape, 0) // (slots // groups)
    rank_panel = lax.broadcasted_iota(jnp.int32, picked.shape, 1) // rank
    picked = jnp.where(row_panel == rank_panel, picked, 0.0).astype(jnp.bfloat16)
    copies = []
    for part, owner in enumerate(exchange_order(parts)):
        made_ref[part] = jnp.dot(
            picked,
            up_ref[:, owner * columns : (owner + 1) * columns],
            preferred_element_type=jnp.float32,
        ).astype(made_ref.dtype)
        copies.append(
            pltpu.make_async_copy(made_ref.at[part], out_ref.at[part], sems.at[part])
        )
        copies[-1].start()
    for copy in copies:
        copy.wait()


def add_kernel(place_ref, base_ref, lifts_ref, out_ref):
    place = lax.broadcasted_iota(jnp.int32, (base_ref.shape[0], lifts_ref.shape[0]), 1)
    chosen = (place == place_ref[...]).astype(jnp.bfloat16)
    lift = jnp.dot(chosen, lifts_ref[...], preferred_element_type=jnp.float32)
    out_ref[...] = (base_ref[...] + adapter_scale * lift).astype(out_ref.dtype)


def on_device(
    tokens,
    base_projection_weight,
    adapter_down_panels,
    adapter_up_panels,
    request_adapter_ids,
    request_token_lengths,
    adapter_store_slot,
):
    groups = lax.axis_size("grp")
    tp = lax.axis_size("tp")
    width, rank = adapter_down_panels.shape[1:]
    columns = base_projection_weight.shape[1]
    tok_all = tokens.shape[1] * tp
    longest = tok_all // 8
    here = groups * longest
    in_vmem = pl.BlockSpec(memory_space=pltpu.VMEM)
    in_smem = pl.BlockSpec(memory_space=pltpu.SMEM)
    small = pltpu.CompilerParams(vmem_limit_bytes=16 * 2**20)

    panels = swapped(adapter_down_panels[0].T, "grp") + swapped(adapter_up_panels[0], "grp")
    down, up = pl.pallas_call(
        functools.partial(stack_kernel, groups),
        out_shape=[
            jax.ShapeDtypeStruct((width, groups * rank), jnp.bfloat16),
            jax.ShapeDtypeStruct((groups * rank, tp * columns), jnp.bfloat16),
        ],
        in_specs=[in_vmem] * len(panels),
        out_specs=[in_vmem] * 2,
        compiler_params=small,
        name="stack",
    )(*panels)
    row, column = pl.pallas_call(
        functools.partial(place_kernel, groups, tp),
        out_shape=[
            jax.ShapeDtypeStruct((1, tok_all), jnp.int32),
            jax.ShapeDtypeStruct((tok_all, 1), jnp.int32),
        ],
        in_specs=[in_smem] * 3,
        out_specs=[in_vmem] * 2,
        compiler_params=small,
        name="place",
    )(request_adapter_ids, request_token_lengths, adapter_store_slot)
    pieces = ring_gather(tokens[0], "tp", (down, up, row, column))

    gathered, lifts = pl.pallas_call(
        functools.partial(lift_kernel, groups),
        out_shape=[
            jax.ShapeDtypeStruct((tok_all, width), jnp.bfloat16),
            jax.ShapeDtypeStruct((tp, here, columns), jnp.bfloat16),
        ],
        in_specs=[in_vmem] * (3 + len(pieces)),
        out_specs=[in_vmem, pl.BlockSpec(memory_space=pl.ANY)],
        scratch_shapes=[
            pltpu.VMEM((tp, here, columns), jnp.bfloat16),
            pltpu.SemaphoreType.DMA((tp,)),
        ],
        compiler_params=pltpu.CompilerParams(vmem_limit_bytes=24 * 2**20),
        cost_estimate=pl.CostEstimate(
            flops=2 * groups * rank * (tok_all * width + here * tp * columns),
            bytes_accessed=2 * groups * rank * (width + tp * columns),
            transcendentals=0,
        ),
        name="lift",
    )(row, down, up, *pieces)
    lifts = lax.all_to_all(
        lifts, "tp", split_axis=0, concat_axis=0, axis_index_groups=[exchange_order(tp)], tiled=True
    )

    base = jnp.dot(gathered, base_projection_weight, preferred_element_type=jnp.float32)
    out = pl.pallas_call(
        add_kernel,
        out_shape=jax.ShapeDtypeStruct((tok_all, columns), jnp.bfloat16),
        in_specs=[in_vmem] * 3,
        out_specs=in_vmem,
        compiler_params=small,
        name="add",
    )(column, base, lifts.reshape(tp * here, columns))
    return out[None]


def solution(mesh):
    return jax.shard_map(
        on_device,
        mesh=mesh,
        in_specs=(
            P(("rep", "grp"), "tp", None),
            P(None, "tp"),
            P(("grp", "tp"), None, None),
            P(("grp", "tp"), None, None),
            P("rep", None),
            P(("rep", "grp"), None),
            P(),
        ),
        out_specs=P(("rep", "grp"), None, "tp"),
        check_vma=False,
    )
```

```python
import functools

import jax
import jax.numpy as jnp
from jax import lax
from jax.experimental import pallas as pl
from jax.experimental.pallas import tpu as pltpu
from jax.sharding import PartitionSpec as P

adapter_scale = 1.0


def swapped(x, axis):
    n = lax.axis_size(axis)
    return [x] + [
        lax.ppermute(x, axis, [((i + s) % n, i) for i in range(n)]) for s in range(1, n)
    ]


def ring_of(n):
    return list(range(0, n, 2)) + list(range(1, n, 2))[::-1]


def ring_gather(block, axis, first):
    n = lax.axis_size(axis)
    ring = ring_of(n)
    up = [(ring[i], ring[(i + 1) % n]) for i in range(n)]
    down = [(ring[(i + 1) % n], ring[i]) for i in range(n)]
    half = block.shape[1] // 2
    neighbours = lax.ppermute(block, axis, up), lax.ppermute(block, axis, down)
    cuts = [(0, 0), (1, 0), (0, half), (1, half)]
    streams = handed_on(neighbours, first, cuts, half)
    pieces = [block, *neighbours]
    for step in range(2, n // 2):
        streams = [lax.ppermute(x, axis, way) for x, way in zip(streams, (up, down) * 2)]
        pieces += streams
    return pieces + [lax.ppermute(streams[0], axis, up), lax.ppermute(streams[3], axis, down)]


def pass_kernel(cuts, *refs):
    for (i, start), target in zip(cuts, refs[-len(cuts) :]):
        target[...] = refs[i][:, start : start + target.shape[1]]


def handed_on(arrays, values, cuts, width):
    in_vmem = pl.BlockSpec(memory_space=pltpu.VMEM)
    return pl.pallas_call(
        functools.partial(pass_kernel, cuts),
        out_shape=[jax.ShapeDtypeStruct((arrays[0].shape[0], width), arrays[0].dtype)] * len(cuts),
        in_specs=[in_vmem] * len(arrays) + [pl.BlockSpec(memory_space=pl.ANY)] * len(values),
        out_specs=[in_vmem] * len(cuts),
        compiler_params=pltpu.CompilerParams(vmem_limit_bytes=16 * 2**20),
        name="pass",
    )(*arrays, *values)


def ring_place(i, n):
    return jnp.where(lax.rem(i, 2) == 0, i // 2, n - 1 - i // 2)


def exchange_order(n):
    ring = ring_of(n)
    return ring[1:] + ring[:1]


def exchange_place(i, n):
    return lax.rem(ring_place(i, n) + n - 1, n)


def ring_sources(axis, half):
    n = lax.axis_size(axis)
    place = ring_place(lax.axis_index(axis), n)
    found = [(0, 0), (1, 0), (-1, 0)]
    for i in range(2, n // 2):
        found += [(i, 0), (-i, 0), (i, half), (-i, half)]
    found += [(n // 2, 0), (n // 2, half)]
    sources = []
    for distance, column in found:
        at = lax.rem(place - distance + n, n)
        sources.append((jnp.where(at < n // 2, 2 * at, 2 * (n - 1 - at) + 1), column))
    return sources


def prepare_kernel(groups, tp, ids_ref, lengths_ref, slots_ref, *refs):
    downs, ups = refs[:groups], refs[groups:-4]
    down_ref, up_ref, row_ref, column_ref = refs[-4:]
    rank = ups[0].shape[0]
    down_ref[...] = jnp.concatenate([down[...] for down in downs], axis=0).T
    for s, up in enumerate(ups):
        up_ref[s * rank : (s + 1) * rank, :] = up[...]
    group = lax.axis_index("grp")
    longest = row_ref.shape[1] // 8
    along = lax.broadcasted_iota(jnp.int32, row_ref.shape, 1)
    down = lax.broadcasted_iota(jnp.int32, column_ref.shape, 0)

    def add(request, carry):
        start, row, column = carry
        slot = slots_ref[ids_ref[group, request]]
        end = start + lengths_ref[0, request]
        panel = lax.rem(slot // tp - group + groups, groups)
        first = (exchange_place(lax.rem(slot, tp), tp) * groups + panel) * longest - start
        row = jnp.where((along >= start) & (along < end), first + along, row)
        column = jnp.where((down >= start) & (down < end), first + down, column)
        return end, row, column

    carry = (jnp.int32(0), jnp.zeros_like(along), jnp.zeros_like(down))
    _, row_ref[...], column_ref[...] = lax.fori_loop(0, ids_ref.shape[1], add, carry)


def lift_kernel(groups, place_ref, down_ref, up_ref, *refs):
    pieces, (tokens_ref, out_ref, made_ref, sems) = refs[:-4], refs[-4:]
    rank = up_ref.shape[0] // groups
    rows = pieces[0].shape[0]
    tok_all = tokens_ref.shape[0]
    parts, slots, columns = out_ref.shape
    for piece, (source, column) in zip(pieces, ring_sources("tp", pieces[-1].shape[1])):
        start = pl.multiple_of(source * rows, rows)
        tokens_ref[pl.ds(start, rows), column : column + piece.shape[1]] = piece[...]
    low = jnp.dot(tokens_ref[...], down_ref[...], preferred_element_type=jnp.float32)
    place = exchange_place(lax.axis_index("tp"), parts)
    here = lax.broadcasted_iota(jnp.int32, (slots, tok_all), 0) + place * slots
    chosen = (here == place_ref[...]).astype(jnp.bfloat16)
    picked = jnp.dot(chosen, low.astype(jnp.bfloat16), preferred_element_type=jnp.float32)
    row_panel = lax.broadcasted_iota(jnp.int32, picked.shape, 0) // (slots // groups)
    rank_panel = lax.broadcasted_iota(jnp.int32, picked.shape, 1) // rank
    picked = jnp.where(row_panel == rank_panel, picked, 0.0).astype(jnp.bfloat16)
    copies = []
    for part, owner in enumerate(exchange_order(parts)):
        made_ref[part] = jnp.dot(
            picked,
            up_ref[:, owner * columns : (owner + 1) * columns],
            preferred_element_type=jnp.float32,
        ).astype(made_ref.dtype)
        copies.append(
            pltpu.make_async_copy(made_ref.at[part], out_ref.at[part], sems.at[part])
        )
        copies[-1].start()
    for copy in copies:
        copy.wait()


def add_kernel(place_ref, base_ref, lifts_ref, out_ref, made_ref, sems):
    place = lax.broadcasted_iota(jnp.int32, (base_ref.shape[0], lifts_ref.shape[0]), 1)
    chosen = (place == place_ref[...]).astype(jnp.bfloat16)
    size = base_ref.shape[1] // sems.shape[0]
    copies = []
    for i in range(sems.shape[0]):
        part = pl.ds(i * size, size)
        lift = jnp.dot(chosen, lifts_ref[:, part], preferred_element_type=jnp.float32)
        made_ref[:, part] = (base_ref[:, part] + adapter_scale * lift).astype(made_ref.dtype)
        copies.append(
            pltpu.make_async_copy(made_ref.at[:, part], out_ref.at[:, part], sems.at[i])
        )
        copies[-1].start()
    for copy in copies:
        copy.wait()


def on_device(
    tokens,
    base_projection_weight,
    adapter_down_panels,
    adapter_up_panels,
    request_adapter_ids,
    request_token_lengths,
    adapter_store_slot,
):
    groups = lax.axis_size("grp")
    tp = lax.axis_size("tp")
    width, rank = adapter_down_panels.shape[1:]
    columns = base_projection_weight.shape[1]
    tok_all = tokens.shape[1] * tp
    longest = tok_all // 8
    here = groups * longest
    in_vmem = pl.BlockSpec(memory_space=pltpu.VMEM)
    in_smem = pl.BlockSpec(memory_space=pltpu.SMEM)
    small = pltpu.CompilerParams(vmem_limit_bytes=16 * 2**20)

    panels = swapped(adapter_down_panels[0].T, "grp") + swapped(adapter_up_panels[0], "grp")
    down, up, row, column = pl.pallas_call(
        functools.partial(prepare_kernel, groups, tp),
        out_shape=[
            jax.ShapeDtypeStruct((width, groups * rank), jnp.bfloat16),
            jax.ShapeDtypeStruct((groups * rank, tp * columns), jnp.bfloat16),
            jax.ShapeDtypeStruct((1, tok_all), jnp.int32),
            jax.ShapeDtypeStruct((tok_all, 1), jnp.int32),
        ],
        in_specs=[in_smem] * 3 + [in_vmem] * len(panels),
        out_specs=[in_vmem] * 4,
        compiler_params=small,
        name="prepare",
    )(request_adapter_ids, request_token_lengths, adapter_store_slot, *panels)
    pieces = ring_gather(tokens[0], "tp", (down, up, row, column))

    gathered, lifts = pl.pallas_call(
        functools.partial(lift_kernel, groups),
        out_shape=[
            jax.ShapeDtypeStruct((tok_all, width), jnp.bfloat16),
            jax.ShapeDtypeStruct((tp, here, columns), jnp.bfloat16),
        ],
        in_specs=[in_vmem] * (3 + len(pieces)),
        out_specs=[in_vmem, pl.BlockSpec(memory_space=pl.ANY)],
        scratch_shapes=[
            pltpu.VMEM((tp, here, columns), jnp.bfloat16),
            pltpu.SemaphoreType.DMA((tp,)),
        ],
        compiler_params=pltpu.CompilerParams(vmem_limit_bytes=24 * 2**20),
        cost_estimate=pl.CostEstimate(
            flops=2 * groups * rank * (tok_all * width + here * tp * columns),
            bytes_accessed=2 * groups * rank * (width + tp * columns),
            transcendentals=0,
        ),
        name="lift",
    )(row, down, up, *pieces)
    lifts = lax.all_to_all(
        lifts, "tp", split_axis=0, concat_axis=0, axis_index_groups=[exchange_order(tp)], tiled=True
    )

    base = jnp.dot(gathered, base_projection_weight, preferred_element_type=jnp.float32)
    out = pl.pallas_call(
        add_kernel,
        out_shape=jax.ShapeDtypeStruct((tok_all, columns), jnp.bfloat16),
        in_specs=[in_vmem] * 3,
        out_specs=pl.BlockSpec(memory_space=pl.ANY),
        scratch_shapes=[
            pltpu.VMEM((tok_all, columns), jnp.bfloat16),
            pltpu.SemaphoreType.DMA((columns // 256 if columns % 256 == 0 else 1,)),
        ],
        compiler_params=small,
        name="add",
    )(column, base, lifts.reshape(tp * here, columns))
    return out[None]


def solution(mesh):
    return jax.shard_map(
        on_device,
        mesh=mesh,
        in_specs=(
            P(("rep", "grp"), "tp", None),
            P(None, "tp"),
            P(("grp", "tp"), None, None),
            P(("grp", "tp"), None, None),
            P("rep", None),
            P(("rep", "grp"), None),
            P(),
        ),
        out_specs=P(("rep", "grp"), None, "tp"),
        check_vma=False,
    )
```

```python
import functools

import jax
import jax.numpy as jnp
from jax import lax
from jax.experimental import pallas as pl
from jax.experimental.pallas import tpu as pltpu
from jax.sharding import PartitionSpec as P

adapter_scale = 1.0


def swapped(x, axis):
    n = lax.axis_size(axis)
    return [x] + [
        lax.ppermute(x, axis, [((i + s) % n, i) for i in range(n)]) for s in range(1, n)
    ]


def ring_of(n):
    return list(range(0, n, 2)) + list(range(1, n, 2))[::-1]


def ring_gather(block, axis, first):
    n = lax.axis_size(axis)
    ring = ring_of(n)
    up = [(ring[i], ring[(i + 1) % n]) for i in range(n)]
    down = [(ring[(i + 1) % n], ring[i]) for i in range(n)]
    half = block.shape[1] // 2
    neighbours = lax.ppermute(block, axis, up), lax.ppermute(block, axis, down)
    cuts = [(0, 0), (1, 0), (0, half), (1, half)]
    streams = handed_on(neighbours, first, cuts, half)
    pieces = [block, *neighbours]
    for step in range(2, n // 2):
        streams = [lax.ppermute(x, axis, way) for x, way in zip(streams, (up, down) * 2)]
        pieces += streams
    return pieces + [lax.ppermute(streams[0], axis, up), lax.ppermute(streams[3], axis, down)]


def pass_kernel(cuts, *refs):
    for (i, start), target in zip(cuts, refs[-len(cuts) :]):
        target[...] = refs[i][:, start : start + target.shape[1]]


def handed_on(arrays, values, cuts, width):
    in_vmem = pl.BlockSpec(memory_space=pltpu.VMEM)
    return pl.pallas_call(
        functools.partial(pass_kernel, cuts),
        out_shape=[jax.ShapeDtypeStruct((arrays[0].shape[0], width), arrays[0].dtype)] * len(cuts),
        in_specs=[in_vmem] * len(arrays) + [pl.BlockSpec(memory_space=pl.ANY)] * len(values),
        out_specs=[in_vmem] * len(cuts),
        compiler_params=pltpu.CompilerParams(vmem_limit_bytes=16 * 2**20),
        name="pass",
    )(*arrays, *values)


def ring_place(i, n):
    return jnp.where(lax.rem(i, 2) == 0, i // 2, n - 1 - i // 2)


def exchange_order(n):
    rows = list(range(0, n, 2)) + list(range(1, n, 2))
    return rows[1:] + rows[:1]


def exchange_place(i, n):
    return lax.rem(i // 2 + lax.rem(i, 2) * (n // 2) + n - 1, n)


def ring_sources(axis, half):
    n = lax.axis_size(axis)
    place = ring_place(lax.axis_index(axis), n)
    found = [(0, 0), (1, 0), (-1, 0)]
    for i in range(2, n // 2):
        found += [(i, 0), (-i, 0), (i, half), (-i, half)]
    found += [(n // 2, 0), (n // 2, half)]
    sources = []
    for distance, column in found:
        at = lax.rem(place - distance + n, n)
        sources.append((jnp.where(at < n // 2, 2 * at, 2 * (n - 1 - at) + 1), column))
    return sources


def stack_kernel(groups, *refs):
    downs, ups, (down_ref, up_ref) = refs[:groups], refs[groups:-2], refs[-2:]
    rank = ups[0].shape[0]
    down_ref[...] = jnp.concatenate([down[...] for down in downs], axis=0).T
    for s, up in enumerate(ups):
        up_ref[s * rank : (s + 1) * rank, :] = up[...]


def place_kernel(groups, tp, ids_ref, lengths_ref, slots_ref, row_ref, column_ref):
    group = lax.axis_index("grp")
    longest = row_ref.shape[1] // 8
    along = lax.broadcasted_iota(jnp.int32, row_ref.shape, 1)
    down = lax.broadcasted_iota(jnp.int32, column_ref.shape, 0)

    def add(request, carry):
        start, row, column = carry
        slot = slots_ref[ids_ref[group, request]]
        end = start + lengths_ref[0, request]
        panel = lax.rem(slot // tp - group + groups, groups)
        first = (exchange_place(lax.rem(slot, tp), tp) * groups + panel) * longest - start
        row = jnp.where((along >= start) & (along < end), first + along, row)
        column = jnp.where((down >= start) & (down < end), first + down, column)
        return end, row, column

    carry = (jnp.int32(0), jnp.zeros_like(along), jnp.zeros_like(down))
    _, row_ref[...], column_ref[...] = lax.fori_loop(0, ids_ref.shape[1], add, carry)


def lift_kernel(groups, place_ref, down_ref, up_ref, *refs):
    pieces, (tokens_ref, out_ref, made_ref, sems) = refs[:-4], refs[-4:]
    rank = up_ref.shape[0] // groups
    rows = pieces[0].shape[0]
    tok_all = tokens_ref.shape[0]
    parts, slots, columns = out_ref.shape
    for piece, (source, column) in zip(pieces, ring_sources("tp", pieces[-1].shape[1])):
        start = pl.multiple_of(source * rows, rows)
        tokens_ref[pl.ds(start, rows), column : column + piece.shape[1]] = piece[...]
    low = jnp.dot(tokens_ref[...], down_ref[...], preferred_element_type=jnp.float32)
    place = exchange_place(lax.axis_index("tp"), parts)
    here = lax.broadcasted_iota(jnp.int32, (slots, tok_all), 0) + place * slots
    chosen = (here == place_ref[...]).astype(jnp.bfloat16)
    picked = jnp.dot(chosen, low.astype(jnp.bfloat16), preferred_element_type=jnp.float32)
    row_panel = lax.broadcasted_iota(jnp.int32, picked.shape, 0) // (slots // groups)
    rank_panel = lax.broadcasted_iota(jnp.int32, picked.shape, 1) // rank
    picked = jnp.where(row_panel == rank_panel, picked, 0.0).astype(jnp.bfloat16)
    copies = []
    for part, owner in enumerate(exchange_order(parts)):
        made_ref[part] = jnp.dot(
            picked,
            up_ref[:, owner * columns : (owner + 1) * columns],
            preferred_element_type=jnp.float32,
        ).astype(made_ref.dtype)
        copies.append(
            pltpu.make_async_copy(made_ref.at[part], out_ref.at[part], sems.at[part])
        )
        copies[-1].start()
    for copy in copies:
        copy.wait()


def add_kernel(place_ref, base_ref, lifts_ref, out_ref):
    place = lax.broadcasted_iota(jnp.int32, (base_ref.shape[0], lifts_ref.shape[0]), 1)
    chosen = (place == place_ref[...]).astype(jnp.bfloat16)
    lift = jnp.dot(chosen, lifts_ref[...], preferred_element_type=jnp.float32)
    out_ref[...] = (base_ref[...] + adapter_scale * lift).astype(out_ref.dtype)


def on_device(
    tokens,
    base_projection_weight,
    adapter_down_panels,
    adapter_up_panels,
    request_adapter_ids,
    request_token_lengths,
    adapter_store_slot,
):
    groups = lax.axis_size("grp")
    tp = lax.axis_size("tp")
    width, rank = adapter_down_panels.shape[1:]
    columns = base_projection_weight.shape[1]
    tok_all = tokens.shape[1] * tp
    longest = tok_all // 8
    here = groups * longest
    in_vmem = pl.BlockSpec(memory_space=pltpu.VMEM)
    in_smem = pl.BlockSpec(memory_space=pltpu.SMEM)
    small = pltpu.CompilerParams(vmem_limit_bytes=16 * 2**20)

    panels = swapped(adapter_down_panels[0].T, "grp") + swapped(adapter_up_panels[0], "grp")
    down, up = pl.pallas_call(
        functools.partial(stack_kernel, groups),
        out_shape=[
            jax.ShapeDtypeStruct((width, groups * rank), jnp.bfloat16),
            jax.ShapeDtypeStruct((groups * rank, tp * columns), jnp.bfloat16),
        ],
        in_specs=[in_vmem] * len(panels),
        out_specs=[in_vmem] * 2,
        compiler_params=small,
        name="stack",
    )(*panels)
    row, column = pl.pallas_call(
        functools.partial(place_kernel, groups, tp),
        out_shape=[
            jax.ShapeDtypeStruct((1, tok_all), jnp.int32),
            jax.ShapeDtypeStruct((tok_all, 1), jnp.int32),
        ],
        in_specs=[in_smem] * 3,
        out_specs=[in_vmem] * 2,
        compiler_params=small,
        name="place",
    )(request_adapter_ids, request_token_lengths, adapter_store_slot)
    pieces = ring_gather(tokens[0], "tp", (down, up, row, column))

    gathered, lifts = pl.pallas_call(
        functools.partial(lift_kernel, groups),
        out_shape=[
            jax.ShapeDtypeStruct((tok_all, width), jnp.bfloat16),
            jax.ShapeDtypeStruct((tp, here, columns), jnp.bfloat16),
        ],
        in_specs=[in_vmem] * (3 + len(pieces)),
        out_specs=[in_vmem, pl.BlockSpec(memory_space=pl.ANY)],
        scratch_shapes=[
            pltpu.VMEM((tp, here, columns), jnp.bfloat16),
            pltpu.SemaphoreType.DMA((tp,)),
        ],
        compiler_params=pltpu.CompilerParams(vmem_limit_bytes=24 * 2**20),
        cost_estimate=pl.CostEstimate(
            flops=2 * groups * rank * (tok_all * width + here * tp * columns),
            bytes_accessed=2 * groups * rank * (width + tp * columns),
            transcendentals=0,
        ),
        name="lift",
    )(row, down, up, *pieces)
    lifts = lax.all_to_all(
        lifts, "tp", split_axis=0, concat_axis=0, axis_index_groups=[exchange_order(tp)], tiled=True
    )

    base = jnp.dot(gathered, base_projection_weight, preferred_element_type=jnp.float32)
    out = pl.pallas_call(
        add_kernel,
        out_shape=jax.ShapeDtypeStruct((tok_all, columns), jnp.bfloat16),
        in_specs=[in_vmem] * 3,
        out_specs=in_vmem,
        compiler_params=small,
        name="add",
    )(column, base, lifts.reshape(tp * here, columns))
    return out[None]


def solution(mesh):
    return jax.shard_map(
        on_device,
        mesh=mesh,
        in_specs=(
            P(("rep", "grp"), "tp", None),
            P(None, "tp"),
            P(("grp", "tp"), None, None),
            P(("grp", "tp"), None, None),
            P("rep", None),
            P(("rep", "grp"), None),
            P(),
        ),
        out_specs=P(("rep", "grp"), None, "tp"),
        check_vma=False,
    )
```

```python
import functools

import jax
import jax.numpy as jnp
from jax import lax
from jax.experimental import pallas as pl
from jax.experimental.pallas import tpu as pltpu
from jax.sharding import PartitionSpec as P

adapter_scale = 1.0


def swapped(x, axis):
    n = lax.axis_size(axis)
    return [x] + [
        lax.ppermute(x, axis, [((i + s) % n, i) for i in range(n)]) for s in range(1, n)
    ]


def ring_of(n):
    return list(range(0, n, 2)) + list(range(1, n, 2))[::-1]


def ring_gather(block, axis, first):
    n = lax.axis_size(axis)
    ring = ring_of(n)
    up = [(ring[i], ring[(i + 1) % n]) for i in range(n)]
    down = [(ring[(i + 1) % n], ring[i]) for i in range(n)]
    half = block.shape[1] // 2
    neighbours = lax.ppermute(block, axis, up), lax.ppermute(block, axis, down)
    cuts = [(0, 0), (1, 0), (0, half), (1, half)]
    streams = handed_on(neighbours, first, cuts, half)
    pieces = [block, *neighbours]
    for step in range(2, n // 2):
        streams = [lax.ppermute(x, axis, way) for x, way in zip(streams, (up, down) * 2)]
        pieces += streams
    return pieces + [lax.ppermute(streams[0], axis, up), lax.ppermute(streams[3], axis, down)]


def pass_kernel(cuts, *refs):
    for (i, start), target in zip(cuts, refs[-len(cuts) :]):
        target[...] = refs[i][:, start : start + target.shape[1]]


def handed_on(arrays, values, cuts, width):
    in_vmem = pl.BlockSpec(memory_space=pltpu.VMEM)
    return pl.pallas_call(
        functools.partial(pass_kernel, cuts),
        out_shape=[jax.ShapeDtypeStruct((arrays[0].shape[0], width), arrays[0].dtype)] * len(cuts),
        in_specs=[in_vmem] * len(arrays) + [pl.BlockSpec(memory_space=pl.ANY)] * len(values),
        out_specs=[in_vmem] * len(cuts),
        compiler_params=pltpu.CompilerParams(vmem_limit_bytes=16 * 2**20),
        name="pass",
    )(*arrays, *values)


def ring_place(i, n):
    return jnp.where(lax.rem(i, 2) == 0, i // 2, n - 1 - i // 2)


def exchange_order(n):
    ring = ring_of(n)
    return [ring[1 - p] for p in range(n)]


def exchange_place(i, n):
    return lax.rem(n + 1 - ring_place(i, n), n)


def ring_sources(axis, half):
    n = lax.axis_size(axis)
    place = ring_place(lax.axis_index(axis), n)
    found = [(0, 0), (1, 0), (-1, 0)]
    for i in range(2, n // 2):
        found += [(i, 0), (-i, 0), (i, half), (-i, half)]
    found += [(n // 2, 0), (n // 2, half)]
    sources = []
    for distance, column in found:
        at = lax.rem(place - distance + n, n)
        sources.append((jnp.where(at < n // 2, 2 * at, 2 * (n - 1 - at) + 1), column))
    return sources


def stack_kernel(groups, *refs):
    downs, ups, (down_ref, up_ref) = refs[:groups], refs[groups:-2], refs[-2:]
    rank = ups[0].shape[0]
    down_ref[...] = jnp.concatenate([down[...] for down in downs], axis=0).T
    for s, up in enumerate(ups):
        up_ref[s * rank : (s + 1) * rank, :] = up[...]


def place_kernel(groups, tp, ids_ref, lengths_ref, slots_ref, row_ref, column_ref):
    group = lax.axis_index("grp")
    longest = row_ref.shape[1] // 8
    along = lax.broadcasted_iota(jnp.int32, row_ref.shape, 1)
    down = lax.broadcasted_iota(jnp.int32, column_ref.shape, 0)

    def add(request, carry):
        start, row, column = carry
        slot = slots_ref[ids_ref[group, request]]
        end = start + lengths_ref[0, request]
        panel = lax.rem(slot // tp - group + groups, groups)
        first = (exchange_place(lax.rem(slot, tp), tp) * groups + panel) * longest - start
        row = jnp.where((along >= start) & (along < end), first + along, row)
        column = jnp.where((down >= start) & (down < end), first + down, column)
        return end, row, column

    carry = (jnp.int32(0), jnp.zeros_like(along), jnp.zeros_like(down))
    _, row_ref[...], column_ref[...] = lax.fori_loop(0, ids_ref.shape[1], add, carry)


def lift_kernel(groups, place_ref, down_ref, up_ref, *refs):
    pieces, (tokens_ref, out_ref, made_ref, sems) = refs[:-4], refs[-4:]
    rank = up_ref.shape[0] // groups
    rows = pieces[0].shape[0]
    tok_all = tokens_ref.shape[0]
    parts, slots, columns = out_ref.shape
    for piece, (source, column) in zip(pieces, ring_sources("tp", pieces[-1].shape[1])):
        start = pl.multiple_of(source * rows, rows)
        tokens_ref[pl.ds(start, rows), column : column + piece.shape[1]] = piece[...]
    low = jnp.dot(tokens_ref[...], down_ref[...], preferred_element_type=jnp.float32)
    place = exchange_place(lax.axis_index("tp"), parts)
    here = lax.broadcasted_iota(jnp.int32, (slots, tok_all), 0) + place * slots
    chosen = (here == place_ref[...]).astype(jnp.bfloat16)
    picked = jnp.dot(chosen, low.astype(jnp.bfloat16), preferred_element_type=jnp.float32)
    row_panel = lax.broadcasted_iota(jnp.int32, picked.shape, 0) // (slots // groups)
    rank_panel = lax.broadcasted_iota(jnp.int32, picked.shape, 1) // rank
    picked = jnp.where(row_panel == rank_panel, picked, 0.0).astype(jnp.bfloat16)
    copies = []
    for part, owner in enumerate(exchange_order(parts)):
        made_ref[part] = jnp.dot(
            picked,
            up_ref[:, owner * columns : (owner + 1) * columns],
            preferred_element_type=jnp.float32,
        ).astype(made_ref.dtype)
        copies.append(
            pltpu.make_async_copy(made_ref.at[part], out_ref.at[part], sems.at[part])
        )
        copies[-1].start()
    for copy in copies:
        copy.wait()


def add_kernel(place_ref, base_ref, lifts_ref, out_ref):
    place = lax.broadcasted_iota(jnp.int32, (base_ref.shape[0], lifts_ref.shape[0]), 1)
    chosen = (place == place_ref[...]).astype(jnp.bfloat16)
    lift = jnp.dot(chosen, lifts_ref[...], preferred_element_type=jnp.float32)
    out_ref[...] = (base_ref[...] + adapter_scale * lift).astype(out_ref.dtype)


def on_device(
    tokens,
    base_projection_weight,
    adapter_down_panels,
    adapter_up_panels,
    request_adapter_ids,
    request_token_lengths,
    adapter_store_slot,
):
    groups = lax.axis_size("grp")
    tp = lax.axis_size("tp")
    width, rank = adapter_down_panels.shape[1:]
    columns = base_projection_weight.shape[1]
    tok_all = tokens.shape[1] * tp
    longest = tok_all // 8
    here = groups * longest
    in_vmem = pl.BlockSpec(memory_space=pltpu.VMEM)
    in_smem = pl.BlockSpec(memory_space=pltpu.SMEM)
    small = pltpu.CompilerParams(vmem_limit_bytes=16 * 2**20)

    panels = swapped(adapter_down_panels[0].T, "grp") + swapped(adapter_up_panels[0], "grp")
    down, up = pl.pallas_call(
        functools.partial(stack_kernel, groups),
        out_shape=[
            jax.ShapeDtypeStruct((width, groups * rank), jnp.bfloat16),
            jax.ShapeDtypeStruct((groups * rank, tp * columns), jnp.bfloat16),
        ],
        in_specs=[in_vmem] * len(panels),
        out_specs=[in_vmem] * 2,
        compiler_params=small,
        name="stack",
    )(*panels)
    row, column = pl.pallas_call(
        functools.partial(place_kernel, groups, tp),
        out_shape=[
            jax.ShapeDtypeStruct((1, tok_all), jnp.int32),
            jax.ShapeDtypeStruct((tok_all, 1), jnp.int32),
        ],
        in_specs=[in_smem] * 3,
        out_specs=[in_vmem] * 2,
        compiler_params=small,
        name="place",
    )(request_adapter_ids, request_token_lengths, adapter_store_slot)
    pieces = ring_gather(tokens[0], "tp", (down, up, row, column))

    gathered, lifts = pl.pallas_call(
        functools.partial(lift_kernel, groups),
        out_shape=[
            jax.ShapeDtypeStruct((tok_all, width), jnp.bfloat16),
            jax.ShapeDtypeStruct((tp, here, columns), jnp.bfloat16),
        ],
        in_specs=[in_vmem] * (3 + len(pieces)),
        out_specs=[in_vmem, pl.BlockSpec(memory_space=pl.ANY)],
        scratch_shapes=[
            pltpu.VMEM((tp, here, columns), jnp.bfloat16),
            pltpu.SemaphoreType.DMA((tp,)),
        ],
        compiler_params=pltpu.CompilerParams(vmem_limit_bytes=24 * 2**20),
        cost_estimate=pl.CostEstimate(
            flops=2 * groups * rank * (tok_all * width + here * tp * columns),
            bytes_accessed=2 * groups * rank * (width + tp * columns),
            transcendentals=0,
        ),
        name="lift",
    )(row, down, up, *pieces)
    lifts = lax.all_to_all(
        lifts, "tp", split_axis=0, concat_axis=0, axis_index_groups=[exchange_order(tp)], tiled=True
    )

    base = jnp.dot(gathered, base_projection_weight, preferred_element_type=jnp.float32)
    out = pl.pallas_call(
        add_kernel,
        out_shape=jax.ShapeDtypeStruct((tok_all, columns), jnp.bfloat16),
        in_specs=[in_vmem] * 3,
        out_specs=in_vmem,
        compiler_params=small,
        name="add",
    )(column, base, lifts.reshape(tp * here, columns))
    return out[None]


def solution(mesh):
    return jax.shard_map(
        on_device,
        mesh=mesh,
        in_specs=(
            P(("rep", "grp"), "tp", None),
            P(None, "tp"),
            P(("grp", "tp"), None, None),
            P(("grp", "tp"), None, None),
            P("rep", None),
            P(("rep", "grp"), None),
            P(),
        ),
        out_specs=P(("rep", "grp"), None, "tp"),
        check_vma=False,
    )
```

```python
import functools

import jax
import jax.numpy as jnp
from jax import lax
from jax.experimental import pallas as pl
from jax.experimental.pallas import tpu as pltpu
from jax.sharding import PartitionSpec as P

adapter_scale = 1.0


def swapped(x, axis):
    n = lax.axis_size(axis)
    return [x] + [
        lax.ppermute(x, axis, [((i + s) % n, i) for i in range(n)]) for s in range(1, n)
    ]


def ring_of(n):
    return list(range(0, n, 2)) + list(range(1, n, 2))[::-1]


def ring_gather(block, axis, first):
    n = lax.axis_size(axis)
    ring = ring_of(n)
    up = [(ring[i], ring[(i + 1) % n]) for i in range(n)]
    down = [(ring[(i + 1) % n], ring[i]) for i in range(n)]
    half = block.shape[1] // 2
    neighbours = lax.ppermute(block, axis, up), lax.ppermute(block, axis, down)
    cuts = [(0, 0), (1, 0), (0, half), (1, half)]
    streams = handed_on(neighbours, first, cuts, half)
    pieces = [block, *neighbours]
    for step in range(2, n // 2):
        streams = [lax.ppermute(x, axis, way) for x, way in zip(streams, (up, down) * 2)]
        pieces += streams
    return pieces + [lax.ppermute(streams[0], axis, up), lax.ppermute(streams[3], axis, down)]


def pass_kernel(cuts, *refs):
    for (i, start), target in zip(cuts, refs[-len(cuts) :]):
        target[...] = refs[i][:, start : start + target.shape[1]]


def handed_on(arrays, values, cuts, width):
    in_vmem = pl.BlockSpec(memory_space=pltpu.VMEM)
    return pl.pallas_call(
        functools.partial(pass_kernel, cuts),
        out_shape=[jax.ShapeDtypeStruct((arrays[0].shape[0], width), arrays[0].dtype)] * len(cuts),
        in_specs=[in_vmem] * len(arrays) + [pl.BlockSpec(memory_space=pl.ANY)] * len(values),
        out_specs=[in_vmem] * len(cuts),
        compiler_params=pltpu.CompilerParams(vmem_limit_bytes=16 * 2**20),
        name="pass",
    )(*arrays, *values)


def ring_place(i, n):
    return jnp.where(lax.rem(i, 2) == 0, i // 2, n - 1 - i // 2)


def exchange_order(n):
    ring = ring_of(n)
    return ring[2:] + ring[:2]


def exchange_place(i, n):
    return lax.rem(ring_place(i, n) + n - 2, n)


def ring_sources(axis, half):
    n = lax.axis_size(axis)
    place = ring_place(lax.axis_index(axis), n)
    found = [(0, 0), (1, 0), (-1, 0)]
    for i in range(2, n // 2):
        found += [(i, 0), (-i, 0), (i, half), (-i, half)]
    found += [(n // 2, 0), (n // 2, half)]
    sources = []
    for distance, column in found:
        at = lax.rem(place - distance + n, n)
        sources.append((jnp.where(at < n // 2, 2 * at, 2 * (n - 1 - at) + 1), column))
    return sources


def stack_kernel(groups, *refs):
    downs, ups, (down_ref, up_ref) = refs[:groups], refs[groups:-2], refs[-2:]
    rank = ups[0].shape[0]
    down_ref[...] = jnp.concatenate([down[...] for down in downs], axis=0).T
    for s, up in enumerate(ups):
        up_ref[s * rank : (s + 1) * rank, :] = up[...]


def place_kernel(groups, tp, ids_ref, lengths_ref, slots_ref, row_ref, column_ref):
    group = lax.axis_index("grp")
    longest = row_ref.shape[1] // 8
    along = lax.broadcasted_iota(jnp.int32, row_ref.shape, 1)
    down = lax.broadcasted_iota(jnp.int32, column_ref.shape, 0)

    def add(request, carry):
        start, row, column = carry
        slot = slots_ref[ids_ref[group, request]]
        end = start + lengths_ref[0, request]
        panel = lax.rem(slot // tp - group + groups, groups)
        first = (exchange_place(lax.rem(slot, tp), tp) * groups + panel) * longest - start
        row = jnp.where((along >= start) & (along < end), first + along, row)
        column = jnp.where((down >= start) & (down < end), first + down, column)
        return end, row, column

    carry = (jnp.int32(0), jnp.zeros_like(along), jnp.zeros_like(down))
    _, row_ref[...], column_ref[...] = lax.fori_loop(0, ids_ref.shape[1], add, carry)


def lift_kernel(groups, place_ref, down_ref, up_ref, *refs):
    pieces, (tokens_ref, out_ref, made_ref, sems) = refs[:-4], refs[-4:]
    rank = up_ref.shape[0] // groups
    rows = pieces[0].shape[0]
    tok_all = tokens_ref.shape[0]
    parts, slots, columns = out_ref.shape
    for piece, (source, column) in zip(pieces, ring_sources("tp", pieces[-1].shape[1])):
        start = pl.multiple_of(source * rows, rows)
        tokens_ref[pl.ds(start, rows), column : column + piece.shape[1]] = piece[...]
    low = jnp.dot(tokens_ref[...], down_ref[...], preferred_element_type=jnp.float32)
    place = exchange_place(lax.axis_index("tp"), parts)
    here = lax.broadcasted_iota(jnp.int32, (slots, tok_all), 0) + place * slots
    chosen = (here == place_ref[...]).astype(jnp.bfloat16)
    picked = jnp.dot(chosen, low.astype(jnp.bfloat16), preferred_element_type=jnp.float32)
    row_panel = lax.broadcasted_iota(jnp.int32, picked.shape, 0) // (slots // groups)
    rank_panel = lax.broadcasted_iota(jnp.int32, picked.shape, 1) // rank
    picked = jnp.where(row_panel == rank_panel, picked, 0.0).astype(jnp.bfloat16)
    copies = []
    for part, owner in enumerate(exchange_order(parts)):
        made_ref[part] = jnp.dot(
            picked,
            up_ref[:, owner * columns : (owner + 1) * columns],
            preferred_element_type=jnp.float32,
        ).astype(made_ref.dtype)
        copies.append(
            pltpu.make_async_copy(made_ref.at[part], out_ref.at[part], sems.at[part])
        )
        copies[-1].start()
    for copy in copies:
        copy.wait()


def add_kernel(place_ref, base_ref, lifts_ref, out_ref):
    place = lax.broadcasted_iota(jnp.int32, (base_ref.shape[0], lifts_ref.shape[0]), 1)
    chosen = (place == place_ref[...]).astype(jnp.bfloat16)
    lift = jnp.dot(chosen, lifts_ref[...], preferred_element_type=jnp.float32)
    out_ref[...] = (base_ref[...] + adapter_scale * lift).astype(out_ref.dtype)


def on_device(
    tokens,
    base_projection_weight,
    adapter_down_panels,
    adapter_up_panels,
    request_adapter_ids,
    request_token_lengths,
    adapter_store_slot,
):
    groups = lax.axis_size("grp")
    tp = lax.axis_size("tp")
    width, rank = adapter_down_panels.shape[1:]
    columns = base_projection_weight.shape[1]
    tok_all = tokens.shape[1] * tp
    longest = tok_all // 8
    here = groups * longest
    in_vmem = pl.BlockSpec(memory_space=pltpu.VMEM)
    in_smem = pl.BlockSpec(memory_space=pltpu.SMEM)
    small = pltpu.CompilerParams(vmem_limit_bytes=16 * 2**20)

    panels = swapped(adapter_down_panels[0].T, "grp") + swapped(adapter_up_panels[0], "grp")
    down, up = pl.pallas_call(
        functools.partial(stack_kernel, groups),
        out_shape=[
            jax.ShapeDtypeStruct((width, groups * rank), jnp.bfloat16),
            jax.ShapeDtypeStruct((groups * rank, tp * columns), jnp.bfloat16),
        ],
        in_specs=[in_vmem] * len(panels),
        out_specs=[in_vmem] * 2,
        compiler_params=small,
        name="stack",
    )(*panels)
    row, column = pl.pallas_call(
        functools.partial(place_kernel, groups, tp),
        out_shape=[
            jax.ShapeDtypeStruct((1, tok_all), jnp.int32),
            jax.ShapeDtypeStruct((tok_all, 1), jnp.int32),
        ],
        in_specs=[in_smem] * 3,
        out_specs=[in_vmem] * 2,
        compiler_params=small,
        name="place",
    )(request_adapter_ids, request_token_lengths, adapter_store_slot)
    pieces = ring_gather(tokens[0], "tp", (down, up, row, column))

    gathered, lifts = pl.pallas_call(
        functools.partial(lift_kernel, groups),
        out_shape=[
            jax.ShapeDtypeStruct((tok_all, width), jnp.bfloat16),
            jax.ShapeDtypeStruct((tp, here, columns), jnp.bfloat16),
        ],
        in_specs=[in_vmem] * (3 + len(pieces)),
        out_specs=[in_vmem, pl.BlockSpec(memory_space=pl.ANY)],
        scratch_shapes=[
            pltpu.VMEM((tp, here, columns), jnp.bfloat16),
            pltpu.SemaphoreType.DMA((tp,)),
        ],
        compiler_params=pltpu.CompilerParams(vmem_limit_bytes=24 * 2**20),
        cost_estimate=pl.CostEstimate(
            flops=2 * groups * rank * (tok_all * width + here * tp * columns),
            bytes_accessed=2 * groups * rank * (width + tp * columns),
            transcendentals=0,
        ),
        name="lift",
    )(row, down, up, *pieces)
    lifts = lax.all_to_all(
        lifts, "tp", split_axis=0, concat_axis=0, axis_index_groups=[exchange_order(tp)], tiled=True
    )

    base = jnp.dot(gathered, base_projection_weight, preferred_element_type=jnp.float32)
    out = pl.pallas_call(
        add_kernel,
        out_shape=jax.ShapeDtypeStruct((tok_all, columns), jnp.bfloat16),
        in_specs=[in_vmem] * 3,
        out_specs=in_vmem,
        compiler_params=small,
        name="add",
    )(column, base, lifts.reshape(tp * here, columns))
    return out[None]


def solution(mesh):
    return jax.shard_map(
        on_device,
        mesh=mesh,
        in_specs=(
            P(("rep", "grp"), "tp", None),
            P(None, "tp"),
            P(("grp", "tp"), None, None),
            P(("grp", "tp"), None, None),
            P("rep", None),
            P(("rep", "grp"), None),
            P(),
        ),
        out_specs=P(("rep", "grp"), None, "tp"),
        check_vma=False,
    )
```

```python
import functools

import jax
import jax.numpy as jnp
from jax import lax
from jax.experimental import pallas as pl
from jax.experimental.pallas import tpu as pltpu
from jax.sharding import PartitionSpec as P

adapter_scale = 1.0


def swapped(x, axis):
    n = lax.axis_size(axis)
    return [x] + [
        lax.ppermute(x, axis, [((i + s) % n, i) for i in range(n)]) for s in range(1, n)
    ]


def ring_of(n):
    return list(range(0, n, 2)) + list(range(1, n, 2))[::-1]


def ring_gather(block, axis, first):
    n = lax.axis_size(axis)
    ring = ring_of(n)
    up = [(ring[i], ring[(i + 1) % n]) for i in range(n)]
    down = [(ring[(i + 1) % n], ring[i]) for i in range(n)]
    half = block.shape[1] // 2
    neighbours = lax.ppermute(block, axis, up), lax.ppermute(block, axis, down)
    cuts = [(0, 0), (1, 0), (0, half), (1, half)]
    streams = handed_on(neighbours, first, cuts, half)
    pieces = [block, *neighbours]
    for step in range(2, n // 2):
        streams = [lax.ppermute(x, axis, way) for x, way in zip(streams, (up, down) * 2)]
        pieces += streams
    return pieces + [lax.ppermute(streams[0], axis, up), lax.ppermute(streams[3], axis, down)]


def pass_kernel(cuts, *refs):
    for (i, start), target in zip(cuts, refs[-len(cuts) :]):
        target[...] = refs[i][:, start : start + target.shape[1]]


def handed_on(arrays, values, cuts, width):
    in_vmem = pl.BlockSpec(memory_space=pltpu.VMEM)
    return pl.pallas_call(
        functools.partial(pass_kernel, cuts),
        out_shape=[jax.ShapeDtypeStruct((arrays[0].shape[0], width), arrays[0].dtype)] * len(cuts),
        in_specs=[in_vmem] * len(arrays) + [pl.BlockSpec(memory_space=pl.ANY)] * len(values),
        out_specs=[in_vmem] * len(cuts),
        compiler_params=pltpu.CompilerParams(vmem_limit_bytes=16 * 2**20),
        name="pass",
    )(*arrays, *values)


def ring_place(i, n):
    return jnp.where(lax.rem(i, 2) == 0, i // 2, n - 1 - i // 2)


def exchange_order(n):
    ring = ring_of(n)
    return ring[3:] + ring[:3]


def exchange_place(i, n):
    return lax.rem(ring_place(i, n) + n - 3, n)


def ring_sources(axis, half):
    n = lax.axis_size(axis)
    place = ring_place(lax.axis_index(axis), n)
    found = [(0, 0), (1, 0), (-1, 0)]
    for i in range(2, n // 2):
        found += [(i, 0), (-i, 0), (i, half), (-i, half)]
    found += [(n // 2, 0), (n // 2, half)]
    sources = []
    for distance, column in found:
        at = lax.rem(place - distance + n, n)
        sources.append((jnp.where(at < n // 2, 2 * at, 2 * (n - 1 - at) + 1), column))
    return sources


def stack_kernel(groups, *refs):
    downs, ups, (down_ref, up_ref) = refs[:groups], refs[groups:-2], refs[-2:]
    rank = ups[0].shape[0]
    down_ref[...] = jnp.concatenate([down[...] for down in downs], axis=0).T
    for s, up in enumerate(ups):
        up_ref[s * rank : (s + 1) * rank, :] = up[...]


def place_kernel(groups, tp, ids_ref, lengths_ref, slots_ref, row_ref, column_ref):
    group = lax.axis_index("grp")
    longest = row_ref.shape[1] // 8
    along = lax.broadcasted_iota(jnp.int32, row_ref.shape, 1)
    down = lax.broadcasted_iota(jnp.int32, column_ref.shape, 0)

    def add(request, carry):
        start, row, column = carry
        slot = slots_ref[ids_ref[group, request]]
        end = start + lengths_ref[0, request]
        panel = lax.rem(slot // tp - group + groups, groups)
        first = (exchange_place(lax.rem(slot, tp), tp) * groups + panel) * longest - start
        row = jnp.where((along >= start) & (along < end), first + along, row)
        column = jnp.where((down >= start) & (down < end), first + down, column)
        return end, row, column

    carry = (jnp.int32(0), jnp.zeros_like(along), jnp.zeros_like(down))
    _, row_ref[...], column_ref[...] = lax.fori_loop(0, ids_ref.shape[1], add, carry)


def lift_kernel(groups, place_ref, down_ref, up_ref, *refs):
    pieces, (tokens_ref, out_ref, made_ref, sems) = refs[:-4], refs[-4:]
    rank = up_ref.shape[0] // groups
    rows = pieces[0].shape[0]
    tok_all = tokens_ref.shape[0]
    parts, slots, columns = out_ref.shape
    for piece, (source, column) in zip(pieces, ring_sources("tp", pieces[-1].shape[1])):
        start = pl.multiple_of(source * rows, rows)
        tokens_ref[pl.ds(start, rows), column : column + piece.shape[1]] = piece[...]
    low = jnp.dot(tokens_ref[...], down_ref[...], preferred_element_type=jnp.float32)
    place = exchange_place(lax.axis_index("tp"), parts)
    here = lax.broadcasted_iota(jnp.int32, (slots, tok_all), 0) + place * slots
    chosen = (here == place_ref[...]).astype(jnp.bfloat16)
    picked = jnp.dot(chosen, low.astype(jnp.bfloat16), preferred_element_type=jnp.float32)
    row_panel = lax.broadcasted_iota(jnp.int32, picked.shape, 0) // (slots // groups)
    rank_panel = lax.broadcasted_iota(jnp.int32, picked.shape, 1) // rank
    picked = jnp.where(row_panel == rank_panel, picked, 0.0).astype(jnp.bfloat16)
    copies = []
    for part, owner in enumerate(exchange_order(parts)):
        made_ref[part] = jnp.dot(
            picked,
            up_ref[:, owner * columns : (owner + 1) * columns],
            preferred_element_type=jnp.float32,
        ).astype(made_ref.dtype)
        copies.append(
            pltpu.make_async_copy(made_ref.at[part], out_ref.at[part], sems.at[part])
        )
        copies[-1].start()
    for copy in copies:
        copy.wait()


def add_kernel(place_ref, base_ref, lifts_ref, out_ref):
    place = lax.broadcasted_iota(jnp.int32, (base_ref.shape[0], lifts_ref.shape[0]), 1)
    chosen = (place == place_ref[...]).astype(jnp.bfloat16)
    lift = jnp.dot(chosen, lifts_ref[...], preferred_element_type=jnp.float32)
    out_ref[...] = (base_ref[...] + adapter_scale * lift).astype(out_ref.dtype)


def on_device(
    tokens,
    base_projection_weight,
    adapter_down_panels,
    adapter_up_panels,
    request_adapter_ids,
    request_token_lengths,
    adapter_store_slot,
):
    groups = lax.axis_size("grp")
    tp = lax.axis_size("tp")
    width, rank = adapter_down_panels.shape[1:]
    columns = base_projection_weight.shape[1]
    tok_all = tokens.shape[1] * tp
    longest = tok_all // 8
    here = groups * longest
    in_vmem = pl.BlockSpec(memory_space=pltpu.VMEM)
    in_smem = pl.BlockSpec(memory_space=pltpu.SMEM)
    small = pltpu.CompilerParams(vmem_limit_bytes=16 * 2**20)

    panels = swapped(adapter_down_panels[0].T, "grp") + swapped(adapter_up_panels[0], "grp")
    down, up = pl.pallas_call(
        functools.partial(stack_kernel, groups),
        out_shape=[
            jax.ShapeDtypeStruct((width, groups * rank), jnp.bfloat16),
            jax.ShapeDtypeStruct((groups * rank, tp * columns), jnp.bfloat16),
        ],
        in_specs=[in_vmem] * len(panels),
        out_specs=[in_vmem] * 2,
        compiler_params=small,
        name="stack",
    )(*panels)
    row, column = pl.pallas_call(
        functools.partial(place_kernel, groups, tp),
        out_shape=[
            jax.ShapeDtypeStruct((1, tok_all), jnp.int32),
            jax.ShapeDtypeStruct((tok_all, 1), jnp.int32),
        ],
        in_specs=[in_smem] * 3,
        out_specs=[in_vmem] * 2,
        compiler_params=small,
        name="place",
    )(request_adapter_ids, request_token_lengths, adapter_store_slot)
    pieces = ring_gather(tokens[0], "tp", (down, up, row, column))

    gathered, lifts = pl.pallas_call(
        functools.partial(lift_kernel, groups),
        out_shape=[
            jax.ShapeDtypeStruct((tok_all, width), jnp.bfloat16),
            jax.ShapeDtypeStruct((tp, here, columns), jnp.bfloat16),
        ],
        in_specs=[in_vmem] * (3 + len(pieces)),
        out_specs=[in_vmem, pl.BlockSpec(memory_space=pl.ANY)],
        scratch_shapes=[
            pltpu.VMEM((tp, here, columns), jnp.bfloat16),
            pltpu.SemaphoreType.DMA((tp,)),
        ],
        compiler_params=pltpu.CompilerParams(vmem_limit_bytes=24 * 2**20),
        cost_estimate=pl.CostEstimate(
            flops=2 * groups * rank * (tok_all * width + here * tp * columns),
            bytes_accessed=2 * groups * rank * (width + tp * columns),
            transcendentals=0,
        ),
        name="lift",
    )(row, down, up, *pieces)
    lifts = lax.all_to_all(
        lifts, "tp", split_axis=0, concat_axis=0, axis_index_groups=[exchange_order(tp)], tiled=True
    )

    base = jnp.dot(gathered, base_projection_weight, preferred_element_type=jnp.float32)
    out = pl.pallas_call(
        add_kernel,
        out_shape=jax.ShapeDtypeStruct((tok_all, columns), jnp.bfloat16),
        in_specs=[in_vmem] * 3,
        out_specs=in_vmem,
        compiler_params=small,
        name="add",
    )(column, base, lifts.reshape(tp * here, columns))
    return out[None]


def solution(mesh):
    return jax.shard_map(
        on_device,
        mesh=mesh,
        in_specs=(
            P(("rep", "grp"), "tp", None),
            P(None, "tp"),
            P(("grp", "tp"), None, None),
            P(("grp", "tp"), None, None),
            P("rep", None),
            P(("rep", "grp"), None),
            P(),
        ),
        out_specs=P(("rep", "grp"), None, "tp"),
        check_vma=False,
    )
```

```python
import functools

import jax
import jax.numpy as jnp
from jax import lax
from jax.experimental import pallas as pl
from jax.experimental.pallas import tpu as pltpu
from jax.sharding import PartitionSpec as P

adapter_scale = 1.0


def swapped(x, axis):
    n = lax.axis_size(axis)
    return [x] + [
        lax.ppermute(x, axis, [((i + s) % n, i) for i in range(n)]) for s in range(1, n)
    ]


def ring_of(n):
    return list(range(0, n, 2)) + list(range(1, n, 2))[::-1]


def ring_gather(block, axis, first):
    n = lax.axis_size(axis)
    ring = ring_of(n)
    up = [(ring[i], ring[(i + 1) % n]) for i in range(n)]
    down = [(ring[(i + 1) % n], ring[i]) for i in range(n)]
    half = block.shape[1] // 2
    neighbours = lax.ppermute(block, axis, up), lax.ppermute(block, axis, down)
    cuts = [(0, 0), (1, 0), (0, half), (1, half)]
    streams = handed_on(neighbours, first, cuts, half)
    pieces = [block, *neighbours]
    for step in range(2, n // 2):
        streams = [lax.ppermute(x, axis, way) for x, way in zip(streams, (up, down) * 2)]
        pieces += streams
    return pieces + [lax.ppermute(streams[0], axis, up), lax.ppermute(streams[3], axis, down)]


def pass_kernel(cuts, *refs):
    for (i, start), target in zip(cuts, refs[-len(cuts) :]):
        target[...] = refs[i][:, start : start + target.shape[1]]


def handed_on(arrays, values, cuts, width):
    in_vmem = pl.BlockSpec(memory_space=pltpu.VMEM)
    return pl.pallas_call(
        functools.partial(pass_kernel, cuts),
        out_shape=[jax.ShapeDtypeStruct((arrays[0].shape[0], width), arrays[0].dtype)] * len(cuts),
        in_specs=[in_vmem] * len(arrays) + [pl.BlockSpec(memory_space=pl.ANY)] * len(values),
        out_specs=[in_vmem] * len(cuts),
        compiler_params=pltpu.CompilerParams(vmem_limit_bytes=16 * 2**20),
        name="pass",
    )(*arrays, *values)


def ring_place(i, n):
    return jnp.where(lax.rem(i, 2) == 0, i // 2, n - 1 - i // 2)


def exchange_groups(groups, n):
    ring = ring_of(n)
    return [[g * n + ring[(2 - p if g % 2 else 2 + p) % n] for p in range(n)] for g in range(groups)]


def exchange_place(i, n):
    ahead = ring_place(i, n) + n - 2
    return lax.rem(jnp.where(lax.rem(lax.axis_index("grp"), 2) == 0, ahead, 2 * n - ahead), n)


def ring_sources(axis, half):
    n = lax.axis_size(axis)
    place = ring_place(lax.axis_index(axis), n)
    found = [(0, 0), (1, 0), (-1, 0)]
    for i in range(2, n // 2):
        found += [(i, 0), (-i, 0), (i, half), (-i, half)]
    found += [(n // 2, 0), (n // 2, half)]
    sources = []
    for distance, column in found:
        at = lax.rem(place - distance + n, n)
        sources.append((jnp.where(at < n // 2, 2 * at, 2 * (n - 1 - at) + 1), column))
    return sources


def stack_kernel(groups, *refs):
    downs, ups, (down_ref, up_ref) = refs[:groups], refs[groups:-2], refs[-2:]
    rank = ups[0].shape[0]
    down_ref[...] = jnp.concatenate([down[...] for down in downs], axis=0).T
    for s, up in enumerate(ups):
        up_ref[s * rank : (s + 1) * rank, :] = up[...]


def place_kernel(groups, tp, ids_ref, lengths_ref, slots_ref, row_ref, column_ref):
    group = lax.axis_index("grp")
    longest = row_ref.shape[1] // 8
    along = lax.broadcasted_iota(jnp.int32, row_ref.shape, 1)
    down = lax.broadcasted_iota(jnp.int32, column_ref.shape, 0)

    def add(request, carry):
        start, row, column = carry
        slot = slots_ref[ids_ref[group, request]]
        end = start + lengths_ref[0, request]
        panel = lax.rem(slot // tp - group + groups, groups)
        first = (exchange_place(lax.rem(slot, tp), tp) * groups + panel) * longest - start
        row = jnp.where((along >= start) & (along < end), first + along, row)
        column = jnp.where((down >= start) & (down < end), first + down, column)
        return end, row, column

    carry = (jnp.int32(0), jnp.zeros_like(along), jnp.zeros_like(down))
    _, row_ref[...], column_ref[...] = lax.fori_loop(0, ids_ref.shape[1], add, carry)


def lift_kernel(groups, place_ref, down_ref, up_ref, *refs):
    pieces, (tokens_ref, out_ref, made_ref, sems) = refs[:-4], refs[-4:]
    rank = up_ref.shape[0] // groups
    rows = pieces[0].shape[0]
    tok_all = tokens_ref.shape[0]
    parts, slots, columns = out_ref.shape
    for piece, (source, column) in zip(pieces, ring_sources("tp", pieces[-1].shape[1])):
        start = pl.multiple_of(source * rows, rows)
        tokens_ref[pl.ds(start, rows), column : column + piece.shape[1]] = piece[...]
    low = jnp.dot(tokens_ref[...], down_ref[...], preferred_element_type=jnp.float32)
    place = exchange_place(lax.axis_index("tp"), parts)
    here = lax.broadcasted_iota(jnp.int32, (slots, tok_all), 0) + place * slots
    chosen = (here == place_ref[...]).astype(jnp.bfloat16)
    picked = jnp.dot(chosen, low.astype(jnp.bfloat16), preferred_element_type=jnp.float32)
    row_panel = lax.broadcasted_iota(jnp.int32, picked.shape, 0) // (slots // groups)
    rank_panel = lax.broadcasted_iota(jnp.int32, picked.shape, 1) // rank
    picked = jnp.where(row_panel == rank_panel, picked, 0.0).astype(jnp.bfloat16)
    copies = []
    for owner in range(parts):
        part = exchange_place(jnp.int32(owner), parts)
        made_ref[owner] = jnp.dot(
            picked,
            up_ref[:, owner * columns : (owner + 1) * columns],
            preferred_element_type=jnp.float32,
        ).astype(made_ref.dtype)
        copies.append(
            pltpu.make_async_copy(made_ref.at[owner], out_ref.at[part], sems.at[owner])
        )
        copies[-1].start()
    for copy in copies:
        copy.wait()


def add_kernel(place_ref, base_ref, lifts_ref, out_ref):
    place = lax.broadcasted_iota(jnp.int32, (base_ref.shape[0], lifts_ref.shape[0]), 1)
    chosen = (place == place_ref[...]).astype(jnp.bfloat16)
    lift = jnp.dot(chosen, lifts_ref[...], preferred_element_type=jnp.float32)
    out_ref[...] = (base_ref[...] + adapter_scale * lift).astype(out_ref.dtype)


def on_device(
    tokens,
    base_projection_weight,
    adapter_down_panels,
    adapter_up_panels,
    request_adapter_ids,
    request_token_lengths,
    adapter_store_slot,
):
    groups = lax.axis_size("grp")
    tp = lax.axis_size("tp")
    width, rank = adapter_down_panels.shape[1:]
    columns = base_projection_weight.shape[1]
    tok_all = tokens.shape[1] * tp
    longest = tok_all // 8
    here = groups * longest
    in_vmem = pl.BlockSpec(memory_space=pltpu.VMEM)
    in_smem = pl.BlockSpec(memory_space=pltpu.SMEM)
    small = pltpu.CompilerParams(vmem_limit_bytes=16 * 2**20)

    panels = swapped(adapter_down_panels[0].T, "grp") + swapped(adapter_up_panels[0], "grp")
    down, up = pl.pallas_call(
        functools.partial(stack_kernel, groups),
        out_shape=[
            jax.ShapeDtypeStruct((width, groups * rank), jnp.bfloat16),
            jax.ShapeDtypeStruct((groups * rank, tp * columns), jnp.bfloat16),
        ],
        in_specs=[in_vmem] * len(panels),
        out_specs=[in_vmem] * 2,
        compiler_params=small,
        name="stack",
    )(*panels)
    row, column = pl.pallas_call(
        functools.partial(place_kernel, groups, tp),
        out_shape=[
            jax.ShapeDtypeStruct((1, tok_all), jnp.int32),
            jax.ShapeDtypeStruct((tok_all, 1), jnp.int32),
        ],
        in_specs=[in_smem] * 3,
        out_specs=[in_vmem] * 2,
        compiler_params=small,
        name="place",
    )(request_adapter_ids, request_token_lengths, adapter_store_slot)
    pieces = ring_gather(tokens[0], "tp", (down, up, row, column))

    gathered, lifts = pl.pallas_call(
        functools.partial(lift_kernel, groups),
        out_shape=[
            jax.ShapeDtypeStruct((tok_all, width), jnp.bfloat16),
            jax.ShapeDtypeStruct((tp, here, columns), jnp.bfloat16),
        ],
        in_specs=[in_vmem] * (3 + len(pieces)),
        out_specs=[in_vmem, pl.BlockSpec(memory_space=pl.ANY)],
        scratch_shapes=[
            pltpu.VMEM((tp, here, columns), jnp.bfloat16),
            pltpu.SemaphoreType.DMA((tp,)),
        ],
        compiler_params=pltpu.CompilerParams(vmem_limit_bytes=24 * 2**20),
        cost_estimate=pl.CostEstimate(
            flops=2 * groups * rank * (tok_all * width + here * tp * columns),
            bytes_accessed=2 * groups * rank * (width + tp * columns),
            transcendentals=0,
        ),
        name="lift",
    )(row, down, up, *pieces)
    lifts = lax.all_to_all(
        lifts,
        ("grp", "tp"),
        split_axis=0,
        concat_axis=0,
        axis_index_groups=exchange_groups(groups, tp),
        tiled=True,
    )

    base = jnp.dot(gathered, base_projection_weight, preferred_element_type=jnp.float32)
    out = pl.pallas_call(
        add_kernel,
        out_shape=jax.ShapeDtypeStruct((tok_all, columns), jnp.bfloat16),
        in_specs=[in_vmem] * 3,
        out_specs=in_vmem,
        compiler_params=small,
        name="add",
    )(column, base, lifts.reshape(tp * here, columns))
    return out[None]


def solution(mesh):
    return jax.shard_map(
        on_device,
        mesh=mesh,
        in_specs=(
            P(("rep", "grp"), "tp", None),
            P(None, "tp"),
            P(("grp", "tp"), None, None),
            P(("grp", "tp"), None, None),
            P("rep", None),
            P(("rep", "grp"), None),
            P(),
        ),
        out_specs=P(("rep", "grp"), None, "tp"),
        check_vma=False,
    )
```
